32 devices in a mesh: dp: 4 (over x, core), seq: 8 (over z, y).
Axes of the slice: x: 2, y: 2, z: 4, core: 2. Of those that a mesh axis runs over, the one named last changes fastest.
Arguments:
- inputs: bfloat16 [4, 2048, 2048], P('dp', 'seq'), may hold values from -6 to 6
- reset: int32 [4, 2048], P('dp', 'seq'), may hold values 0 or 1
- initial_state: float32 [4, 2560], P('dp', 'seq'), may hold values from -6 to 6
- cotangent: bfloat16 [4, 2048, 2048], P('dp', 'seq'), may hold values from -6 to 6
- norm1_gain: bfloat16 [2048], P(('dp', 'seq')), may hold values from 0.5 to 1.5
- w_gate: bfloat16 [2048, 2560], P(('dp', 'seq')), may hold values from -0.125 to 0.125
- w_in: bfloat16 [2048, 2560], P(('dp', 'seq')), may hold values from -0.125 to 0.125
- conv_w: bfloat16 [4, 2560], P(None, ('dp', 'seq')), may hold values from -3 to 3
- conv_bias: bfloat16 [2560], P(('dp', 'seq')), may hold values from -2 to 2
- w_rgate: bfloat16 [2560, 256], P(('dp', 'seq')), may hold values from -0.375 to 0.375
- rgate_bias: bfloat16 [2560], P(('dp', 'seq')), may hold values from -3 to 3
- w_igate: bfloat16 [2560, 256], P(('dp', 'seq')), may hold values from -0.375 to 0.375
- igate_bias: bfloat16 [2560], P(('dp', 'seq')), may hold values from -3 to 3
- decay_param: bfloat16 [2560], P(('dp', 'seq')), may hold values from 4 to 9
- w_out: bfloat16 [2560, 2048], P(('dp', 'seq')), may hold values from -0.5 to 0.5
- norm2_gain: bfloat16 [2048], P(('dp', 'seq')), may hold values from 0.5 to 1.5
- w_ffgate: bfloat16 [2048, 6144], P('dp', 'seq'), may hold values from -0.125 to 0.125
- w_ffup: bfloat16 [2048, 6144], P('dp', 'seq'), may hold values from -0.125 to 0.125
- w_ffdown: bfloat16 [6144, 2048], P('seq', 'dp'), may hold values from -0.15625 to 0.15625
Outputs:
- output: bfloat16 [4, 2048, 2048], P('dp', 'seq')
- input_grad: float32 [4, 2048, 2048], P('dp', 'seq')
- final_state: float32 [4, 2560], P('dp', 'seq')
- grad_norm1: float32 [2048], P(('dp', 'seq'))
- grad_gate: float32 [2048, 2560], P(('dp', 'seq'))
- grad_in: float32 [2048, 2560], P(('dp', 'seq'))
- grad_conv: float32 [4, 2560], P(None, ('dp', 'seq'))
- grad_conv_bias: float32 [2560], P(('dp', 'seq'))
- grad_rgate: float32 [2560, 256], P(('dp', 'seq'))
- grad_rgate_bias: float32 [2560], P(('dp', 'seq'))
- grad_igate: float32 [2560, 256], P(('dp', 'seq'))
- grad_igate_bias: float32 [2560], P(('dp', 'seq'))
- grad_decay: float32 [2560], P(('dp', 'seq'))
- grad_out: float32 [2560, 2048], P(('dp', 'seq'))
- grad_norm2: float32 [2048], P(('dp', 'seq'))
- grad_ffgate: float32 [2048, 6144], P('dp', 'seq')
- grad_ffup: float32 [2048, 6144], P('dp', 'seq')
- grad_ffdown: float32 [6144, 2048], P('seq', 'dp')
The draws below stay inside these ranges and needn't reach their ends.
Inputs may be any that keep to these rules, and one draw needn't show every extreme that they name: `reset`: 1 marks a token that begins a new document: the recurrence and the convolution read nothing before it.
All inputs are finite; a program needn't handle non-finite values. No bound on the sum of `reset` on one device may be relied on, other than what follows from the above.
Results may differ from the reference program's by a relative error of at most 0.0177.
Values may be sent and summed in bfloat16 or wider, within the bound.
A program may use at most 320 MiB of HBM per device.

```python
import jax
import jax.numpy as jnp
from jax import lax

D = 2048
HEADS = 10
HW = 256
FF = 6144
CONV = 4
LEN = 2048
R = 2560
BATCH = 4


def plant(values, rng, low, top_value):
    index_at = [jax.random.randint(jax.random.fold_in(rng, axis), (), 0, length) for axis, length in enumerate(values.shape)]
    longest = values.shape.index(max(values.shape))
    neighbour = index_at[:longest] + [(index_at[longest] + 1) % values.shape[longest]] + index_at[longest + 1:]
    return values.at[tuple(index_at)].set(low).at[tuple(neighbour)].set(top_value)


def level_of(rng, extent, cuts, least, high):
    level = 1.0
    for axis_at, parts in cuts:
        steps = jax.random.uniform(jax.random.fold_in(jax.random.fold_in(rng, 6), axis_at), (parts,), jnp.float32, least / len(cuts), high / len(cuts))
        level = level * jnp.repeat(jnp.exp(steps), extent[axis_at] // parts).reshape((-1,) + (1,) * (len(extent) - 1 - axis_at))
    return level


def noise(rng, extent, spread, limit, shards=(), kind=jnp.bfloat16):
    level = level_of(rng, extent, shards, -0.22, 0.18) if shards else 1.0
    drawn = jax.random.normal(rng, extent, jnp.float32) * spread * level
    return jnp.minimum(jnp.maximum(drawn, -limit), limit).astype(kind)


def setup_inputs(seed: int = 0) -> dict:
    splits = jax.random.split(jax.random.key(seed), 20)
    return {
        "inputs": noise(splits[0], (BATCH, LEN, D), 1.0, 6.0, ((0, 4), (1, 8))),
        "reset": plant((jax.random.randint(splits[1], (BATCH, LEN), 0, 128) < 1).astype(jnp.int32), jax.random.fold_in(splits[1], 1), 0, 1),
        "initial_state": noise(splits[2], (BATCH, R), 1.0, 6.0, ((0, 4), (1, 8)), jnp.float32),
        "cotangent": noise(splits[3], (BATCH, LEN, D), 1.0, 6.0, ((0, 4), (1, 8))),
        "norm1_gain": jnp.clip(1.0 + 0.1 * jax.random.normal(splits[4], (D,), jnp.float32), 0.5, 1.5).astype(jnp.bfloat16),
        "w_gate": noise(splits[5], (D, R), D ** -0.5, 0.125, ((0, 32),)),
        "w_in": noise(splits[6], (D, R), D ** -0.5, 0.125, ((0, 32),)),
        "conv_w": noise(splits[7], (CONV, R), 0.5, 3.0, ((1, 32),)),
        "conv_bias": noise(splits[8], (R,), 0.3, 2.0, ((0, 32),)),
        "w_rgate": noise(splits[9], (R, HW), HW ** -0.5, 0.375, ((0, 32),)),
        "rgate_bias": noise(splits[10], (R,), 0.5, 3.0, ((0, 32),)),
        "w_igate": noise(splits[11], (R, HW), HW ** -0.5, 0.375, ((0, 32),)),
        "igate_bias": noise(splits[12], (R,), 0.5, 3.0, ((0, 32),)),
        "decay_param": jnp.clip(4.0 + 5.0 * jax.random.uniform(splits[13], (R,), jnp.float32) ** level_of(splits[13], (R,), ((0, 32),), -0.2, 0.2), 4.0, 9.0).astype(jnp.bfloat16),
        "w_out": noise(splits[14], (R, D), (R // 16) ** -0.5, 0.5, ((0, 32),)),
        "norm2_gain": jnp.clip(1.0 + 0.1 * jax.random.normal(splits[15], (D,), jnp.float32), 0.5, 1.5).astype(jnp.bfloat16),
        "w_ffgate": noise(splits[16], (D, FF), D ** -0.5, 0.125, ((0, 4), (1, 8))),
        "w_ffup": noise(splits[17], (D, FF), D ** -0.5, 0.125, ((0, 4), (1, 8))),
        "w_ffdown": noise(splits[18], (FF, D), (FF // 4) ** -0.5, 0.15625, ((0, 8), (1, 4))),
    }


epsilon = 1e-06
floor_value = 0.0001
highest = lax.Precision.HIGHEST
scan_block = 64

@jax.custom_vjp
def low(v):
    return lax.optimization_barrier(v.astype(jnp.bfloat16)).astype(jnp.float32)

@jax.custom_vjp
def low_back(v):
    return v

def low_keep(v):
    return (low(v), None)

def low_pass(kept, grad):
    return (grad,)

def back_keep(v):
    return (v, None)

def back_low(kept, grad):
    return (low(grad),)
low.defvjp(low_keep, low_pass)
low_back.defvjp(back_keep, back_low)

def gelu_tanh(values):
    return jax.nn.gelu(values, approximate=True)

def rms_scale(values, norm_gain):
    return values * lax.rsqrt(lax.optimization_barrier(jnp.mean(values * values, axis=-1, keepdims=True)) + epsilon) * norm_gain

def matmul(left, right):
    return jnp.dot(left, right, precision=highest, preferred_element_type=jnp.float32)

def rows_of(values, first_row, row_count):
    return lax.slice_in_dim(values, first_row, first_row + row_count, axis=values.ndim - 2)

def conv_apply(padded, open_pad, conv_w, conv_bias, row_count):
    rim_rows = conv_w.shape[0] - 1
    conv_total = conv_bias + conv_w[0] * rows_of(padded, rim_rows, row_count)
    running = rows_of(open_pad, rim_rows, row_count)
    for offset in range(1, rim_rows + 1):
        if offset > 1:
            running = running * rows_of(open_pad, rim_rows + 1 - offset, row_count)
        conv_total = conv_total + running * conv_w[offset] * rows_of(padded, rim_rows - offset, row_count)
    return conv_total

def gate_math(rate_pre, input_pre, conv_vals, decay_param, reset_col):
    rate = jax.nn.sigmoid(rate_pre)
    in_gate = jax.nn.sigmoid(input_pre)
    log_decay = -8.0 * jax.nn.softplus(-decay_param) * rate
    keep_mask = 1.0 - reset_col
    decay_rows = jnp.exp(log_decay) * keep_mask
    root_term = jnp.sqrt(jnp.maximum(-jnp.expm1(2.0 * log_decay), floor_value))
    drive_rows = (reset_col + keep_mask * root_term) * in_gate * conv_vals
    return (decay_rows, drive_rows)

def block_scan(state_now, block_pair):

    def step_once(carry_state, entry):
        carry_state = entry[0] * carry_state + entry[1]
        return (carry_state, carry_state)
    return lax.scan(step_once, state_now, block_pair)

def time_scan(decay_rows, drive_rows, initial):
    blocks = decay_rows.shape[0] // scan_block
    shaped = (decay_rows.reshape(blocks, scan_block, -1), drive_rows.reshape(blocks, scan_block, -1))
    last_state, states = lax.scan(jax.checkpoint(block_scan), initial, shaped)
    return (states.reshape(decay_rows.shape), last_state)

def block_forward(token_rows, initial, reset_col, weights_f):
    norm1_gain, w_gate, w_in, conv_w, conv_bias, w_rgate, rgate_bias, w_igate, igate_bias, decay_param, w_out, norm2_gain, w_ffgate, w_ffup, w_ffdown = weights_f
    length = token_rows.shape[0]
    rim_rows = conv_w.shape[0] - 1
    normed = low(rms_scale(token_rows, norm1_gain))
    gate_pre = low_back(matmul(normed, w_gate))
    branch = low_back(low(matmul(normed, w_in)))
    padded = jnp.concatenate([jnp.zeros((rim_rows, R), branch.dtype), branch], 0)
    open_pad = jnp.concatenate([jnp.ones((rim_rows, 1), reset_col.dtype), 1.0 - reset_col], 0)
    conv_vals = low_back(low(conv_apply(padded, open_pad, conv_w, conv_bias, length)))
    head_view = conv_vals.reshape(length, HEADS, HW)
    rate_pre = low_back(jnp.einsum('nhi,hij->nhj', head_view, w_rgate.reshape(HEADS, HW, HW), precision=highest).reshape(length, R) + rgate_bias)
    input_pre = low_back(jnp.einsum('nhi,hij->nhj', head_view, w_igate.reshape(HEADS, HW, HW), precision=highest).reshape(length, R) + igate_bias)
    decay_rows, drive_rows = gate_math(rate_pre, input_pre, conv_vals, decay_param, reset_col)
    states, last_state = time_scan(decay_rows, drive_rows, initial)
    states_low = low_back(low(states))
    mixed_rows = low(states_low * gelu_tanh(gate_pre))
    residual = token_rows + low_back(matmul(mixed_rows, w_out))
    normed_two = low(rms_scale(residual, norm2_gain))
    ff_gate = low_back(matmul(normed_two, w_ffgate))
    ff_up = low_back(matmul(normed_two, w_ffup))
    hidden = low(gelu_tanh(ff_gate) * ff_up)
    return (residual + low_back(matmul(hidden, w_ffdown)), last_state)

def reference(inputs, reset, initial_state, cotangent, norm1_gain, w_gate, w_in, conv_w, conv_bias, w_rgate, rgate_bias, w_igate, igate_bias, decay_param, w_out, norm2_gain, w_ffgate, w_ffup, w_ffdown):
    weights_f = tuple((weight.astype(jnp.float32) for weight in (norm1_gain, w_gate, w_in, conv_w, conv_bias, w_rgate, rgate_bias, w_igate, igate_bias, decay_param, w_out, norm2_gain, w_ffgate, w_ffup, w_ffdown)))
    zero_grads = tuple((jnp.zeros_like(weight) for weight in weights_f))

    def per_sequence(totals, entry):
        token_rows, resets, init_state, cotan_rows = entry
        reset_col = resets.astype(jnp.float32)[:, None]

        def forward(tokens_f, params_f):
            return block_forward(tokens_f, init_state, reset_col, params_f)
        (result, last_state), backward = jax.vjp(forward, token_rows.astype(jnp.float32), weights_f)
        token_grad, param_grads = backward((cotan_rows.astype(jnp.float32), jnp.zeros_like(last_state)))
        totals = tuple((total_now + grad_now for total_now, grad_now in zip(totals, param_grads)))
        return (totals, (result.astype(jnp.bfloat16), token_grad, last_state))
    totals, (results, token_grads, last_states) = lax.scan(per_sequence, zero_grads, (inputs, reset, initial_state, cotangent))
    return (results, token_grads, last_states, totals[0], totals[1], totals[2], totals[3], totals[4], totals[5], totals[6], totals[7], totals[8], totals[9], totals[10], totals[11], totals[12], totals[13], totals[14])
```

```python
import functools

import jax
import jax.numpy as jnp
from jax import lax
from jax.experimental import pallas as pl
from jax.experimental.pallas import tpu as pltpu
from jax.sharding import PartitionSpec as P

HW = 256
LANES = 8


epsilon = 1e-06
floor_value = 0.0001
f32 = jnp.float32
bf16 = jnp.bfloat16


def seq_order(count):
    if count % 8:
        return list(range(count))
    wide = count // 4
    path = []
    for z in range(4):
        ys = range(1, wide) if z % 2 == 0 else range(wide - 1, 0, -1)
        path += [z * wide + y for y in ys]
    return path + [z * wide for z in (3, 2, 1, 0)]


class Ring:
    def __init__(self, axis, cycles):
        self.axis = axis
        self.cycles = cycles
        self.count = len(cycles[0])

    def shift(self, value, step):
        pairs = [
            (cycle[i], cycle[(i + step) % self.count])
            for cycle in self.cycles
            for i in range(self.count)
        ]
        return lax.ppermute(value, self.axis, pairs)

    def place(self):
        table = [0] * (self.count * len(self.cycles))
        for cycle in self.cycles:
            for i, device in enumerate(cycle):
                table[device] = i
        return jnp.asarray(table, jnp.int32)[lax.axis_index(self.axis)]

    def gather(self, value):
        count, half = self.count, self.count // 2
        blocks = [value] * count
        if count == 1:
            return blocks
        ahead = behind = value
        for step in range(1, half):
            behind = self.shift(behind, 1)
            ahead = self.shift(ahead, -1)
            blocks[count - step] = behind
            blocks[step] = ahead
        rows = value.shape[0]
        if half > 1 and rows % 32 == 0:
            top = self.shift(behind[: rows // 2], 1)
            bottom = self.shift(ahead[rows // 2 :], -1)
            blocks[half] = jnp.concatenate([top, bottom], 0)
        else:
            blocks[half] = self.shift(behind, 1)
        return blocks

    def scatter(self, part):
        count, half = self.count, self.count // 2
        if count == 1:
            return part(0).astype(f32)
        far = part(half).astype(bf16)
        if half == 1:
            return part(0).astype(f32) + self.shift(far, 1).astype(f32)
        rows = far.shape[0]
        cut = rows // 2 if rows % 32 == 0 else rows
        ahead, behind = far[:cut], far[cut:]
        for k in range(half - 1, 0, -1):
            got_ahead = self.shift(ahead, 1).astype(f32)
            mine_ahead = part(k).astype(f32)
            mine_behind = part(count - k).astype(f32)
            if k == half - 1 and cut == rows:
                ahead = (mine_ahead + got_ahead).astype(bf16)
                behind = mine_behind.astype(bf16)
                continue
            got_behind = self.shift(behind, -1).astype(f32)
            if k == half - 1:
                ahead = jnp.concatenate([mine_ahead[:cut] + got_ahead, mine_ahead[cut:]], 0)
                behind = jnp.concatenate([mine_behind[:cut], mine_behind[cut:] + got_behind], 0)
            else:
                ahead = mine_ahead + got_ahead
                behind = mine_behind + got_behind
            ahead, behind = ahead.astype(bf16), behind.astype(bf16)
        return (
            part(0).astype(f32)
            + self.shift(ahead, 1).astype(f32)
            + self.shift(behind, -1).astype(f32)
        )


class Net:
    def __init__(self):
        self.seq_count = lax.axis_size("seq")
        self.dp_count = lax.axis_size("dp")
        self.order = seq_order(self.seq_count)
        self.seq = Ring("seq", [self.order])
        self.cores = 2 if self.dp_count % 2 == 0 else 1
        self.chips = self.dp_count // self.cores
        cores, chips = self.cores, self.chips
        self.chip = Ring("dp", [[o * cores + c for o in range(chips)] for c in range(cores)])
        self.core = Ring("dp", [[o * cores + c for c in range(cores)] for o in range(chips)])
        self.place = self.seq.place()
        dp = lax.axis_index("dp")
        self.my_chip, self.my_core = dp // cores, dp % cores

    def seq_at(self, k):
        return jnp.asarray(self.order, jnp.int32)[(self.place + k) % self.seq_count]

    def rel(self):
        return [(c, k) for c in range(self.cores) for k in range(self.chips)]

    def dp_at(self, c, k):
        return ((self.my_chip + k) % self.chips) * self.cores + (self.my_core + c) % self.cores

    def columns_out(self, values):
        chunk = values.shape[1] // self.dp_count
        return jnp.concatenate(
            [lax.dynamic_slice_in_dim(values, self.dp_at(c, k) * chunk, chunk, 1) for c, k in self.rel()],
            1,
        )

    def columns_back(self, values):
        chunk = values.shape[1] // self.dp_count
        pieces = []
        for dp in range(self.dp_count):
            chip, core = dp // self.cores, dp % self.cores
            at = ((core - self.my_core) % self.cores) * self.chips + (chip - self.my_chip) % self.chips
            pieces.append(lax.dynamic_slice_in_dim(values, at * chunk, chunk, 1))
        return jnp.concatenate(pieces, 1)

    def gather_dp(self, value):
        blocks = self.chip.gather(value)
        if self.cores == 1:
            return blocks
        return blocks + [self.core.shift(block, 1) for block in blocks]

    def scatter_dp(self, part):
        sums = [part(0, k) for k in range(self.chips)]
        if self.cores > 1:
            sums = [
                mine.astype(f32) + self.core.shift(part(1, k).astype(bf16), 1).astype(f32)
                for k, mine in enumerate(sums)
            ]
        return self.chip.scatter(lambda k: sums[k])

    def gather_seq_placed(self, value):
        blocks = self.seq.gather(value)
        whole = jnp.zeros((self.seq_count,) + value.shape, value.dtype)
        for k, block in enumerate(blocks):
            whole = lax.dynamic_update_index_in_dim(whole, block, self.seq_at(k), 0)
        return whole

    def gather_all(self, value):
        return self.gather_dp(self.gather_seq_placed(value))

    def scatter_seq_placed(self, whole):
        return self.seq.scatter(
            lambda k: lax.dynamic_index_in_dim(whole, self.seq_at(k), 0, keepdims=False)
        )

    def scatter_all(self, part):
        return self.scatter_seq_placed(self.scatter_dp(part).astype(bf16))


def exchange(totals, everyone, send_sem, recv_sem, count):
    me = lax.axis_index("seq")
    everyone[me] = totals[...]
    copies = []
    for step in range(1, count):
        peer = lax.rem(me + step, count)
        copy = pltpu.make_async_remote_copy(
            src_ref=totals,
            dst_ref=everyone.at[me],
            send_sem=send_sem.at[step],
            recv_sem=recv_sem.at[step],
            device_id={"seq": peer},
            device_id_type=pl.DeviceIdType.MESH,
        )
        copy.start()
    for step in range(1, count):
        source = lax.rem(me + count - step, count)
        copy = pltpu.make_async_remote_copy(
            src_ref=totals,
            dst_ref=everyone.at[source],
            send_sem=send_sem.at[step],
            recv_sem=recv_sem.at[step],
            device_id={"seq": source},
            device_id_type=pl.DeviceIdType.MESH,
        )
        copy.wait()


def greet(count):
    me = lax.axis_index("seq")
    barrier = pltpu.get_barrier_semaphore()
    for step in range(1, count):
        pl.semaphore_signal(
            barrier,
            inc=1,
            device_id={"seq": lax.rem(me + step, count)},
            device_id_type=pl.DeviceIdType.MESH,
        )
    pl.semaphore_wait(barrier, count - 1)


def tiles(channels):
    wide = 512 if channels % 512 == 0 else 128
    return [pl.ds(at, wide) for at in range(0, channels, wide)]


def tile_prefix(product, total, step):
    row = lax.broadcasted_iota(jnp.int32, product.shape, 0)
    reach = 1
    while reach < LANES:
        turn = reach if step > 0 else LANES - reach
        inside = row >= reach if step > 0 else row < LANES - reach
        total = total + product * jnp.where(inside, pltpu.roll(total, turn, 0), 0.0)
        product = product * jnp.where(inside, pltpu.roll(product, turn, 0), 1.0)
        reach *= 2
    return (product, total)


def scan_kernel(
    count, decay_ref, drive_ref, start_ref, state_ref, prev_ref, last_ref,
    totals, everyone, send_sem, recv_sem,
):
    greet(count)
    rows, channels = decay_ref.shape
    end = LANES - 1
    for cols in tiles(channels):

        def first_pass(t, carry):
            run_product, run_sum = carry
            at = pl.ds(pl.multiple_of(t * LANES, LANES), LANES)
            product, total = tile_prefix(decay_ref[at, cols], drive_ref[at, cols], 1)
            prev_ref[at, cols] = product
            state_ref[at, cols] = total
            last = product[end:]
            return (last * run_product, last * run_sum + total[end:])

        zero = jnp.zeros((1, cols.size), f32)
        run_product, run_sum = lax.fori_loop(
            0, rows // LANES, first_pass, (zero + 1.0, zero), unroll=4
        )
        totals[0:1, cols] = run_product
        totals[1:2, cols] = run_sum
    exchange(totals, everyone, send_sem, recv_sem, count)
    me = lax.axis_index("seq")
    for cols in tiles(channels):
        state = start_ref[0:1, cols]
        entering = state
        for device in range(count):
            entering = jnp.where(me == device, state, entering)
            state = everyone[device, 0:1, cols] * state + everyone[device, 1:2, cols]
        last_ref[0:1, cols] = state

        def second_pass(t, entry):
            at = pl.ds(pl.multiple_of(t * LANES, LANES), LANES)
            state = prev_ref[at, cols] * entry + state_ref[at, cols]
            row = lax.broadcasted_iota(jnp.int32, state.shape, 0)
            state_ref[at, cols] = state
            prev_ref[at, cols] = jnp.where(row == 0, entry, pltpu.roll(state, 1, 0))
            return state[end:]

        lax.fori_loop(0, rows // LANES, second_pass, entering, unroll=4)


def scan_back_kernel(
    count, decay_ref, d_state_ref, prev_ref, d_drive_ref, d_decay_ref,
    totals, everyone, send_sem, recv_sem,
):
    greet(count)
    rows, channels = decay_ref.shape
    last_tile = rows // LANES - 1
    end = LANES - 1
    for cols in tiles(channels):

        def first_pass(i, carry):
            run_product, run_sum = carry
            at = pl.ds(pl.multiple_of((last_tile - i) * LANES, LANES), LANES)
            decay = decay_ref[at, cols]
            product, total = tile_prefix(decay, decay * d_state_ref[at, cols], -1)
            d_decay_ref[at, cols] = product
            d_drive_ref[at, cols] = total
            first = product[:1]
            return (first * run_product, first * run_sum + total[:1])

        zero = jnp.zeros((1, cols.size), f32)
        run_product, run_sum = lax.fori_loop(
            0, rows // LANES, first_pass, (zero + 1.0, zero), unroll=4
        )
        totals[0:1, cols] = run_product
        totals[1:2, cols] = run_sum
    exchange(totals, everyone, send_sem, recv_sem, count)
    me = lax.axis_index("seq")
    for cols in tiles(channels):
        state = jnp.zeros((1, cols.size), f32)
        entering = state
        for device in reversed(range(count)):
            entering = jnp.where(me == device, state, entering)
            state = everyone[device, 0:1, cols] * state + everyone[device, 1:2, cols]

        def second_pass(i, entry):
            at = pl.ds(pl.multiple_of((last_tile - i) * LANES, LANES), LANES)
            outgoing = d_decay_ref[at, cols] * entry + d_drive_ref[at, cols]
            row = lax.broadcasted_iota(jnp.int32, outgoing.shape, 0)
            incoming = jnp.where(row == end, entry, pltpu.roll(outgoing, end, 0))
            carry = d_state_ref[at, cols] + incoming
            d_drive_ref[at, cols] = carry
            d_decay_ref[at, cols] = carry * prev_ref[at, cols]
            return outgoing[:1]

        lax.fori_loop(0, rows // LANES, second_pass, entering, unroll=4)


def scan_call(kernel, collective_id, count, operands, out_shapes):
    channels = operands[0].shape[1]
    vmem = pl.BlockSpec(memory_space=pltpu.VMEM)
    return pl.pallas_call(
        functools.partial(kernel, count),
        out_shape=out_shapes,
        in_specs=[vmem] * len(operands),
        out_specs=[vmem] * len(out_shapes),
        scratch_shapes=[
            pltpu.VMEM((2, channels), f32),
            pltpu.VMEM((count, 2, channels), f32),
            pltpu.SemaphoreType.DMA((count,)),
            pltpu.SemaphoreType.DMA((count,)),
        ],
        compiler_params=pltpu.CompilerParams(
            collective_id=collective_id, has_side_effects=True, vmem_limit_bytes=40 * 2**20
        ),
        cost_estimate=pl.CostEstimate(
            flops=8 * operands[0].size, bytes_accessed=20 * operands[0].size, transcendentals=0
        ),
    )(*operands)


def passed_along(value, axis, steps):
    count = lax.axis_size(axis)
    first, last = (max(0, -steps), min(count, count - steps))
    return lax.ppermute(value, axis, [(source, source + steps) for source in range(first, last)])


def gelu_tanh(values):
    return jax.nn.gelu(values, approximate=True)


def rms_parts(values, norm_gain):
    root_scale = lax.rsqrt(jnp.mean(values * values, axis=-1, keepdims=True) + epsilon)
    unit_rows = values * root_scale
    return (unit_rows * norm_gain, root_scale, unit_rows)


def norm_back(d_normed, norm_gain, root_scale, unit_rows):
    weighted = d_normed * norm_gain
    grad_gain = jnp.sum(d_normed * unit_rows, axis=0)
    d_values = root_scale * (
        weighted - unit_rows * jnp.mean(weighted * unit_rows, axis=-1, keepdims=True)
    )
    return (grad_gain, d_values)


def rows_of(values, first_row, row_count):
    return lax.slice_in_dim(values, first_row, first_row + row_count, axis=values.ndim - 2)


def gate_math(rate_pre, input_pre, conv_vals, decay_param, reset_col):
    rate = jax.nn.sigmoid(rate_pre)
    in_gate = jax.nn.sigmoid(input_pre)
    log_decay = -8.0 * jax.nn.softplus(-decay_param) * rate
    keep_mask = 1.0 - reset_col
    decay_rows = jnp.exp(log_decay) * keep_mask
    root_term = jnp.sqrt(jnp.maximum(-jnp.expm1(2.0 * log_decay), floor_value))
    drive_rows = (reset_col + keep_mask * root_term) * in_gate * conv_vals
    return (decay_rows, drive_rows)


def dot(left, right):
    return jnp.dot(left, right, preferred_element_type=f32)


def dot_t(left, right):
    return lax.dot_general(left, right, (((1,), (1,)), ((), ())), preferred_element_type=f32)


def t_dot(left, right):
    return lax.dot_general(left, right, (((0,), (0,)), ((), ())), preferred_element_type=f32)


def total(terms):
    result = terms[0]
    for term in terms[1:]:
        result = result + term
    return result


def per_device(
    inputs,
    reset,
    initial_state,
    cotangent,
    norm1_gain,
    w_gate,
    w_in,
    conv_w,
    conv_bias,
    w_rgate,
    rgate_bias,
    w_igate,
    igate_bias,
    decay_param,
    w_out,
    norm2_gain,
    w_ffgate,
    w_ffup,
    w_ffdown,
):
    net = Net()
    seqs_here, len_here, width = inputs.shape
    assert seqs_here == 1
    rows_here = len_here
    dp_count, seq_count = net.dp_count, net.seq_count
    devices = dp_count * seq_count
    chan_here, channels = w_rgate.shape[0], w_rgate.shape[0] * devices
    wide_here = norm1_gain.shape[0]
    head_count = channels // HW
    taps = conv_w.shape[0]
    rim_rows = taps - 1
    rel = net.rel()

    vectors = [norm1_gain, norm2_gain, conv_w.reshape(-1), conv_bias, rgate_bias, igate_bias, decay_param]
    lengths = [v.shape[0] for v in vectors]
    flat = jnp.concatenate(vectors)
    small_rows = -(-flat.shape[0] // HW)
    flat = jnp.pad(flat, (0, small_rows * HW - flat.shape[0]))
    packed = jnp.concatenate([w_rgate, w_igate, flat.reshape(small_rows, HW)], 0)
    pack_blocks = net.gather_all(packed)
    pack_all = jnp.zeros((dp_count,) + pack_blocks[0].shape, bf16)
    for (c, k), block in zip(rel, pack_blocks):
        pack_all = lax.dynamic_update_index_in_dim(pack_all, block, net.dp_at(c, k), 0)
    pack_all = pack_all.reshape((devices,) + packed.shape)
    full_rgate = pack_all[:, :chan_here].reshape(channels, HW)
    full_igate = pack_all[:, chan_here : 2 * chan_here].reshape(channels, HW)
    flat_all = pack_all[:, 2 * chan_here :].reshape(devices, small_rows * HW)
    pieces, at = [], 0
    for length in lengths:
        pieces.append(flat_all[:, at : at + length])
        at += length
    full_norm1 = pieces[0].reshape(-1).astype(f32)
    full_norm2 = pieces[1].reshape(-1).astype(f32)
    conv_wf = pieces[2].reshape(devices, taps, chan_here).transpose(1, 0, 2).reshape(taps, channels).astype(f32)
    full_cbias, full_rbias, full_ibias, decay_f = (p.reshape(-1).astype(f32) for p in pieces[3:])
    start_state = net.gather_seq_placed(initial_state).reshape(1, channels)

    in_blocks = [
        b.reshape(seq_count * wide_here, 2 * channels)
        for b in net.gather_all(jnp.concatenate([w_in, w_gate], 1))
    ]
    out_blocks = [b.reshape(seq_count * chan_here, width) for b in net.gather_all(w_out)]
    slab_gate = jnp.concatenate(net.gather_dp(w_ffgate), 0)
    slab_up = jnp.concatenate(net.gather_dp(w_ffup), 0)
    slab_down = jnp.concatenate(net.gather_dp(w_ffdown), 1)
    cotan_rows = cotangent.reshape(rows_here, width)
    group_cotan = jnp.concatenate(net.seq.gather(net.columns_out(cotan_rows)), 0)

    token_rows = inputs.reshape(rows_here, width).astype(f32)
    normed_f, scale_one, unit_one = rms_parts(token_rows, full_norm1)
    normed = net.columns_out(normed_f.astype(bf16))
    step_cols = width // dp_count
    normed_parts = [normed[:, i * step_cols : (i + 1) * step_cols] for i in range(dp_count)]
    both = total([dot(n, w) for n, w in zip(normed_parts, in_blocks)])
    branch = both[:, :channels].astype(bf16)
    gate_pre = both[:, channels:]
    reset_flags = reset.reshape(rows_here).astype(bf16)
    rim_branch, rim_flags = passed_along(
        (branch[len_here - rim_rows :], reset_flags[len_here - rim_rows :]), "seq", 1
    )
    padded = jnp.concatenate([rim_branch, branch], 0).astype(f32)
    open_pad = (1.0 - jnp.concatenate([rim_flags, reset_flags], 0).astype(f32))[:, None]
    open_masks = [None]
    conv_total = full_cbias + conv_wf[0] * rows_of(padded, rim_rows, len_here)
    running = rows_of(open_pad, rim_rows, len_here)
    for offset in range(1, rim_rows + 1):
        if offset > 1:
            running = running * rows_of(open_pad, rim_rows + 1 - offset, len_here)
        open_masks.append(running)
        conv_total = conv_total + running * conv_wf[offset] * rows_of(
            padded, rim_rows - offset, len_here
        )
    conv_low = conv_total.astype(bf16)
    conv_f = conv_low.astype(f32)
    head_view = conv_low.reshape(rows_here, head_count, HW)
    rgate_blocks = full_rgate.reshape(head_count, HW, HW)
    igate_blocks = full_igate.reshape(head_count, HW, HW)
    rate_pre = (
        jnp.einsum("nhi,hij->nhj", head_view, rgate_blocks, preferred_element_type=f32).reshape(
            rows_here, channels
        )
        + full_rbias
    )
    input_pre = (
        jnp.einsum("nhi,hij->nhj", head_view, igate_blocks, preferred_element_type=f32).reshape(
            rows_here, channels
        )
        + full_ibias
    )
    reset_col = reset.astype(f32).reshape(rows_here, 1)

    def gate_local(rate_in, input_in, conv_in, decay_in):
        return gate_math(rate_in, input_in, conv_in, decay_in, reset_col)

    (decay_rows, drive_rows), gate_grad_fn = jax.vjp(
        gate_local, rate_pre, input_pre, conv_f, decay_f
    )
    row_shape = jax.ShapeDtypeStruct((rows_here, channels), f32)
    states, prev_states, last_state = scan_call(
        scan_kernel,
        0,
        seq_count,
        (decay_rows, drive_rows, start_state),
        [row_shape, row_shape, jax.ShapeDtypeStruct((1, channels), f32)],
    )
    final_here = initial_state.shape[1]
    final_state = lax.dynamic_slice_in_dim(
        last_state, lax.axis_index("seq") * final_here, final_here, 1
    )
    state_f = states.astype(bf16).astype(f32)
    gate_act, gate_back = jax.vjp(gelu_tanh, gate_pre)
    mixed_rows = net.columns_out((state_f * gate_act).astype(bf16))
    step_chan = channels // dp_count
    mixed_parts = [mixed_rows[:, i * step_chan : (i + 1) * step_chan] for i in range(dp_count)]
    residual = token_rows + total([dot(m, w) for m, w in zip(mixed_parts, out_blocks)])

    normed_two_f, scale_two, unit_two = rms_parts(residual, full_norm2)
    normed_two = net.columns_out(normed_two_f.astype(bf16))
    group_normed = jnp.concatenate(net.seq.gather(normed_two), 0)
    ff_gate = dot(group_normed, slab_gate)
    ff_up = dot(group_normed, slab_up)
    ff_act, ff_back = jax.vjp(gelu_tanh, ff_gate)
    hidden = (ff_act * ff_up).astype(bf16)
    d_hidden = dot_t(group_cotan, slab_down)
    d_ffgate = ff_back(d_hidden * ff_up)[0].astype(bf16)
    d_ffup = (d_hidden * ff_act).astype(bf16)
    d_normed_part = (dot_t(d_ffgate, slab_gate) + dot_t(d_ffup, slab_up)).astype(bf16)
    out_part = dot(hidden, slab_down).astype(bf16)

    def block_rows(whole):
        return lambda k: whole[k * rows_here : (k + 1) * rows_here]

    d_normed_two = net.columns_back(net.seq.scatter(block_rows(d_normed_part)))
    ff_out = net.columns_back(net.seq.scatter(block_rows(out_part)))
    gate_part = t_dot(group_normed, d_ffgate).astype(bf16)
    up_part = t_dot(group_normed, d_ffup).astype(bf16)
    down_part = t_dot(hidden, group_cotan).astype(bf16)

    def dp_chunk(whole, axis):
        size = whole.shape[axis] // dp_count
        return lambda c, k: lax.slice_in_dim(
            whole, (c * net.chips + k) * size, (c * net.chips + k + 1) * size, axis=axis
        )

    grad_ffgate = net.scatter_dp(dp_chunk(gate_part, 0))
    grad_ffup = net.scatter_dp(dp_chunk(up_part, 0))
    grad_ffdown = net.scatter_dp(dp_chunk(down_part, 1))
    output = (residual + ff_out).astype(bf16).reshape(seqs_here, len_here, width)

    grad_norm2, d_resid_norm = norm_back(d_normed_two, full_norm2, scale_two, unit_two)
    d_residual = cotan_rows.astype(f32) + d_resid_norm
    d_residual_low = d_residual.astype(bf16)
    d_mixed = net.columns_back(jnp.concatenate([dot_t(d_residual_low, w) for w in out_blocks], 1))
    d_state = (d_mixed * gate_act).astype(bf16)
    d_gate_pre = gate_back(d_mixed * state_f)[0].astype(bf16)
    d_drive, d_decay = scan_call(
        scan_back_kernel,
        1,
        seq_count,
        (decay_rows, d_state.astype(f32), prev_states),
        [row_shape, row_shape],
    )

    def grad_all(parts, right):
        return net.scatter_all(
            lambda c, k: t_dot(parts[c * net.chips + k], right)
            .astype(bf16)
            .reshape(seq_count, -1, right.shape[1])
        )

    grad_out = grad_all(mixed_parts, d_residual_low)
    grad_gate = grad_all(normed_parts, d_gate_pre)
    d_rate_pre, d_input_pre, d_conv_direct, grad_decay = gate_grad_fn((d_decay, d_drive))
    d_rate_low = d_rate_pre.astype(bf16)
    d_input_low = d_input_pre.astype(bf16)
    d_rate_heads = d_rate_low.reshape(rows_here, head_count, HW)
    d_input_heads = d_input_low.reshape(rows_here, head_count, HW)
    grad_rgate = jnp.einsum("nhi,nhj->hij", head_view, d_rate_heads, preferred_element_type=f32)
    grad_igate = jnp.einsum("nhi,nhj->hij", head_view, d_input_heads, preferred_element_type=f32)
    grad_rbias = jnp.sum(d_rate_low.astype(f32), axis=0)
    grad_ibias = jnp.sum(d_input_low.astype(f32), axis=0)
    d_conv = (
        d_conv_direct
        + jnp.einsum("nhj,hij->nhi", d_rate_heads, rgate_blocks, preferred_element_type=f32).reshape(
            rows_here, channels
        )
        + jnp.einsum("nhj,hij->nhi", d_input_heads, igate_blocks, preferred_element_type=f32).reshape(
            rows_here, channels
        )
    )
    d_conv_low = d_conv.astype(bf16)
    rim_grad, rim_next = passed_along((d_conv_low[:rim_rows], reset_flags[:rim_rows]), "seq", -1)
    grad_ext = jnp.concatenate([d_conv_low, rim_grad], 0).astype(f32)
    open_next = (1.0 - jnp.concatenate([reset_flags, rim_next], 0).astype(f32))[:, None]
    d_conv_f = rows_of(grad_ext, 0, len_here)
    d_branch = conv_wf[0] * d_conv_f
    ahead = None
    conv_grads = [jnp.sum(rows_of(padded, rim_rows, len_here) * d_conv_f, axis=0)]
    for offset in range(1, rim_rows + 1):
        step_open = rows_of(open_next, offset, len_here)
        ahead = step_open if offset == 1 else ahead * step_open
        d_branch = d_branch + ahead * conv_wf[offset] * rows_of(grad_ext, offset, len_here)
        conv_grads.append(
            jnp.sum(
                open_masks[offset] * rows_of(padded, rim_rows - offset, len_here) * d_conv_f,
                axis=0,
            )
        )
    grad_conv = jnp.stack(conv_grads, 0)
    grad_cbias = jnp.sum(d_conv_f, axis=0)
    d_branch_low = d_branch.astype(bf16)
    grad_in = grad_all(normed_parts, d_branch_low)
    d_both = jnp.concatenate([d_branch_low, d_gate_pre], 1)
    d_normed_one = net.columns_back(jnp.concatenate([dot_t(d_both, w) for w in in_blocks], 1))
    grad_norm1, d_token_norm = norm_back(d_normed_one, full_norm1, scale_one, unit_one)
    input_grad = (d_residual + d_token_norm).reshape(seqs_here, len_here, width)

    conv_flat = grad_conv.reshape(taps, devices, chan_here).transpose(1, 0, 2)
    flat_grads = jnp.concatenate(
        [
            v.reshape(devices, -1)
            for v in (grad_norm1, grad_norm2, conv_flat, grad_cbias, grad_rbias, grad_ibias, grad_decay)
        ],
        1,
    )
    flat_grads = jnp.pad(flat_grads, ((0, 0), (0, small_rows * HW - flat_grads.shape[1])))
    pack_grads = jnp.concatenate(
        [
            grad_rgate.astype(bf16).reshape(devices, chan_here, HW),
            grad_igate.astype(bf16).reshape(devices, chan_here, HW),
            flat_grads.astype(bf16).reshape(devices, small_rows, HW),
        ],
        1,
    ).reshape(dp_count, seq_count, 2 * chan_here + small_rows, HW)
    pack_mine = net.scatter_all(
        lambda c, k: lax.dynamic_index_in_dim(pack_grads, net.dp_at(c, k), 0, keepdims=False)
    )
    flat_mine = pack_mine[2 * chan_here :].reshape(-1)
    mine, at = [], 0
    for length in lengths:
        mine.append(flat_mine[at : at + length])
        at += length
    return (
        output,
        input_grad,
        final_state,
        mine[0],
        grad_gate,
        grad_in,
        mine[2].reshape(taps, chan_here),
        mine[3],
        pack_mine[:chan_here],
        mine[4],
        pack_mine[chan_here : 2 * chan_here],
        mine[5],
        mine[6],
        grad_out,
        mine[1],
        grad_ffgate,
        grad_ffup,
        grad_ffdown,
    )


def solution(mesh):
    split = ("dp", "seq")
    return jax.shard_map(
        per_device,
        mesh=mesh,
        in_specs=(
            P("dp", "seq", None),
            P("dp", "seq"),
            P("dp", "seq"),
            P("dp", "seq", None),
            P(split),
            P(split, None),
            P(split, None),
            P(None, split),
            P(split),
            P(split, None),
            P(split),
            P(split, None),
            P(split),
            P(split),
            P(split, None),
            P(split),
            P("dp", "seq"),
            P("dp", "seq"),
            P("seq", "dp"),
        ),
        out_specs=(
            P("dp", "seq", None),
            P("dp", "seq", None),
            P("dp", "seq"),
            P(split),
            P(split, None),
            P(split, None),
            P(None, split),
            P(split),
            P(split, None),
            P(split),
            P(split, None),
            P(split),
            P(split),
            P(split, None),
            P(split),
            P("dp", "seq"),
            P("dp", "seq"),
            P("seq", "dp"),
        ),
        check_vma=False,
    )
```

```python
import functools

import jax
import jax.numpy as jnp
from jax import lax
from jax.experimental import pallas as pl
from jax.experimental.pallas import tpu as pltpu
from jax.sharding import PartitionSpec as P

HW = 256
LANES = 8


epsilon = 1e-06
floor_value = 0.0001
f32 = jnp.float32
bf16 = jnp.bfloat16


def seq_order(count):
    if count % 8:
        return list(range(count))
    wide = count // 4
    path = []
    for z in range(4):
        ys = range(1, wide) if z % 2 == 0 else range(wide - 1, 0, -1)
        path += [z * wide + y for y in ys]
    return path + [z * wide for z in (3, 2, 1, 0)]


class Ring:
    def __init__(self, axis, cycles):
        self.axis = axis
        self.cycles = cycles
        self.count = len(cycles[0])

    def shift(self, value, step):
        pairs = [
            (cycle[i], cycle[(i + step) % self.count])
            for cycle in self.cycles
            for i in range(self.count)
        ]
        return lax.ppermute(value, self.axis, pairs)

    def place(self):
        table = [0] * (self.count * len(self.cycles))
        for cycle in self.cycles:
            for i, device in enumerate(cycle):
                table[device] = i
        return jnp.asarray(table, jnp.int32)[lax.axis_index(self.axis)]

    def gather(self, value):
        count, half = self.count, self.count // 2
        blocks = [value] * count
        if count == 1:
            return blocks
        ahead = behind = value
        for step in range(1, half):
            behind = self.shift(behind, 1)
            ahead = self.shift(ahead, -1)
            blocks[count - step] = behind
            blocks[step] = ahead
        rows = value.shape[0]
        if half > 1 and rows % 32 == 0:
            top = self.shift(behind[: rows // 2], 1)
            bottom = self.shift(ahead[rows // 2 :], -1)
            blocks[half] = jnp.concatenate([top, bottom], 0)
        else:
            blocks[half] = self.shift(behind, 1)
        return blocks

    def scatter(self, part):
        count, half = self.count, self.count // 2
        if count == 1:
            return part(0).astype(f32)
        far = part(half).astype(bf16)
        if half == 1:
            return part(0).astype(f32) + self.shift(far, 1).astype(f32)
        rows = far.shape[0]
        cut = rows // 2 if rows % 32 == 0 else rows
        ahead, behind = far[:cut], far[cut:]
        for k in range(half - 1, 0, -1):
            got_ahead = self.shift(ahead, 1).astype(f32)
            mine_ahead = part(k).astype(f32)
            mine_behind = part(count - k).astype(f32)
            if k == half - 1 and cut == rows:
                ahead = (mine_ahead + got_ahead).astype(bf16)
                behind = mine_behind.astype(bf16)
                continue
            got_behind = self.shift(behind, -1).astype(f32)
            if k == half - 1:
                ahead = jnp.concatenate([mine_ahead[:cut] + got_ahead, mine_ahead[cut:]], 0)
                behind = jnp.concatenate([mine_behind[:cut], mine_behind[cut:] + got_behind], 0)
            else:
                ahead = mine_ahead + got_ahead
                behind = mine_behind + got_behind
            ahead, behind = ahead.astype(bf16), behind.astype(bf16)
        return (
            part(0).astype(f32)
            + self.shift(ahead, 1).astype(f32)
            + self.shift(behind, -1).astype(f32)
        )


class Net:
    def __init__(self):
        self.seq_count = lax.axis_size("seq")
        self.dp_count = lax.axis_size("dp")
        self.order = seq_order(self.seq_count)
        self.seq = Ring("seq", [self.order])
        self.cores = 2 if self.dp_count % 2 == 0 else 1
        self.chips = self.dp_count // self.cores
        cores, chips = self.cores, self.chips
        self.chip = Ring("dp", [[o * cores + c for o in range(chips)] for c in range(cores)])
        self.core = Ring("dp", [[o * cores + c for c in range(cores)] for o in range(chips)])
        self.place = self.seq.place()
        dp = lax.axis_index("dp")
        self.my_chip, self.my_core = dp // cores, dp % cores

    def seq_at(self, k):
        return jnp.asarray(self.order, jnp.int32)[(self.place + k) % self.seq_count]

    def rel(self):
        return [(c, k) for c in range(self.cores) for k in range(self.chips)]

    def dp_at(self, c, k):
        return ((self.my_chip + k) % self.chips) * self.cores + (self.my_core + c) % self.cores

    def columns_out(self, values):
        chunk = values.shape[1] // self.dp_count
        return jnp.concatenate(
            [lax.dynamic_slice_in_dim(values, self.dp_at(c, k) * chunk, chunk, 1) for c, k in self.rel()],
            1,
        )

    def columns_back(self, values):
        chunk = values.shape[1] // self.dp_count
        pieces = []
        for dp in range(self.dp_count):
            chip, core = dp // self.cores, dp % self.cores
            at = ((core - self.my_core) % self.cores) * self.chips + (chip - self.my_chip) % self.chips
            pieces.append(lax.dynamic_slice_in_dim(values, at * chunk, chunk, 1))
        return jnp.concatenate(pieces, 1)

    def gather_dp(self, value):
        blocks = self.chip.gather(value)
        if self.cores == 1:
            return blocks
        return blocks + [self.core.shift(block, 1) for block in blocks]

    def scatter_dp(self, part):
        sums = [part(0, k) for k in range(self.chips)]
        if self.cores > 1:
            sums = [
                mine.astype(f32) + self.core.shift(part(1, k).astype(bf16), 1).astype(f32)
                for k, mine in enumerate(sums)
            ]
        return self.chip.scatter(lambda k: sums[k])

    def gather_seq_placed(self, value):
        blocks = self.seq.gather(value)
        whole = jnp.zeros((self.seq_count,) + value.shape, value.dtype)
        for k, block in enumerate(blocks):
            whole = lax.dynamic_update_index_in_dim(whole, block, self.seq_at(k), 0)
        return whole

    def gather_all(self, value):
        return self.gather_dp(self.gather_seq_placed(value))

    def scatter_seq_placed(self, whole):
        return self.seq.scatter(
            lambda k: lax.dynamic_index_in_dim(whole, self.seq_at(k), 0, keepdims=False)
        )

    def scatter_all(self, part):
        return self.scatter_seq_placed(self.scatter_dp(part).astype(bf16))


def lookup(table, index):
    value = jnp.int32(table[0])
    for i, entry in enumerate(table):
        value = jnp.where(index == i, jnp.int32(entry), value)
    return value


class Links:
    def __init__(self, order, chips, cores):
        self.count, self.chips, self.cores = len(order), chips, cores
        me, dp = lax.axis_index("seq"), lax.axis_index("dp")
        count = self.count
        place = [0] * count
        for i, device in enumerate(order):
            place[device] = i
        self.seq_at = [
            lookup([order[(place[d] + k) % count] for d in range(count)], me) for k in range(count)
        ]
        self.ring = ({"seq": self.seq_at[1]}, {"seq": self.seq_at[count - 1]})
        chip, core = dp // cores, dp % cores
        self.chip = [
            {"dp": lax.rem(chip + step, chips) * cores + core} for step in range(1, chips)
        ]
        self.core = {"dp": chip * cores + (1 - core)} if cores == 2 else None

    def greet(self):
        barrier = pltpu.get_barrier_semaphore()
        peers = list(self.ring) + self.chip + ([self.core] if self.cores == 2 else [])
        for peer in peers:
            pl.semaphore_signal(
                barrier, inc=1, device_id=peer, device_id_type=pl.DeviceIdType.MESH
            )
        pl.semaphore_wait(barrier, len(peers))


def remote(source, target, send_sem, recv_sem, peer):
    return pltpu.make_async_remote_copy(
        src_ref=source,
        dst_ref=target,
        send_sem=send_sem,
        recv_sem=recv_sem,
        device_id=peer,
        device_id_type=pl.DeviceIdType.MESH,
    )


RING_FIRST, CHIP_FIRST, RING_ONLY = 0, 1, 2


def gather_kernel(order, chips, cores, pieces, arrays, *refs):
    ins, outs = refs[:arrays], refs[arrays : 2 * arrays]
    own_sem, recv_sem, ring_sem, chip_sem, core_sem = refs[2 * arrays :]
    links = Links(order, chips, cores)
    count, half = links.count, links.count // 2
    links.greet()

    owns = [
        pltpu.make_async_copy(ins[i], outs[i].at[0, links.seq_at[0]], own_sem.at[i])
        for i in range(arrays)
    ]
    for copy in owns:
        copy.start()
    sent = []

    def whole(p, r, k):
        array, first, rows, _ = pieces[p]
        place = outs[array].at[r, links.seq_at[k]]
        return place if rows == ins[array].shape[0] else place.at[pl.ds(first, rows)]

    def rows_in(p, r, k, first, rows):
        return outs[pieces[p][0]].at[r, links.seq_at[k], pl.ds(pieces[p][1] + first, rows)]

    def held(p, r, k):
        array, first, rows, _ = pieces[p]
        if r == 0 and k == 0:
            return ins[array] if rows == ins[array].shape[0] else ins[array].at[pl.ds(first, rows)]
        return whole(p, r, k)

    def cut_of(p):
        return pieces[p][2] // 32 * 16

    def start(copy):
        copy.start()
        sent.append(copy)

    def ring_copies(p, r, s):
        cut, rows = cut_of(p), pieces[p][2]
        if s < half - 1:
            return [
                remote(
                    held(p, r, (count - s) % count), whole(p, r, (count - s) % count),
                    ring_sem.at[p, r, 0, s], recv_sem.at[p, r, count - s - 1], links.ring[0],
                ),
                remote(
                    held(p, r, s), whole(p, r, s),
                    ring_sem.at[p, r, 1, s], recv_sem.at[p, r, s + 1], links.ring[1],
                ),
            ]
        back = count - s
        if not cut:
            return [
                remote(
                    whole(p, r, back), whole(p, r, back),
                    ring_sem.at[p, r, 0, s], recv_sem.at[p, r, half], links.ring[0],
                )
            ]
        top, bottom = rows_in(p, r, back, 0, cut), rows_in(p, r, s, cut, rows - cut)
        return [
            remote(top, top, ring_sem.at[p, r, 0, s], recv_sem.at[p, r, half], links.ring[0]),
            remote(
                bottom, bottom, ring_sem.at[p, r, 1, s], recv_sem.at[p, r, count], links.ring[1]
            ),
        ]

    def arrived(p, r, k):
        cut, rows = cut_of(p), pieces[p][2]
        if k == half and cut:
            for part, sem in (((0, cut), half), ((cut, rows - cut), count)):
                ref = rows_in(p, r, k, *part)
                remote(ref, ref, ring_sem.at[p, r, 0, 0], recv_sem.at[p, r, sem], links.ring[0]).wait_recv()
        else:
            ref = whole(p, r, k)
            remote(ref, ref, ring_sem.at[p, r, 0, 0], recv_sem.at[p, r, k], links.ring[0]).wait_recv()

    def to_chips(p, k):
        for step in range(1, chips):
            start(
                remote(
                    held(p, 0, k), whole(p, chips - step, k),
                    chip_sem.at[p, step - 1, k], recv_sem.at[p, chips - step, k], links.chip[step - 1],
                )
            )

    def to_core(p, r, k):
        if cores == 2:
            start(
                remote(
                    held(p, r, k), whole(p, chips + r, k),
                    core_sem.at[p, r, k], recv_sem.at[p, chips + r, k], links.core,
                )
            )

    method = [piece[3] for piece in pieces]
    everyone = range(len(pieces))

    def planes(p):
        return range(chips) if method[p] == CHIP_FIRST else range(1)

    for p in everyone:
        if method[p] != RING_ONLY:
            to_chips(p, 0)
        for copy in ring_copies(p, 0, 0):
            start(copy)
    for p in everyone:
        if method[p] != RING_ONLY:
            to_core(p, 0, 0)
    for s in range(1, half + 1):
        steps = sorted({count - s, s})
        before = sorted({(count - s + 1) % count, s - 1})
        for p in everyone:
            for r in planes(p):
                if r == 0 or s > 1:
                    for k in steps:
                        arrived(p, r, k)
                    if s < half:
                        for copy in ring_copies(p, r, s):
                            start(copy)
                    if method[p] == RING_FIRST:
                        for k in steps:
                            to_chips(p, k)
                    if method[p] != RING_ONLY:
                        for k in steps:
                            to_core(p, r, k)
        for p in everyone:
            if method[p] == RING_FIRST:
                for r in range(1, chips):
                    for k in before:
                        arrived_from_chip(links, whole(p, r, k), chip_sem.at[p, 0, 0], recv_sem.at[p, r, k])
                        to_core(p, r, k)
            if method[p] == CHIP_FIRST and s == 1:
                for r in range(1, chips):
                    arrived_from_chip(links, whole(p, r, 0), chip_sem.at[p, 0, 0], recv_sem.at[p, r, 0])
                    for copy in ring_copies(p, r, 0):
                        start(copy)
                    to_core(p, r, 0)
                for r in range(1, chips):
                    for k in steps:
                        arrived(p, r, k)
                    if s < half:
                        for copy in ring_copies(p, r, s):
                            start(copy)
                    for k in steps:
                        to_core(p, r, k)
    for p in everyone:
        if method[p] == RING_FIRST:
            for r in range(1, chips):
                arrived_from_chip(links, whole(p, r, half), chip_sem.at[p, 0, 0], recv_sem.at[p, r, half])
                to_core(p, r, half)
    for p in everyone:
        if method[p] != RING_ONLY and cores == 2:
            for r in range(chips):
                for k in range(count):
                    arrived_from_chip(
                        links, whole(p, chips + r, k), core_sem.at[p, r, k], recv_sem.at[p, chips + r, k]
                    )
    for copy in sent:
        copy.wait_send()
    for copy in owns:
        copy.wait()


def arrived_from_chip(links, ref, send_sem, recv_sem):
    remote(ref, ref, send_sem, recv_sem, links.ring[0]).wait_recv()


def gather_call(net, arrays, pieces):
    chips, cores, count = net.chips, net.cores, net.seq_count
    slots = chips * cores
    only_ring = {piece[0] for piece in pieces if piece[3] == RING_ONLY}
    anywhere = pl.BlockSpec(memory_space=pl.ANY)
    return pl.pallas_call(
        functools.partial(gather_kernel, net.order, chips, cores, pieces, len(arrays)),
        out_shape=[
            jax.ShapeDtypeStruct((1 if i in only_ring else slots, count) + v.shape, v.dtype)
            for i, v in enumerate(arrays)
        ],
        in_specs=[anywhere] * len(arrays),
        out_specs=[anywhere] * len(arrays),
        scratch_shapes=[
            pltpu.SemaphoreType.DMA((len(arrays),)),
            pltpu.SemaphoreType.DMA((len(pieces), slots, count + 1)),
            pltpu.SemaphoreType.DMA((len(pieces), chips, 2, count // 2)),
            pltpu.SemaphoreType.DMA((len(pieces), max(chips - 1, 1), count)),
            pltpu.SemaphoreType.DMA((len(pieces), chips, count)),
        ],
        compiler_params=pltpu.CompilerParams(
            collective_id=3, has_side_effects=True, vmem_limit_bytes=32 * 2**20
        ),
        cost_estimate=pl.CostEstimate(
            flops=0, bytes_accessed=slots * count * sum(v.size for v in arrays) * 4, transcendentals=0
        ),
    )(*arrays)


def exchange(totals, everyone, send_sem, recv_sem, count):
    me = lax.axis_index("seq")
    everyone[me] = totals[...]
    copies = []
    for step in range(1, count):
        peer = lax.rem(me + step, count)
        copy = pltpu.make_async_remote_copy(
            src_ref=totals,
            dst_ref=everyone.at[me],
            send_sem=send_sem.at[step],
            recv_sem=recv_sem.at[step],
            device_id={"seq": peer},
            device_id_type=pl.DeviceIdType.MESH,
        )
        copy.start()
    for step in range(1, count):
        source = lax.rem(me + count - step, count)
        copy = pltpu.make_async_remote_copy(
            src_ref=totals,
            dst_ref=everyone.at[source],
            send_sem=send_sem.at[step],
            recv_sem=recv_sem.at[step],
            device_id={"seq": source},
            device_id_type=pl.DeviceIdType.MESH,
        )
        copy.wait()


def greet(count):
    me = lax.axis_index("seq")
    barrier = pltpu.get_barrier_semaphore()
    for step in range(1, count):
        pl.semaphore_signal(
            barrier,
            inc=1,
            device_id={"seq": lax.rem(me + step, count)},
            device_id_type=pl.DeviceIdType.MESH,
        )
    pl.semaphore_wait(barrier, count - 1)


def tiles(channels):
    wide = 512 if channels % 512 == 0 else 128
    return [pl.ds(at, wide) for at in range(0, channels, wide)]


def tile_prefix(product, total, step):
    row = lax.broadcasted_iota(jnp.int32, product.shape, 0)
    reach = 1
    while reach < LANES:
        turn = reach if step > 0 else LANES - reach
        inside = row >= reach if step > 0 else row < LANES - reach
        total = total + product * jnp.where(inside, pltpu.roll(total, turn, 0), 0.0)
        product = product * jnp.where(inside, pltpu.roll(product, turn, 0), 1.0)
        reach *= 2
    return (product, total)


def scan_kernel(
    count, decay_ref, drive_ref, start_ref, state_ref, prev_ref, last_ref,
    totals, everyone, send_sem, recv_sem,
):
    greet(count)
    rows, channels = decay_ref.shape
    end = LANES - 1
    for cols in tiles(channels):

        def first_pass(t, carry):
            run_product, run_sum = carry
            at = pl.ds(pl.multiple_of(t * LANES, LANES), LANES)
            product, total = tile_prefix(decay_ref[at, cols], drive_ref[at, cols], 1)
            prev_ref[at, cols] = product
            state_ref[at, cols] = total
            last = product[end:]
            return (last * run_product, last * run_sum + total[end:])

        zero = jnp.zeros((1, cols.size), f32)
        run_product, run_sum = lax.fori_loop(
            0, rows // LANES, first_pass, (zero + 1.0, zero), unroll=4
        )
        totals[0:1, cols] = run_product
        totals[1:2, cols] = run_sum
    exchange(totals, everyone, send_sem, recv_sem, count)
    me = lax.axis_index("seq")
    for cols in tiles(channels):
        state = start_ref[0:1, cols]
        entering = state
        for device in range(count):
            entering = jnp.where(me == device, state, entering)
            state = everyone[device, 0:1, cols] * state + everyone[device, 1:2, cols]
        last_ref[0:1, cols] = state

        def second_pass(t, entry):
            at = pl.ds(pl.multiple_of(t * LANES, LANES), LANES)
            state = prev_ref[at, cols] * entry + state_ref[at, cols]
            row = lax.broadcasted_iota(jnp.int32, state.shape, 0)
            state_ref[at, cols] = state
            prev_ref[at, cols] = jnp.where(row == 0, entry, pltpu.roll(state, 1, 0))
            return state[end:]

        lax.fori_loop(0, rows // LANES, second_pass, entering, unroll=4)


def scan_back_kernel(
    count, decay_ref, d_state_ref, prev_ref, d_drive_ref, d_decay_ref,
    totals, everyone, send_sem, recv_sem,
):
    greet(count)
    rows, channels = decay_ref.shape
    last_tile = rows // LANES - 1
    end = LANES - 1
    for cols in tiles(channels):

        def first_pass(i, carry):
            run_product, run_sum = carry
            at = pl.ds(pl.multiple_of((last_tile - i) * LANES, LANES), LANES)
            decay = decay_ref[at, cols]
            product, total = tile_prefix(decay, decay * d_state_ref[at, cols], -1)
            d_decay_ref[at, cols] = product
            d_drive_ref[at, cols] = total
            first = product[:1]
            return (first * run_product, first * run_sum + total[:1])

        zero = jnp.zeros((1, cols.size), f32)
        run_product, run_sum = lax.fori_loop(
            0, rows // LANES, first_pass, (zero + 1.0, zero), unroll=4
        )
        totals[0:1, cols] = run_product
        totals[1:2, cols] = run_sum
    exchange(totals, everyone, send_sem, recv_sem, count)
    me = lax.axis_index("seq")
    for cols in tiles(channels):
        state = jnp.zeros((1, cols.size), f32)
        entering = state
        for device in reversed(range(count)):
            entering = jnp.where(me == device, state, entering)
            state = everyone[device, 0:1, cols] * state + everyone[device, 1:2, cols]

        def second_pass(i, entry):
            at = pl.ds(pl.multiple_of((last_tile - i) * LANES, LANES), LANES)
            outgoing = d_decay_ref[at, cols] * entry + d_drive_ref[at, cols]
            row = lax.broadcasted_iota(jnp.int32, outgoing.shape, 0)
            incoming = jnp.where(row == end, entry, pltpu.roll(outgoing, end, 0))
            carry = d_state_ref[at, cols] + incoming
            d_drive_ref[at, cols] = carry
            d_decay_ref[at, cols] = carry * prev_ref[at, cols]
            return outgoing[:1]

        lax.fori_loop(0, rows // LANES, second_pass, entering, unroll=4)


def scan_call(kernel, collective_id, count, operands, out_shapes):
    channels = operands[0].shape[1]
    vmem = pl.BlockSpec(memory_space=pltpu.VMEM)
    return pl.pallas_call(
        functools.partial(kernel, count),
        out_shape=out_shapes,
        in_specs=[vmem] * len(operands),
        out_specs=[vmem] * len(out_shapes),
        scratch_shapes=[
            pltpu.VMEM((2, channels), f32),
            pltpu.VMEM((count, 2, channels), f32),
            pltpu.SemaphoreType.DMA((count,)),
            pltpu.SemaphoreType.DMA((count,)),
        ],
        compiler_params=pltpu.CompilerParams(
            collective_id=collective_id, has_side_effects=True, vmem_limit_bytes=40 * 2**20
        ),
        cost_estimate=pl.CostEstimate(
            flops=8 * operands[0].size, bytes_accessed=20 * operands[0].size, transcendentals=0
        ),
    )(*operands)


def pair_slots(count):
    half = count // 2
    return [k for s in range(1, half) for k in (count - s, s)] + [half, 0]


def gelu_parts(v):
    root, cubic = 0.7978845608028654, 0.044715
    curve = jnp.tanh(root * (v + cubic * v * v * v))
    act = 0.5 * v * (1.0 + curve)
    slope = 0.5 * (1.0 + curve) + 0.5 * v * (1.0 - curve * curve) * root * (
        1.0 + 3.0 * cubic * v * v
    )
    return (act, slope)


def contract(left, right, left_dim, right_dim):
    return lax.dot_general(
        left, right, (((left_dim,), (right_dim,)), ((), ())), preferred_element_type=f32
    )


def ff_kernel(
    order, own_ref, cot_ref, gate_hbm, up_hbm, down_hbm,
    blocks_ref, hidden_ref, d_gate_ref, d_up_ref, out_ref, d_in_ref,
    gate_ref, up_ref, down_ref, rows_ref, cots_ref, h_ref, g_ref, u_ref, o_ref, d_ref,
    send_sem, recv_sem, load_sem, store_sem,
):
    count = len(order)
    half = count // 2
    rows, width = own_ref.shape
    hidden_here = gate_ref.shape[1]
    cut = rows // 2
    me = lax.axis_index("seq")
    ahead_of, behind_of = [0] * count, [0] * count
    for i, device in enumerate(order):
        ahead_of[device] = order[(i + 1) % count]
        behind_of[device] = order[(i - 1) % count]
    sides = (lookup(ahead_of, me), lookup(behind_of, me))

    barrier = pltpu.get_barrier_semaphore()
    for side in sides:
        pl.semaphore_signal(
            barrier, inc=1, device_id={"seq": side}, device_id_type=pl.DeviceIdType.MESH
        )
    weights = [
        pltpu.make_async_copy(hbm, vmem, load_sem.at[i])
        for i, (hbm, vmem) in enumerate(
            ((gate_hbm, gate_ref), (up_hbm, up_ref), (down_hbm, down_ref))
        )
    ]
    for copy in weights:
        copy.start()
    keep = pltpu.make_async_copy(own_ref, blocks_ref.at[count - 1], load_sem.at[3])
    keep.start()
    pl.semaphore_wait(barrier, 2)

    def full(side, source, slot, s):
        return pltpu.make_async_remote_copy(
            src_ref=source,
            dst_ref=blocks_ref.at[slot],
            send_sem=send_sem.at[side, s],
            recv_sem=recv_sem.at[slot],
            device_id={"seq": sides[side]},
            device_id_type=pl.DeviceIdType.MESH,
        )

    def part(side):
        at = pl.ds(0, cut) if side == 0 else pl.ds(cut, rows - cut)
        return pltpu.make_async_remote_copy(
            src_ref=blocks_ref.at[2 * (half - 2) + side, at],
            dst_ref=blocks_ref.at[count - 2, at],
            send_sem=send_sem.at[side, half - 1],
            recv_sem=recv_sem.at[count - 2 + side],
            device_id={"seq": sides[side]},
            device_id_type=pl.DeviceIdType.MESH,
        )

    for side in range(2):
        full(side, own_ref, side, 0).start()
    keep.wait()
    for copy in weights:
        copy.wait()

    def loads(s):
        return [
            pltpu.make_async_copy(blocks_ref.at[pl.ds(2 * (s - 1), 2)], rows_ref, load_sem.at[4]),
            pltpu.make_async_copy(cot_ref.at[pl.ds(2 * (s - 1), 2)], cots_ref, load_sem.at[5]),
        ]

    def stores(s):
        return [
            pltpu.make_async_copy(vmem, hbm.at[s - 1], store_sem.at[i])
            for i, (vmem, hbm) in enumerate(
                (
                    (h_ref, hidden_ref),
                    (g_ref, d_gate_ref),
                    (u_ref, d_up_ref),
                    (o_ref, out_ref),
                    (d_ref, d_in_ref),
                )
            )
        ]

    def step(s, carry):
        @pl.when(s < half)
        def _():
            for side in range(2):
                full(side, own_ref, 2 * (s - 1) + side, s).wait_recv()

            @pl.when(s < half - 1)
            def _():
                for side in range(2):
                    slot = 2 * (s - 1) + side
                    full(side, blocks_ref.at[slot], slot + 2, s).start()

            @pl.when(s == half - 1)
            def _():
                for side in range(2):
                    part(side).start()

        @pl.when(s == half)
        def _():
            for side in range(2):
                part(side).wait_recv()

        for copy in loads(s):
            copy.start()

        @pl.when(s > 1)
        def _():
            for copy in stores(s - 1):
                copy.wait()

        for copy in loads(s):
            copy.wait()
        wide = 256 if hidden_here % 256 == 0 else 128

        def inner(j, carry):
            at = pl.ds(pl.multiple_of(j * wide, wide), wide)
            x = rows_ref[...].reshape(2 * rows, width)
            c = cots_ref[...].reshape(2 * rows, width)
            ff_gate = contract(x, gate_ref[:, at], 1, 0)
            ff_up = contract(x, up_ref[:, at], 1, 0)
            d_hidden = contract(c, down_ref[at, :], 1, 1)
            act, slope = gelu_parts(ff_gate)
            h_ref[:, at] = (act * ff_up).astype(bf16)
            g_ref[:, at] = (d_hidden * ff_up * slope).astype(bf16)
            u_ref[:, at] = (d_hidden * act).astype(bf16)
            return carry

        lax.fori_loop(0, hidden_here // wide, inner, 0)
        out_wide = 512

        def outer(j, carry):
            at = pl.ds(pl.multiple_of(j * out_wide, out_wide), out_wide)
            o_ref[:, at] = contract(h_ref[...], down_ref[:, at], 1, 0).astype(bf16)
            d_ref[:, at] = (
                contract(g_ref[...], gate_ref[at, :], 1, 1)
                + contract(u_ref[...], up_ref[at, :], 1, 1)
            ).astype(bf16)
            return carry

        lax.fori_loop(0, width // out_wide, outer, 0)
        for copy in stores(s):
            copy.start()
        return carry

    lax.fori_loop(1, half + 1, step, 0)
    for copy in stores(half):
        copy.wait()
    for side in range(2):
        for s in range(half - 1):
            full(side, own_ref, side, s).wait_send()
        part(side).wait_send()


def ff_call(order, own, cot, slab_gate, slab_up, slab_down):
    rows, width = own.shape
    count, half = len(order), len(order) // 2
    hidden_here = slab_gate.shape[1]
    anywhere = pl.BlockSpec(memory_space=pl.ANY)
    pair = 2 * rows
    shape = jax.ShapeDtypeStruct
    flops = 12 * count * rows * width * hidden_here
    return pl.pallas_call(
        functools.partial(ff_kernel, order),
        out_shape=[shape((count, rows, width), bf16)]
        + [shape((half, pair, hidden_here), bf16)] * 3
        + [shape((half, pair, width), bf16)] * 2,
        in_specs=[anywhere] * 5,
        out_specs=[anywhere] * 6,
        scratch_shapes=[
            pltpu.VMEM((width, hidden_here), bf16),
            pltpu.VMEM((width, hidden_here), bf16),
            pltpu.VMEM((hidden_here, width), bf16),
            pltpu.VMEM((2, rows, width), bf16),
            pltpu.VMEM((2, rows, width), bf16),
            pltpu.VMEM((pair, hidden_here), bf16),
            pltpu.VMEM((pair, hidden_here), bf16),
            pltpu.VMEM((pair, hidden_here), bf16),
            pltpu.VMEM((pair, width), bf16),
            pltpu.VMEM((pair, width), bf16),
            pltpu.SemaphoreType.DMA((2, half)),
            pltpu.SemaphoreType.DMA((count,)),
            pltpu.SemaphoreType.DMA((6,)),
            pltpu.SemaphoreType.DMA((5,)),
        ],
        compiler_params=pltpu.CompilerParams(
            collective_id=2, has_side_effects=True, vmem_limit_bytes=48 * 2**20
        ),
        cost_estimate=pl.CostEstimate(
            flops=flops, bytes_accessed=60 * 2**20, transcendentals=count * rows * hidden_here
        ),
    )(own, cot, slab_gate, slab_up, slab_down)


def passed_along(value, axis, steps):
    count = lax.axis_size(axis)
    first, last = (max(0, -steps), min(count, count - steps))
    return lax.ppermute(value, axis, [(source, source + steps) for source in range(first, last)])


def gelu_tanh(values):
    return jax.nn.gelu(values, approximate=True)


def rms_parts(values, norm_gain):
    root_scale = lax.rsqrt(jnp.mean(values * values, axis=-1, keepdims=True) + epsilon)
    unit_rows = values * root_scale
    return (unit_rows * norm_gain, root_scale, unit_rows)


def norm_back(d_normed, norm_gain, root_scale, unit_rows):
    weighted = d_normed * norm_gain
    grad_gain = jnp.sum(d_normed * unit_rows, axis=0)
    d_values = root_scale * (
        weighted - unit_rows * jnp.mean(weighted * unit_rows, axis=-1, keepdims=True)
    )
    return (grad_gain, d_values)


def rows_of(values, first_row, row_count):
    return lax.slice_in_dim(values, first_row, first_row + row_count, axis=values.ndim - 2)


def gate_math(rate_pre, input_pre, conv_vals, decay_param, reset_col):
    rate = jax.nn.sigmoid(rate_pre)
    in_gate = jax.nn.sigmoid(input_pre)
    log_decay = -8.0 * jax.nn.softplus(-decay_param) * rate
    keep_mask = 1.0 - reset_col
    decay_rows = jnp.exp(log_decay) * keep_mask
    root_term = jnp.sqrt(jnp.maximum(-jnp.expm1(2.0 * log_decay), floor_value))
    drive_rows = (reset_col + keep_mask * root_term) * in_gate * conv_vals
    return (decay_rows, drive_rows)


def dot(left, right):
    return jnp.dot(left, right, preferred_element_type=f32)


def dot_t(left, right):
    return lax.dot_general(left, right, (((1,), (1,)), ((), ())), preferred_element_type=f32)


def t_dot(left, right):
    return lax.dot_general(left, right, (((0,), (0,)), ((), ())), preferred_element_type=f32)


def total(terms):
    result = terms[0]
    for term in terms[1:]:
        result = result + term
    return result


def per_device(
    inputs,
    reset,
    initial_state,
    cotangent,
    norm1_gain,
    w_gate,
    w_in,
    conv_w,
    conv_bias,
    w_rgate,
    rgate_bias,
    w_igate,
    igate_bias,
    decay_param,
    w_out,
    norm2_gain,
    w_ffgate,
    w_ffup,
    w_ffdown,
):
    net = Net()
    seqs_here, len_here, width = inputs.shape
    assert seqs_here == 1
    rows_here = len_here
    dp_count, seq_count = net.dp_count, net.seq_count
    devices = dp_count * seq_count
    chan_here, channels = w_rgate.shape[0], w_rgate.shape[0] * devices
    wide_here = norm1_gain.shape[0]
    head_count = channels // HW
    taps = conv_w.shape[0]
    rim_rows = taps - 1
    rel = net.rel()

    vectors = [norm1_gain, norm2_gain, conv_w.reshape(-1), conv_bias, rgate_bias, igate_bias, decay_param]
    lengths = [v.shape[0] for v in vectors]
    flat = jnp.concatenate(vectors)
    small_rows = -(-flat.shape[0] // HW)
    small_rows += -(2 * chan_here + small_rows) % 16
    flat = jnp.pad(flat, (0, small_rows * HW - flat.shape[0]))
    packed = jnp.concatenate([w_rgate, w_igate, flat.reshape(small_rows, HW)], 0)
    half_rows = chan_here * 3 // 5 // 16 * 16
    out_pieces = [(3, 0, half_rows, RING_FIRST), (3, half_rows, chan_here - half_rows, CHIP_FIRST)]
    if half_rows == 0 or chan_here % 16:
        out_pieces = [(3, 0, chan_here, RING_FIRST)]
    pack_got, in_got, gate_got, out_got, start_got = gather_call(
        net,
        (packed, w_in, w_gate, w_out, initial_state),
        [
            (0, 0, packed.shape[0], RING_FIRST),
            (1, 0, wide_here, RING_FIRST),
            (2, 0, wide_here, CHIP_FIRST),
        ]
        + out_pieces
        + [(4, 0, 1, RING_ONLY)],
    )
    pack_blocks = [pack_got[i] for i in range(dp_count)]
    pack_all = jnp.zeros((dp_count,) + pack_blocks[0].shape, bf16)
    for (c, k), block in zip(rel, pack_blocks):
        pack_all = lax.dynamic_update_index_in_dim(pack_all, block, net.dp_at(c, k), 0)
    pack_all = pack_all.reshape((devices,) + packed.shape)
    full_rgate = pack_all[:, :chan_here].reshape(channels, HW)
    full_igate = pack_all[:, chan_here : 2 * chan_here].reshape(channels, HW)
    flat_all = pack_all[:, 2 * chan_here :].reshape(devices, small_rows * HW)
    pieces, at = [], 0
    for length in lengths:
        pieces.append(flat_all[:, at : at + length])
        at += length
    full_norm1 = pieces[0].reshape(-1).astype(f32)
    full_norm2 = pieces[1].reshape(-1).astype(f32)
    conv_wf = pieces[2].reshape(devices, taps, chan_here).transpose(1, 0, 2).reshape(taps, channels).astype(f32)
    full_cbias, full_rbias, full_ibias, decay_f = (p.reshape(-1).astype(f32) for p in pieces[3:])
    start_state = start_got.reshape(1, channels)

    in_blocks, gate_blocks = (
        [got[i].reshape(seq_count * wide_here, channels) for i in range(dp_count)]
        for got in (in_got, gate_got)
    )
    out_blocks = [out_got[i].reshape(seq_count * chan_here, width) for i in range(dp_count)]
    w_ffgate, w_ffup, w_ffdown, cotangent, in_blocks[0] = lax.optimization_barrier(
        (w_ffgate, w_ffup, w_ffdown, cotangent, in_blocks[0])
    )
    slab_gate = jnp.concatenate(net.gather_dp(w_ffgate), 0)
    slab_up = jnp.concatenate(net.gather_dp(w_ffup), 0)
    slab_down = jnp.concatenate(net.gather_dp(w_ffdown), 1)
    cotan_rows = cotangent.reshape(rows_here, width)
    cot_blocks = net.seq.gather(net.columns_out(cotan_rows))
    slots = pair_slots(seq_count)
    group_cotan = jnp.stack([cot_blocks[k] for k in slots], 0)

    token_rows = inputs.reshape(rows_here, width).astype(f32)
    normed_f, scale_one, unit_one = rms_parts(token_rows, full_norm1)
    normed = net.columns_out(normed_f.astype(bf16))
    step_cols = width // dp_count
    normed_parts = [normed[:, i * step_cols : (i + 1) * step_cols] for i in range(dp_count)]
    branch = total([dot(n, w) for n, w in zip(normed_parts, in_blocks)]).astype(bf16)
    gate_pre = total([dot(n, w) for n, w in zip(normed_parts, gate_blocks)])
    reset_flags = reset.reshape(rows_here).astype(bf16)
    rim_branch, rim_flags = passed_along(
        (branch[len_here - rim_rows :], reset_flags[len_here - rim_rows :]), "seq", 1
    )
    padded = jnp.concatenate([rim_branch, branch], 0).astype(f32)
    open_pad = (1.0 - jnp.concatenate([rim_flags, reset_flags], 0).astype(f32))[:, None]
    open_masks = [None]
    conv_total = full_cbias + conv_wf[0] * rows_of(padded, rim_rows, len_here)
    running = rows_of(open_pad, rim_rows, len_here)
    for offset in range(1, rim_rows + 1):
        if offset > 1:
            running = running * rows_of(open_pad, rim_rows + 1 - offset, len_here)
        open_masks.append(running)
        conv_total = conv_total + running * conv_wf[offset] * rows_of(
            padded, rim_rows - offset, len_here
        )
    conv_low = conv_total.astype(bf16)
    conv_f = conv_low.astype(f32)
    head_view = conv_low.reshape(rows_here, head_count, HW)
    rgate_blocks = full_rgate.reshape(head_count, HW, HW)
    igate_blocks = full_igate.reshape(head_count, HW, HW)
    rate_pre = (
        jnp.einsum("nhi,hij->nhj", head_view, rgate_blocks, preferred_element_type=f32).reshape(
            rows_here, channels
        )
        + full_rbias
    )
    input_pre = (
        jnp.einsum("nhi,hij->nhj", head_view, igate_blocks, preferred_element_type=f32).reshape(
            rows_here, channels
        )
        + full_ibias
    )
    reset_col = reset.astype(f32).reshape(rows_here, 1)

    def gate_local(rate_in, input_in, conv_in, decay_in):
        return gate_math(rate_in, input_in, conv_in, decay_in, reset_col)

    (decay_rows, drive_rows), gate_grad_fn = jax.vjp(
        gate_local, rate_pre, input_pre, conv_f, decay_f
    )
    row_shape = jax.ShapeDtypeStruct((rows_here, channels), f32)
    states, prev_states, last_state = scan_call(
        scan_kernel,
        0,
        seq_count,
        (decay_rows, drive_rows, start_state),
        [row_shape, row_shape, jax.ShapeDtypeStruct((1, channels), f32)],
    )
    final_here = initial_state.shape[1]
    final_state = lax.dynamic_slice_in_dim(
        last_state, lax.axis_index("seq") * final_here, final_here, 1
    )
    state_f = states.astype(bf16).astype(f32)
    gate_act, gate_back = jax.vjp(gelu_tanh, gate_pre)
    mixed_rows = net.columns_out((state_f * gate_act).astype(bf16))
    step_chan = channels // dp_count
    mixed_parts = [mixed_rows[:, i * step_chan : (i + 1) * step_chan] for i in range(dp_count)]
    residual = token_rows + total([dot(m, w) for m, w in zip(mixed_parts, out_blocks)])

    normed_two_f, scale_two, unit_two = rms_parts(residual, full_norm2)
    normed_two = net.columns_out(normed_two_f.astype(bf16))
    group_normed, hidden, d_ffgate, d_ffup, out_part, d_normed_part = ff_call(
        net.order, normed_two, group_cotan, slab_gate, slab_up, slab_down
    )
    group_rows = seq_count * rows_here
    group_normed = group_normed.reshape(group_rows, width)
    group_cotan = group_cotan.reshape(group_rows, width)
    hidden, d_ffgate, d_ffup = (v.reshape(group_rows, -1) for v in (hidden, d_ffgate, d_ffup))

    def block_rows(whole):
        whole = whole.reshape(seq_count, rows_here, width)
        return lambda k: whole[slots.index(k)]

    d_normed_sum = net.seq.scatter(block_rows(d_normed_part))
    d_normed_sum, out_part = lax.optimization_barrier((d_normed_sum, out_part))
    d_normed_two = net.columns_back(d_normed_sum)
    ff_out = net.columns_back(net.seq.scatter(block_rows(out_part)))
    gate_part = t_dot(group_normed, d_ffgate).astype(bf16)
    up_part = t_dot(group_normed, d_ffup).astype(bf16)
    down_part = t_dot(hidden, group_cotan).astype(bf16)

    def dp_chunk(whole, axis):
        size = whole.shape[axis] // dp_count
        return lambda c, k: lax.slice_in_dim(
            whole, (c * net.chips + k) * size, (c * net.chips + k + 1) * size, axis=axis
        )

    grad_ffgate = net.scatter_dp(dp_chunk(gate_part, 0))
    grad_ffup = net.scatter_dp(dp_chunk(up_part, 0))
    grad_ffdown = net.scatter_dp(dp_chunk(down_part, 1))
    output = (residual + ff_out).astype(bf16).reshape(seqs_here, len_here, width)

    grad_norm2, d_resid_norm = norm_back(d_normed_two, full_norm2, scale_two, unit_two)
    d_residual = cotan_rows.astype(f32) + d_resid_norm
    d_residual_low = d_residual.astype(bf16)
    d_mixed = net.columns_back(jnp.concatenate([dot_t(d_residual_low, w) for w in out_blocks], 1))
    d_state = (d_mixed * gate_act).astype(bf16)
    d_gate_pre = gate_back(d_mixed * state_f)[0].astype(bf16)
    d_drive, d_decay = scan_call(
        scan_back_kernel,
        1,
        seq_count,
        (decay_rows, d_state.astype(f32), prev_states),
        [row_shape, row_shape],
    )

    def grad_all(parts, right):
        return net.scatter_all(
            lambda c, k: t_dot(parts[c * net.chips + k], right)
            .astype(bf16)
            .reshape(seq_count, -1, right.shape[1])
        )

    grad_out = grad_all(mixed_parts, d_residual_low)
    grad_gate = grad_all(normed_parts, d_gate_pre)
    d_rate_pre, d_input_pre, d_conv_direct, grad_decay = gate_grad_fn((d_decay, d_drive))
    d_rate_low = d_rate_pre.astype(bf16)
    d_input_low = d_input_pre.astype(bf16)
    d_rate_heads = d_rate_low.reshape(rows_here, head_count, HW)
    d_input_heads = d_input_low.reshape(rows_here, head_count, HW)
    grad_rgate = jnp.einsum("nhi,nhj->hij", head_view, d_rate_heads, preferred_element_type=f32)
    grad_igate = jnp.einsum("nhi,nhj->hij", head_view, d_input_heads, preferred_element_type=f32)
    grad_rbias = jnp.sum(d_rate_low.astype(f32), axis=0)
    grad_ibias = jnp.sum(d_input_low.astype(f32), axis=0)
    d_conv = (
        d_conv_direct
        + jnp.einsum("nhj,hij->nhi", d_rate_heads, rgate_blocks, preferred_element_type=f32).reshape(
            rows_here, channels
        )
        + jnp.einsum("nhj,hij->nhi", d_input_heads, igate_blocks, preferred_element_type=f32).reshape(
            rows_here, channels
        )
    )
    d_conv_low = d_conv.astype(bf16)
    rim_grad, rim_next = passed_along((d_conv_low[:rim_rows], reset_flags[:rim_rows]), "seq", -1)
    grad_ext = jnp.concatenate([d_conv_low, rim_grad], 0).astype(f32)
    open_next = (1.0 - jnp.concatenate([reset_flags, rim_next], 0).astype(f32))[:, None]
    d_conv_f = rows_of(grad_ext, 0, len_here)
    d_branch = conv_wf[0] * d_conv_f
    ahead = None
    conv_grads = [jnp.sum(rows_of(padded, rim_rows, len_here) * d_conv_f, axis=0)]
    for offset in range(1, rim_rows + 1):
        step_open = rows_of(open_next, offset, len_here)
        ahead = step_open if offset == 1 else ahead * step_open
        d_branch = d_branch + ahead * conv_wf[offset] * rows_of(grad_ext, offset, len_here)
        conv_grads.append(
            jnp.sum(
                open_masks[offset] * rows_of(padded, rim_rows - offset, len_here) * d_conv_f,
                axis=0,
            )
        )
    grad_conv = jnp.stack(conv_grads, 0)
    grad_cbias = jnp.sum(d_conv_f, axis=0)
    d_branch_low = d_branch.astype(bf16)
    grad_in = grad_all(normed_parts, d_branch_low)
    d_normed_one = net.columns_back(
        jnp.concatenate(
            [
                dot_t(d_branch_low, left) + dot_t(d_gate_pre, right)
                for left, right in zip(in_blocks, gate_blocks)
            ],
            1,
        )
    )
    grad_norm1, d_token_norm = norm_back(d_normed_one, full_norm1, scale_one, unit_one)
    input_grad = (d_residual + d_token_norm).reshape(seqs_here, len_here, width)

    conv_flat = grad_conv.reshape(taps, devices, chan_here).transpose(1, 0, 2)
    flat_grads = jnp.concatenate(
        [
            v.reshape(devices, -1)
            for v in (grad_norm1, grad_norm2, conv_flat, grad_cbias, grad_rbias, grad_ibias, grad_decay)
        ],
        1,
    )
    flat_grads = jnp.pad(flat_grads, ((0, 0), (0, small_rows * HW - flat_grads.shape[1])))
    pack_grads = jnp.concatenate(
        [
            grad_rgate.astype(bf16).reshape(devices, chan_here, HW),
            grad_igate.astype(bf16).reshape(devices, chan_here, HW),
            flat_grads.astype(bf16).reshape(devices, small_rows, HW),
        ],
        1,
    ).reshape(dp_count, seq_count, 2 * chan_here + small_rows, HW)
    pack_mine = net.scatter_all(
        lambda c, k: lax.dynamic_index_in_dim(pack_grads, net.dp_at(c, k), 0, keepdims=False)
    )
    flat_mine = pack_mine[2 * chan_here :].reshape(-1)
    mine, at = [], 0
    for length in lengths:
        mine.append(flat_mine[at : at + length])
        at += length
    return (
        output,
        input_grad,
        final_state,
        mine[0],
        grad_gate,
        grad_in,
        mine[2].reshape(taps, chan_here),
        mine[3],
        pack_mine[:chan_here],
        mine[4],
        pack_mine[chan_here : 2 * chan_here],
        mine[5],
        mine[6],
        grad_out,
        mine[1],
        grad_ffgate,
        grad_ffup,
        grad_ffdown,
    )


def solution(mesh):
    split = ("dp", "seq")
    return jax.shard_map(
        per_device,
        mesh=mesh,
        in_specs=(
            P("dp", "seq", None),
            P("dp", "seq"),
            P("dp", "seq"),
            P("dp", "seq", None),
            P(split),
            P(split, None),
            P(split, None),
            P(None, split),
            P(split),
            P(split, None),
            P(split),
            P(split, None),
            P(split),
            P(split),
            P(split, None),
            P(split),
            P("dp", "seq"),
            P("dp", "seq"),
            P("seq", "dp"),
        ),
        out_specs=(
            P("dp", "seq", None),
            P("dp", "seq", None),
            P("dp", "seq"),
            P(split),
            P(split, None),
            P(split, None),
            P(None, split),
            P(split),
            P(split, None),
            P(split),
            P(split, None),
            P(split),
            P(split),
            P(split, None),
            P(split),
            P("dp", "seq"),
            P("dp", "seq"),
            P("seq", "dp"),
        ),
        check_vma=False,
    )
```

```python
import functools

import jax
import jax.numpy as jnp
from jax import lax
from jax.experimental import pallas as pl
from jax.experimental.pallas import tpu as pltpu
from jax.sharding import PartitionSpec as P

HW = 256
LANES = 8


epsilon = 1e-06
floor_value = 0.0001
f32 = jnp.float32
bf16 = jnp.bfloat16


def seq_order(count):
    if count % 8:
        return list(range(count))
    wide = count // 4
    path = []
    for z in range(4):
        ys = range(1, wide) if z % 2 == 0 else range(wide - 1, 0, -1)
        path += [z * wide + y for y in ys]
    return path + [z * wide for z in (3, 2, 1, 0)]


class Ring:
    def __init__(self, axis, cycles):
        self.axis = axis
        self.cycles = cycles
        self.count = len(cycles[0])

    def shift(self, value, step):
        pairs = [
            (cycle[i], cycle[(i + step) % self.count])
            for cycle in self.cycles
            for i in range(self.count)
        ]
        return lax.ppermute(value, self.axis, pairs)

    def place(self):
        table = [0] * (self.count * len(self.cycles))
        for cycle in self.cycles:
            for i, device in enumerate(cycle):
                table[device] = i
        return jnp.asarray(table, jnp.int32)[lax.axis_index(self.axis)]

    def gather_steps(self, value):
        count, half = self.count, self.count // 2
        blocks = [value] * count
        if count == 1:
            return blocks
        ahead = behind = value
        for step in range(1, half):
            behind, ahead = yield [self.shift(behind, 1), self.shift(ahead, -1)]
            blocks[count - step] = behind
            blocks[step] = ahead
        rows = value.shape[0]
        if half > 1 and rows % 32 == 0:
            top, bottom = yield [
                self.shift(behind[: rows // 2], 1),
                self.shift(ahead[rows // 2 :], -1),
            ]
            blocks[half] = jnp.concatenate([top, bottom], 0)
        else:
            (blocks[half],) = yield [self.shift(behind, 1)]
        return blocks

    def scatter_steps(self, part):
        count, half = self.count, self.count // 2
        if count == 1:
            return part(0).astype(f32)
        far = part(half).astype(bf16)
        if half == 1:
            (got,) = yield [self.shift(far, 1)]
            return part(0).astype(f32) + got.astype(f32)
        rows = far.shape[0]
        assert rows % 2 == 0
        cut = rows // 2
        ahead, behind = far[:cut], far[cut:]
        for k in range(half - 1, -1, -1):
            got_ahead, got_behind = yield [self.shift(ahead, 1), self.shift(behind, -1)]
            got_ahead, got_behind = got_ahead.astype(f32), got_behind.astype(f32)
            if k == 0:
                return part(0).astype(f32) + got_ahead + got_behind
            ahead, behind = part(k).astype(f32), part(count - k).astype(f32)
            if k == half - 1:
                ahead = jnp.concatenate([ahead[:cut] + got_ahead, ahead[cut:]], 0)
                behind = jnp.concatenate([behind[:cut], behind[cut:] + got_behind], 0)
            else:
                ahead, behind = ahead + got_ahead, behind + got_behind
            ahead, behind = ahead.astype(bf16), behind.astype(bf16)


class Flow:
    def __init__(self, steps):
        self.steps, self.pending, self.result = steps, [], None
        self.advance(None)

    def advance(self, arrived):
        try:
            self.pending = self.steps.send(arrived)
        except StopIteration as stop:
            self.pending, self.result = [], stop.value

    def finish(self):
        while self.pending:
            self.advance(self.pending)
        return self.result


def beside(values, *flows):
    values, arrived = lax.optimization_barrier((values, [flow.pending for flow in flows]))
    for flow, got in zip(flows, arrived):
        if got:
            flow.advance(got)
    return values


class Net:
    def __init__(self):
        self.seq_count = lax.axis_size("seq")
        self.dp_count = lax.axis_size("dp")
        self.order = seq_order(self.seq_count)
        self.seq = Ring("seq", [self.order])
        self.cores = 2 if self.dp_count % 2 == 0 else 1
        self.chips = self.dp_count // self.cores
        cores, chips = self.cores, self.chips
        self.chip = Ring("dp", [[o * cores + c for o in range(chips)] for c in range(cores)])
        self.core = Ring("dp", [[o * cores + c for c in range(cores)] for o in range(chips)])
        self.place = self.seq.place()
        dp = lax.axis_index("dp")
        self.my_chip, self.my_core = dp // cores, dp % cores

    def seq_at(self, k):
        return jnp.asarray(self.order, jnp.int32)[(self.place + k) % self.seq_count]

    def rel(self):
        return [(c, k) for c in range(self.cores) for k in range(self.chips)]

    def dp_at(self, c, k):
        return ((self.my_chip + k) % self.chips) * self.cores + (self.my_core + c) % self.cores

    def columns_out(self, values):
        chunk = values.shape[1] // self.dp_count
        return jnp.concatenate(
            [lax.dynamic_slice_in_dim(values, self.dp_at(c, k) * chunk, chunk, 1) for c, k in self.rel()],
            1,
        )

    def columns_back(self, values):
        chunk = values.shape[1] // self.dp_count
        pieces = []
        for dp in range(self.dp_count):
            chip, core = dp // self.cores, dp % self.cores
            at = ((core - self.my_core) % self.cores) * self.chips + (chip - self.my_chip) % self.chips
            pieces.append(lax.dynamic_slice_in_dim(values, at * chunk, chunk, 1))
        return jnp.concatenate(pieces, 1)

    def gather_dp_steps(self, value):
        blocks = yield from self.chip.gather_steps(value)
        if self.cores == 1:
            return blocks
        others = yield [self.core.shift(block, 1) for block in blocks]
        return blocks + others

    def scatter_dp_steps(self, part):
        sums = [part(0, k) for k in range(self.chips)]
        if self.cores > 1:
            got = yield [self.core.shift(part(1, k).astype(bf16), 1) for k in range(self.chips)]
            sums = [mine.astype(f32) + theirs.astype(f32) for mine, theirs in zip(sums, got)]
        return (yield from self.chip.scatter_steps(lambda k: sums[k]))


def lookup(table, index):
    value = jnp.int32(table[0])
    for i, entry in enumerate(table):
        value = jnp.where(index == i, jnp.int32(entry), value)
    return value


class Links:
    def __init__(self, order, chips, cores):
        self.count, self.chips, self.cores = len(order), chips, cores
        me, dp = lax.axis_index("seq"), lax.axis_index("dp")
        count = self.count
        place = [0] * count
        for i, device in enumerate(order):
            place[device] = i
        self.seq_at = [
            lookup([order[(place[d] + k) % count] for d in range(count)], me) for k in range(count)
        ]
        self.ring = ({"seq": self.seq_at[1]}, {"seq": self.seq_at[count - 1]})
        chip, core = dp // cores, dp % cores
        self.chip = [
            {"dp": lax.rem(chip + step, chips) * cores + core} for step in range(1, chips)
        ]
        self.core = {"dp": chip * cores + (1 - core)} if cores == 2 else None

    def greet(self):
        barrier = pltpu.get_barrier_semaphore()
        peers = list(self.ring) + self.chip + ([self.core] if self.cores == 2 else [])
        for peer in peers:
            pl.semaphore_signal(
                barrier, inc=1, device_id=peer, device_id_type=pl.DeviceIdType.MESH
            )
        pl.semaphore_wait(barrier, len(peers))


def remote(source, target, send_sem, recv_sem, peer):
    return pltpu.make_async_remote_copy(
        src_ref=source,
        dst_ref=target,
        send_sem=send_sem,
        recv_sem=recv_sem,
        device_id=peer,
        device_id_type=pl.DeviceIdType.MESH,
    )


RING_FIRST, CHIP_FIRST, RING_ONLY = 0, 1, 2


def gather_kernel(order, chips, cores, pieces, arrays, *refs):
    ins, outs = refs[:arrays], refs[arrays : 2 * arrays]
    own_sem, recv_sem, ring_sem, chip_sem, core_sem = refs[2 * arrays :]
    links = Links(order, chips, cores)
    count, half = links.count, links.count // 2
    links.greet()

    owns = [
        pltpu.make_async_copy(ins[i], outs[i].at[0, links.seq_at[0]], own_sem.at[i])
        for i in range(arrays)
    ]
    for copy in owns:
        copy.start()
    sent = []

    def whole(p, r, k):
        array, first, rows, _ = pieces[p]
        place = outs[array].at[r, links.seq_at[k]]
        return place if rows == ins[array].shape[0] else place.at[pl.ds(first, rows)]

    def rows_in(p, r, k, first, rows):
        return outs[pieces[p][0]].at[r, links.seq_at[k], pl.ds(pieces[p][1] + first, rows)]

    def held(p, r, k):
        array, first, rows, _ = pieces[p]
        if r == 0 and k == 0:
            return ins[array] if rows == ins[array].shape[0] else ins[array].at[pl.ds(first, rows)]
        return whole(p, r, k)

    def cut_of(p):
        return pieces[p][2] // 32 * 16

    def start(copy):
        copy.start()
        sent.append(copy)

    def ring_copies(p, r, s):
        cut, rows = cut_of(p), pieces[p][2]
        if s < half - 1:
            return [
                remote(
                    held(p, r, (count - s) % count), whole(p, r, (count - s) % count),
                    ring_sem.at[p, r, 0, s], recv_sem.at[p, r, count - s - 1], links.ring[0],
                ),
                remote(
                    held(p, r, s), whole(p, r, s),
                    ring_sem.at[p, r, 1, s], recv_sem.at[p, r, s + 1], links.ring[1],
                ),
            ]
        back = count - s
        if not cut:
            return [
                remote(
                    whole(p, r, back), whole(p, r, back),
                    ring_sem.at[p, r, 0, s], recv_sem.at[p, r, half], links.ring[0],
                )
            ]
        top, bottom = rows_in(p, r, back, 0, cut), rows_in(p, r, s, cut, rows - cut)
        return [
            remote(top, top, ring_sem.at[p, r, 0, s], recv_sem.at[p, r, half], links.ring[0]),
            remote(
                bottom, bottom, ring_sem.at[p, r, 1, s], recv_sem.at[p, r, count], links.ring[1]
            ),
        ]

    def arrived(p, r, k):
        cut, rows = cut_of(p), pieces[p][2]
        if k == half and cut:
            for part, sem in (((0, cut), half), ((cut, rows - cut), count)):
                ref = rows_in(p, r, k, *part)
                remote(ref, ref, ring_sem.at[p, r, 0, 0], recv_sem.at[p, r, sem], links.ring[0]).wait_recv()
        else:
            ref = whole(p, r, k)
            remote(ref, ref, ring_sem.at[p, r, 0, 0], recv_sem.at[p, r, k], links.ring[0]).wait_recv()

    def to_chips(p, k):
        for step in range(1, chips):
            start(
                remote(
                    held(p, 0, k), whole(p, chips - step, k),
                    chip_sem.at[p, step - 1, k], recv_sem.at[p, chips - step, k], links.chip[step - 1],
                )
            )

    def to_core(p, r, k):
        if cores == 2:
            start(
                remote(
                    held(p, r, k), whole(p, chips + r, k),
                    core_sem.at[p, r, k], recv_sem.at[p, chips + r, k], links.core,
                )
            )

    method = [piece[3] for piece in pieces]
    everyone = range(len(pieces))

    def planes(p):
        return range(chips) if method[p] == CHIP_FIRST else range(1)

    for p in everyone:
        if method[p] != RING_ONLY:
            to_chips(p, 0)
        for copy in ring_copies(p, 0, 0):
            start(copy)
    for p in everyone:
        if method[p] != RING_ONLY:
            to_core(p, 0, 0)
    for s in range(1, half + 1):
        steps = sorted({count - s, s})
        before = sorted({(count - s + 1) % count, s - 1})
        for p in everyone:
            for r in planes(p):
                if r == 0 or s > 1:
                    for k in steps:
                        arrived(p, r, k)
                    if s < half:
                        for copy in ring_copies(p, r, s):
                            start(copy)
                    if method[p] == RING_FIRST:
                        for k in steps:
                            to_chips(p, k)
                    if method[p] != RING_ONLY:
                        for k in steps:
                            to_core(p, r, k)
        for p in everyone:
            if method[p] == RING_FIRST:
                for r in range(1, chips):
                    for k in before:
                        arrived_from_chip(links, whole(p, r, k), chip_sem.at[p, 0, 0], recv_sem.at[p, r, k])
                        to_core(p, r, k)
            if method[p] == CHIP_FIRST and s == 1:
                for r in range(1, chips):
                    arrived_from_chip(links, whole(p, r, 0), chip_sem.at[p, 0, 0], recv_sem.at[p, r, 0])
                    for copy in ring_copies(p, r, 0):
                        start(copy)
                    to_core(p, r, 0)
                for r in range(1, chips):
                    for k in steps:
                        arrived(p, r, k)
                    if s < half:
                        for copy in ring_copies(p, r, s):
                            start(copy)
                    for k in steps:
                        to_core(p, r, k)
    for p in everyone:
        if method[p] == RING_FIRST:
            for r in range(1, chips):
                arrived_from_chip(links, whole(p, r, half), chip_sem.at[p, 0, 0], recv_sem.at[p, r, half])
                to_core(p, r, half)
    for p in everyone:
        if method[p] != RING_ONLY and cores == 2:
            for r in range(chips):
                for k in range(count):
                    arrived_from_chip(
                        links, whole(p, chips + r, k), core_sem.at[p, r, k], recv_sem.at[p, chips + r, k]
                    )
    for copy in sent:
        copy.wait_send()
    for copy in owns:
        copy.wait()


def arrived_from_chip(links, ref, send_sem, recv_sem):
    remote(ref, ref, send_sem, recv_sem, links.ring[0]).wait_recv()


def gather_call(net, arrays, pieces):
    chips, cores, count = net.chips, net.cores, net.seq_count
    slots = chips * cores
    only_ring = {piece[0] for piece in pieces if piece[3] == RING_ONLY}
    anywhere = pl.BlockSpec(memory_space=pl.ANY)
    return pl.pallas_call(
        functools.partial(gather_kernel, net.order, chips, cores, pieces, len(arrays)),
        out_shape=[
            jax.ShapeDtypeStruct((1 if i in only_ring else slots, count) + v.shape, v.dtype)
            for i, v in enumerate(arrays)
        ],
        in_specs=[anywhere] * len(arrays),
        out_specs=[anywhere] * len(arrays),
        scratch_shapes=[
            pltpu.SemaphoreType.DMA((len(arrays),)),
            pltpu.SemaphoreType.DMA((len(pieces), slots, count + 1)),
            pltpu.SemaphoreType.DMA((len(pieces), chips, 2, count // 2)),
            pltpu.SemaphoreType.DMA((len(pieces), max(chips - 1, 1), count)),
            pltpu.SemaphoreType.DMA((len(pieces), chips, count)),
        ],
        compiler_params=pltpu.CompilerParams(
            collective_id=3, has_side_effects=True, vmem_limit_bytes=32 * 2**20
        ),
        cost_estimate=pl.CostEstimate(
            flops=0, bytes_accessed=slots * count * sum(v.size for v in arrays) * 4, transcendentals=0
        ),
    )(*arrays)


def add_rows(target, terms, rows):
    if rows % 16:
        target[...] = total([term[...].astype(f32) for term in terms]).astype(target.dtype)
        return

    def body(t, carry):
        at = pl.ds(pl.multiple_of(t * 16, 16), 16)
        target[at] = total([term[at].astype(f32) for term in terms]).astype(target.dtype)
        return carry

    lax.fori_loop(0, rows // 16, body, 0)


def total(terms):
    result = terms[0]
    for term in terms[1:]:
        result = result + term
    return result


def reduce_kernel(order, chips, cores, pieces, arrays, *refs):
    slots = chips * cores
    count, half = len(order), len(order) // 2
    parts = [refs[i * slots : (i + 1) * slots] for i in range(arrays)]
    refs = refs[arrays * slots :]
    outs, refs = refs[:arrays], refs[arrays:]
    mine, refs = refs[:arrays], refs[arrays:]
    other, refs = refs[:arrays], refs[arrays:]
    chip_in, refs = refs[: len(pieces)], refs[len(pieces) :]
    ring_in, refs = refs[: len(pieces)], refs[len(pieces) :]
    load_sem, core_send, core_recv, chip_send, chip_recv, ring_send, ring_recv = refs
    links = Links(order, chips, cores)
    everyone = range(len(pieces))
    method = [piece[3] for piece in pieces]

    loads = [
        [
            pltpu.make_async_copy(parts[i][k], mine[i].at[k], load_sem.at[i, k])
            for k in range(chips)
        ]
        for i in range(arrays)
    ]
    for copies in loads:
        for copy in copies:
            copy.start()
    links.greet()
    sent = []

    def start(copy):
        copy.start()
        sent.append(copy)

    def rows_of_piece(ref, p, first=0, rows=None):
        array, start_row, piece_rows, _ = pieces[p]
        rows = piece_rows if rows is None else rows
        if rows == ref.shape[0]:
            return ref
        return ref.at[pl.ds(start_row + first, rows)]

    def held(p, k, q):
        return rows_of_piece(mine[pieces[p][0]].at[k, links.seq_at[q]], p)

    def core_copy(p, k, q):
        array = pieces[p][0]
        return remote(
            rows_of_piece(parts[array][chips + k].at[links.seq_at[q]], p),
            rows_of_piece(other[array].at[k, links.seq_at[q]], p),
            core_send.at[p, k, q], core_recv.at[p, k, q], links.core,
        )

    def steps(d):
        return sorted({d % count, (count - d) % count})

    def planes(p):
        return range(chips) if method[p] == RING_FIRST else range(1)

    if cores == 2:
        for d in range(half, -1, -1):
            for p in everyone:
                for k in reversed(range(chips)):
                    for q in steps(d):
                        start(core_copy(p, k, q))

    loaded = set()

    def core_sum(p, k, q):
        array = pieces[p][0]
        if (array, k) not in loaded:
            loaded.add((array, k))
            loads[array][k].wait()
        if cores == 2:
            core_copy(p, k, q).wait_recv()
            theirs = rows_of_piece(other[array].at[k, links.seq_at[q]], p)
            add_rows(held(p, k, q), [held(p, k, q), theirs], pieces[p][2])

    def chip_copy(p, k, q):
        if method[p] == CHIP_FIRST:
            target = chip_in[p].at[k - 1, links.seq_at[q]]
        else:
            target = chip_in[p].at[k - 1]
        return remote(
            held(p, k, q), target, chip_send.at[p, k - 1, q], chip_recv.at[p, k - 1, q], links.chip[k - 1]
        )

    def chip_sum(p, q):
        for k in range(1, chips):
            chip_copy(p, k, q).wait_recv()
            if method[p] == CHIP_FIRST:
                add_rows(held(p, 0, q), [held(p, 0, q), chip_in[p].at[k - 1, links.seq_at[q]]], pieces[p][2])
            else:
                out = rows_of_piece(outs[pieces[p][0]], p)
                add_rows(out, [out, chip_in[p].at[k - 1]], pieces[p][2])

    def span(p, side, d):
        rows = pieces[p][2]
        cut = rows // 32 * 16
        if d < half:
            return (0, rows)
        if not cut:
            return (0, rows) if side == 0 else None
        return (0, cut) if side == 0 else (cut, rows - cut)

    def ring_copy(p, k, side, d):
        first, rows = span(p, side, d)
        q = d if side == 0 else (count - d) % count
        source = held(p, k, q)
        target = ring_in[p].at[k, side, d - 1]
        if rows != pieces[p][2]:
            source, target = source.at[pl.ds(first, rows)], target.at[pl.ds(first, rows)]
        return remote(
            source, target, ring_send.at[p, k, side, d - 1], ring_recv.at[p, k, side, d - 1], links.ring[side]
        )

    def ring_step(p, k, d):
        if d == 0:
            got = []
            for side in range(2):
                if half > 1 or span(p, side, 1):
                    ring_copy(p, k, side, 1).wait_recv()
                    got.append(ring_in[p].at[k, side, 0])
            target = rows_of_piece(outs[pieces[p][0]], p) if k == 0 else held(p, k, 0)
            add_rows(target, [held(p, k, 0)] + got, pieces[p][2])
            return
        for side in range(2):
            if span(p, side, d) is None:
                continue
            if d < half and span(p, side, d + 1) is not None:
                ring_copy(p, k, side, d + 1).wait_recv()
                first, rows = span(p, side, d + 1)
                target = held(p, k, d if side == 0 else count - d)
                term = ring_in[p].at[k, side, d]
                if rows != pieces[p][2]:
                    target, term = target.at[pl.ds(first, rows)], term.at[pl.ds(first, rows)]
                add_rows(target, [target, term], rows)
            start(ring_copy(p, k, side, d))

    for d in range(half, -1, -1):
        for p in everyone:
            if method[p] == RING_FIRST:
                for k in reversed(planes(p)):
                    for q in steps(d):
                        core_sum(p, k, q)
                    ring_step(p, k, d)
                    if d == 0 and k > 0:
                        start(chip_copy(p, k, 0))
        for p in everyone:
            if method[p] == CHIP_FIRST:
                for q in steps(d):
                    for k in reversed(range(chips)):
                        core_sum(p, k, q)
                        if k > 0:
                            start(chip_copy(p, k, q))
        for p in everyone:
            if method[p] == CHIP_FIRST and d < half:
                for q in steps(d + 1):
                    chip_sum(p, q)
                ring_step(p, 0, d + 1)
    for p in everyone:
        if method[p] == CHIP_FIRST:
            chip_sum(p, 0)
            ring_step(p, 0, 0)
    for p in everyone:
        if method[p] == RING_FIRST:
            chip_sum(p, 0)
    for copy in sent:
        copy.wait_send()


def reduce_call(net, arrays, pieces):
    chips, cores, count = net.chips, net.cores, net.seq_count
    half = count // 2
    anywhere = pl.BlockSpec(memory_space=pl.ANY)
    shapes = [parts[0].shape[1:] for parts in arrays]
    ahead = max(chips - 1, 1)
    blocks = [(piece[2], shapes[piece[0]][1]) for piece in pieces]
    chip_shapes = [
        (ahead, count) + block if piece[3] == CHIP_FIRST else (ahead,) + block
        for piece, block in zip(pieces, blocks)
    ]
    ring_shapes = [
        (chips if piece[3] == RING_FIRST else 1, 2, half) + block
        for piece, block in zip(pieces, blocks)
    ]
    n = len(pieces)
    return pl.pallas_call(
        functools.partial(reduce_kernel, net.order, chips, cores, pieces, len(arrays)),
        out_shape=[jax.ShapeDtypeStruct(shape, f32) for shape in shapes],
        in_specs=[anywhere] * sum(len(parts) for parts in arrays),
        out_specs=[pl.BlockSpec(memory_space=pltpu.VMEM)] * len(arrays),
        scratch_shapes=[pltpu.VMEM((chips, count) + shape, bf16) for shape in shapes]
        + [pltpu.VMEM((chips, count) + shape, bf16) for shape in shapes]
        + [pltpu.VMEM(shape, bf16) for shape in chip_shapes]
        + [pltpu.VMEM(shape, bf16) for shape in ring_shapes]
        + [
            pltpu.SemaphoreType.DMA((len(arrays), chips)),
            pltpu.SemaphoreType.DMA((n, chips, count)),
            pltpu.SemaphoreType.DMA((n, chips, count)),
            pltpu.SemaphoreType.DMA((n, ahead, count)),
            pltpu.SemaphoreType.DMA((n, ahead, count)),
            pltpu.SemaphoreType.DMA((n, chips, 2, half)),
            pltpu.SemaphoreType.DMA((n, chips, 2, half)),
        ],
        compiler_params=pltpu.CompilerParams(
            collective_id=4, has_side_effects=True, vmem_limit_bytes=62 * 2**20
        ),
        cost_estimate=pl.CostEstimate(
            flops=0, bytes_accessed=sum(p.size for parts in arrays for p in parts) * 4, transcendentals=0
        ),
    )(*[part for parts in arrays for part in parts])


def exchange(totals, everyone, send_sem, recv_sem, count):
    me = lax.axis_index("seq")
    everyone[me] = totals[...]
    copies = []
    for step in range(1, count):
        peer = lax.rem(me + step, count)
        copy = pltpu.make_async_remote_copy(
            src_ref=totals,
            dst_ref=everyone.at[me],
            send_sem=send_sem.at[step],
            recv_sem=recv_sem.at[step],
            device_id={"seq": peer},
            device_id_type=pl.DeviceIdType.MESH,
        )
        copy.start()
    for step in range(1, count):
        source = lax.rem(me + count - step, count)
        copy = pltpu.make_async_remote_copy(
            src_ref=totals,
            dst_ref=everyone.at[source],
            send_sem=send_sem.at[step],
            recv_sem=recv_sem.at[step],
            device_id={"seq": source},
            device_id_type=pl.DeviceIdType.MESH,
        )
        copy.wait()


def greet(count):
    me = lax.axis_index("seq")
    barrier = pltpu.get_barrier_semaphore()
    for step in range(1, count):
        pl.semaphore_signal(
            barrier,
            inc=1,
            device_id={"seq": lax.rem(me + step, count)},
            device_id_type=pl.DeviceIdType.MESH,
        )
    pl.semaphore_wait(barrier, count - 1)


def tiles(channels):
    wide = 512 if channels % 512 == 0 else 128
    return [pl.ds(at, wide) for at in range(0, channels, wide)]


def tile_prefix(product, total, step):
    row = lax.broadcasted_iota(jnp.int32, product.shape, 0)
    reach = 1
    while reach < LANES:
        turn = reach if step > 0 else LANES - reach
        inside = row >= reach if step > 0 else row < LANES - reach
        total = total + product * jnp.where(inside, pltpu.roll(total, turn, 0), 0.0)
        product = product * jnp.where(inside, pltpu.roll(product, turn, 0), 1.0)
        reach *= 2
    return (product, total)


def scan_kernel(
    count, decay_ref, drive_ref, start_ref, state_ref, prev_ref, last_ref,
    totals, everyone, send_sem, recv_sem,
):
    greet(count)
    rows, channels = decay_ref.shape
    end = LANES - 1
    for cols in tiles(channels):

        def first_pass(t, carry):
            run_product, run_sum = carry
            at = pl.ds(pl.multiple_of(t * LANES, LANES), LANES)
            product, total = tile_prefix(decay_ref[at, cols], drive_ref[at, cols], 1)
            prev_ref[at, cols] = product
            state_ref[at, cols] = total
            last = product[end:]
            return (last * run_product, last * run_sum + total[end:])

        zero = jnp.zeros((1, cols.size), f32)
        run_product, run_sum = lax.fori_loop(
            0, rows // LANES, first_pass, (zero + 1.0, zero), unroll=4
        )
        totals[0:1, cols] = run_product
        totals[1:2, cols] = run_sum
    exchange(totals, everyone, send_sem, recv_sem, count)
    me = lax.axis_index("seq")
    for cols in tiles(channels):
        state = start_ref[0:1, cols]
        entering = state
        for device in range(count):
            entering = jnp.where(me == device, state, entering)
            state = everyone[device, 0:1, cols] * state + everyone[device, 1:2, cols]
        last_ref[0:1, cols] = state

        def second_pass(t, entry):
            at = pl.ds(pl.multiple_of(t * LANES, LANES), LANES)
            state = prev_ref[at, cols] * entry + state_ref[at, cols]
            row = lax.broadcasted_iota(jnp.int32, state.shape, 0)
            state_ref[at, cols] = state
            prev_ref[at, cols] = jnp.where(row == 0, entry, pltpu.roll(state, 1, 0))
            return state[end:]

        lax.fori_loop(0, rows // LANES, second_pass, entering, unroll=4)


def scan_back_kernel(
    count, decay_ref, d_state_ref, prev_ref, d_drive_ref, d_decay_ref,
    totals, everyone, send_sem, recv_sem,
):
    greet(count)
    rows, channels = decay_ref.shape
    last_tile = rows // LANES - 1
    end = LANES - 1
    for cols in tiles(channels):

        def first_pass(i, carry):
            run_product, run_sum = carry
            at = pl.ds(pl.multiple_of((last_tile - i) * LANES, LANES), LANES)
            decay = decay_ref[at, cols]
            product, total = tile_prefix(decay, decay * d_state_ref[at, cols], -1)
            d_decay_ref[at, cols] = product
            d_drive_ref[at, cols] = total
            first = product[:1]
            return (first * run_product, first * run_sum + total[:1])

        zero = jnp.zeros((1, cols.size), f32)
        run_product, run_sum = lax.fori_loop(
            0, rows // LANES, first_pass, (zero + 1.0, zero), unroll=4
        )
        totals[0:1, cols] = run_product
        totals[1:2, cols] = run_sum
    exchange(totals, everyone, send_sem, recv_sem, count)
    me = lax.axis_index("seq")
    for cols in tiles(channels):
        state = jnp.zeros((1, cols.size), f32)
        entering = state
        for device in reversed(range(count)):
            entering = jnp.where(me == device, state, entering)
            state = everyone[device, 0:1, cols] * state + everyone[device, 1:2, cols]

        def second_pass(i, entry):
            at = pl.ds(pl.multiple_of((last_tile - i) * LANES, LANES), LANES)
            outgoing = d_decay_ref[at, cols] * entry + d_drive_ref[at, cols]
            row = lax.broadcasted_iota(jnp.int32, outgoing.shape, 0)
            incoming = jnp.where(row == end, entry, pltpu.roll(outgoing, end, 0))
            carry = d_state_ref[at, cols] + incoming
            d_drive_ref[at, cols] = carry
            d_decay_ref[at, cols] = carry * prev_ref[at, cols]
            return outgoing[:1]

        lax.fori_loop(0, rows // LANES, second_pass, entering, unroll=4)


def scan_call(kernel, collective_id, count, operands, out_shapes):
    channels = operands[0].shape[1]
    vmem = pl.BlockSpec(memory_space=pltpu.VMEM)
    return pl.pallas_call(
        functools.partial(kernel, count),
        out_shape=out_shapes,
        in_specs=[vmem] * len(operands),
        out_specs=[vmem] * len(out_shapes),
        scratch_shapes=[
            pltpu.VMEM((2, channels), f32),
            pltpu.VMEM((count, 2, channels), f32),
            pltpu.SemaphoreType.DMA((count,)),
            pltpu.SemaphoreType.DMA((count,)),
        ],
        compiler_params=pltpu.CompilerParams(
            collective_id=collective_id, has_side_effects=True, vmem_limit_bytes=40 * 2**20
        ),
        cost_estimate=pl.CostEstimate(
            flops=8 * operands[0].size, bytes_accessed=20 * operands[0].size, transcendentals=0
        ),
    )(*operands)


def pair_slots(count):
    half = count // 2
    return [k for s in range(1, half) for k in (count - s, s)] + [half, 0]


def gelu_parts(v):
    root, cubic = 0.7978845608028654, 0.044715
    curve = jnp.tanh(root * (v + cubic * v * v * v))
    act = 0.5 * v * (1.0 + curve)
    slope = 0.5 * (1.0 + curve) + 0.5 * v * (1.0 - curve * curve) * root * (
        1.0 + 3.0 * cubic * v * v
    )
    return (act, slope)


def contract(left, right, left_dim, right_dim):
    return lax.dot_general(
        left, right, (((left_dim,), (right_dim,)), ((), ())), preferred_element_type=f32
    )


def ff_kernel(
    order, own_ref, cot_ref, gate_hbm, up_hbm, down_hbm,
    blocks_ref, hidden_ref, d_gate_ref, d_up_ref, out_ref, d_in_ref,
    gate_ref, up_ref, down_ref, rows_ref, cots_ref, h_ref, g_ref, u_ref, o_ref, d_ref,
    send_sem, recv_sem, load_sem, store_sem,
):
    count = len(order)
    half = count // 2
    rows, width = own_ref.shape
    hidden_here = gate_ref.shape[1]
    cut = rows // 2
    me = lax.axis_index("seq")
    ahead_of, behind_of = [0] * count, [0] * count
    for i, device in enumerate(order):
        ahead_of[device] = order[(i + 1) % count]
        behind_of[device] = order[(i - 1) % count]
    sides = (lookup(ahead_of, me), lookup(behind_of, me))

    barrier = pltpu.get_barrier_semaphore()
    for side in sides:
        pl.semaphore_signal(
            barrier, inc=1, device_id={"seq": side}, device_id_type=pl.DeviceIdType.MESH
        )
    weights = [
        pltpu.make_async_copy(hbm, vmem, load_sem.at[i])
        for i, (hbm, vmem) in enumerate(
            ((gate_hbm, gate_ref), (up_hbm, up_ref), (down_hbm, down_ref))
        )
    ]
    for copy in weights:
        copy.start()
    keep = pltpu.make_async_copy(own_ref, blocks_ref.at[count - 1], load_sem.at[3])
    keep.start()
    pl.semaphore_wait(barrier, 2)

    def full(side, source, slot, s):
        return pltpu.make_async_remote_copy(
            src_ref=source,
            dst_ref=blocks_ref.at[slot],
            send_sem=send_sem.at[side, s],
            recv_sem=recv_sem.at[slot],
            device_id={"seq": sides[side]},
            device_id_type=pl.DeviceIdType.MESH,
        )

    def part(side):
        at = pl.ds(0, cut) if side == 0 else pl.ds(cut, rows - cut)
        return pltpu.make_async_remote_copy(
            src_ref=blocks_ref.at[2 * (half - 2) + side, at],
            dst_ref=blocks_ref.at[count - 2, at],
            send_sem=send_sem.at[side, half - 1],
            recv_sem=recv_sem.at[count - 2 + side],
            device_id={"seq": sides[side]},
            device_id_type=pl.DeviceIdType.MESH,
        )

    for side in range(2):
        full(side, own_ref, side, 0).start()
    keep.wait()
    for copy in weights:
        copy.wait()

    def loads(s):
        return [
            pltpu.make_async_copy(blocks_ref.at[pl.ds(2 * (s - 1), 2)], rows_ref, load_sem.at[4]),
            pltpu.make_async_copy(cot_ref.at[pl.ds(2 * (s - 1), 2)], cots_ref, load_sem.at[5]),
        ]

    def stores(s):
        return [
            pltpu.make_async_copy(vmem, hbm.at[s - 1], store_sem.at[i])
            for i, (vmem, hbm) in enumerate(
                (
                    (h_ref, hidden_ref),
                    (g_ref, d_gate_ref),
                    (u_ref, d_up_ref),
                    (o_ref, out_ref),
                    (d_ref, d_in_ref),
                )
            )
        ]

    def step(s, carry):
        @pl.when(s < half)
        def _():
            for side in range(2):
                full(side, own_ref, 2 * (s - 1) + side, s).wait_recv()

            @pl.when(s < half - 1)
            def _():
                for side in range(2):
                    slot = 2 * (s - 1) + side
                    full(side, blocks_ref.at[slot], slot + 2, s).start()

            @pl.when(s == half - 1)
            def _():
                for side in range(2):
                    part(side).start()

        @pl.when(s == half)
        def _():
            for side in range(2):
                part(side).wait_recv()

        for copy in loads(s):
            copy.start()

        @pl.when(s > 1)
        def _():
            for copy in stores(s - 1):
                copy.wait()

        for copy in loads(s):
            copy.wait()
        wide = 256 if hidden_here % 256 == 0 else 128

        def inner(j, carry):
            at = pl.ds(pl.multiple_of(j * wide, wide), wide)
            x = rows_ref[...].reshape(2 * rows, width)
            c = cots_ref[...].reshape(2 * rows, width)
            ff_gate = contract(x, gate_ref[:, at], 1, 0)
            ff_up = contract(x, up_ref[:, at], 1, 0)
            d_hidden = contract(c, down_ref[at, :], 1, 1)
            act, slope = gelu_parts(ff_gate)
            h_ref[:, at] = (act * ff_up).astype(bf16)
            g_ref[:, at] = (d_hidden * ff_up * slope).astype(bf16)
            u_ref[:, at] = (d_hidden * act).astype(bf16)
            return carry

        lax.fori_loop(0, hidden_here // wide, inner, 0)
        out_wide = 512

        def outer(j, carry):
            at = pl.ds(pl.multiple_of(j * out_wide, out_wide), out_wide)
            o_ref[:, at] = contract(h_ref[...], down_ref[:, at], 1, 0).astype(bf16)
            d_ref[:, at] = (
                contract(g_ref[...], gate_ref[at, :], 1, 1)
                + contract(u_ref[...], up_ref[at, :], 1, 1)
            ).astype(bf16)
            return carry

        lax.fori_loop(0, width // out_wide, outer, 0)
        for copy in stores(s):
            copy.start()
        return carry

    lax.fori_loop(1, half + 1, step, 0)
    for copy in stores(half):
        copy.wait()
    for side in range(2):
        for s in range(half - 1):
            full(side, own_ref, side, s).wait_send()
        part(side).wait_send()


def ff_call(order, own, cot, slab_gate, slab_up, slab_down):
    rows, width = own.shape
    count, half = len(order), len(order) // 2
    hidden_here = slab_gate.shape[1]
    anywhere = pl.BlockSpec(memory_space=pl.ANY)
    pair = 2 * rows
    shape = jax.ShapeDtypeStruct
    flops = 12 * count * rows * width * hidden_here
    return pl.pallas_call(
        functools.partial(ff_kernel, order),
        out_shape=[shape((count, rows, width), bf16)]
        + [shape((half, pair, hidden_here), bf16)] * 3
        + [shape((half, pair, width), bf16)] * 2,
        in_specs=[anywhere] * 5,
        out_specs=[anywhere] * 6,
        scratch_shapes=[
            pltpu.VMEM((width, hidden_here), bf16),
            pltpu.VMEM((width, hidden_here), bf16),
            pltpu.VMEM((hidden_here, width), bf16),
            pltpu.VMEM((2, rows, width), bf16),
            pltpu.VMEM((2, rows, width), bf16),
            pltpu.VMEM((pair, hidden_here), bf16),
            pltpu.VMEM((pair, hidden_here), bf16),
            pltpu.VMEM((pair, hidden_here), bf16),
            pltpu.VMEM((pair, width), bf16),
            pltpu.VMEM((pair, width), bf16),
            pltpu.SemaphoreType.DMA((2, half)),
            pltpu.SemaphoreType.DMA((count,)),
            pltpu.SemaphoreType.DMA((6,)),
            pltpu.SemaphoreType.DMA((5,)),
        ],
        compiler_params=pltpu.CompilerParams(
            collective_id=2, has_side_effects=True, vmem_limit_bytes=48 * 2**20
        ),
        cost_estimate=pl.CostEstimate(
            flops=flops, bytes_accessed=60 * 2**20, transcendentals=count * rows * hidden_here
        ),
    )(own, cot, slab_gate, slab_up, slab_down)


def passed_along(value, axis, steps):
    count = lax.axis_size(axis)
    first, last = (max(0, -steps), min(count, count - steps))
    return lax.ppermute(value, axis, [(source, source + steps) for source in range(first, last)])


def gelu_tanh(values):
    return jax.nn.gelu(values, approximate=True)


def rms_parts(values, norm_gain):
    root_scale = lax.rsqrt(jnp.mean(values * values, axis=-1, keepdims=True) + epsilon)
    unit_rows = values * root_scale
    return (unit_rows * norm_gain, root_scale, unit_rows)


def norm_back(d_normed, norm_gain, root_scale, unit_rows):
    weighted = d_normed * norm_gain
    grad_gain = jnp.sum(d_normed * unit_rows, axis=0)
    d_values = root_scale * (
        weighted - unit_rows * jnp.mean(weighted * unit_rows, axis=-1, keepdims=True)
    )
    return (grad_gain, d_values)


def rows_of(values, first_row, row_count):
    return lax.slice_in_dim(values, first_row, first_row + row_count, axis=values.ndim - 2)


def gate_math(rate_pre, input_pre, conv_vals, decay_param, reset_col):
    rate = jax.nn.sigmoid(rate_pre)
    in_gate = jax.nn.sigmoid(input_pre)
    log_decay = -8.0 * jax.nn.softplus(-decay_param) * rate
    keep_mask = 1.0 - reset_col
    decay_rows = jnp.exp(log_decay) * keep_mask
    root_term = jnp.sqrt(jnp.maximum(-jnp.expm1(2.0 * log_decay), floor_value))
    drive_rows = (reset_col + keep_mask * root_term) * in_gate * conv_vals
    return (decay_rows, drive_rows)


def dot(left, right):
    return jnp.dot(left, right, preferred_element_type=f32)


def dot_t(left, right):
    return lax.dot_general(left, right, (((1,), (1,)), ((), ())), preferred_element_type=f32)


def t_dot(left, right):
    return lax.dot_general(left, right, (((0,), (0,)), ((), ())), preferred_element_type=f32)


def per_device(
    inputs,
    reset,
    initial_state,
    cotangent,
    norm1_gain,
    w_gate,
    w_in,
    conv_w,
    conv_bias,
    w_rgate,
    rgate_bias,
    w_igate,
    igate_bias,
    decay_param,
    w_out,
    norm2_gain,
    w_ffgate,
    w_ffup,
    w_ffdown,
):
    net = Net()
    seqs_here, len_here, width = inputs.shape
    assert seqs_here == 1
    rows_here = len_here
    dp_count, seq_count = net.dp_count, net.seq_count
    devices = dp_count * seq_count
    chan_here, channels = w_rgate.shape[0], w_rgate.shape[0] * devices
    wide_here = norm1_gain.shape[0]
    head_count = channels // HW
    taps = conv_w.shape[0]
    rim_rows = taps - 1
    rel = net.rel()

    vectors = [norm1_gain, norm2_gain, conv_w.reshape(-1), conv_bias, rgate_bias, igate_bias, decay_param]
    lengths = [v.shape[0] for v in vectors]
    flat = jnp.concatenate(vectors)
    small_rows = -(-flat.shape[0] // HW)
    small_rows += -(2 * chan_here + small_rows) % 16
    flat = jnp.pad(flat, (0, small_rows * HW - flat.shape[0]))
    packed = jnp.concatenate([w_rgate, w_igate, flat.reshape(small_rows, HW)], 0)
    half_rows = chan_here * 3 // 5 // 16 * 16
    out_pieces = [(3, 0, half_rows, RING_FIRST), (3, half_rows, chan_here - half_rows, CHIP_FIRST)]
    if half_rows == 0 or chan_here % 16:
        out_pieces = [(3, 0, chan_here, RING_FIRST)]
    pack_got, in_got, gate_got, out_got, start_got = gather_call(
        net,
        (packed, w_in, w_gate, w_out, initial_state),
        [
            (0, 0, packed.shape[0], RING_FIRST),
            (1, 0, wide_here, RING_FIRST),
            (2, 0, wide_here, CHIP_FIRST),
        ]
        + out_pieces
        + [(4, 0, 1, RING_ONLY)],
    )
    pack_blocks = [pack_got[i] for i in range(dp_count)]
    pack_all = jnp.zeros((dp_count,) + pack_blocks[0].shape, bf16)
    for (c, k), block in zip(rel, pack_blocks):
        pack_all = lax.dynamic_update_index_in_dim(pack_all, block, net.dp_at(c, k), 0)
    pack_all = pack_all.reshape((devices,) + packed.shape)
    full_rgate = pack_all[:, :chan_here].reshape(channels, HW)
    full_igate = pack_all[:, chan_here : 2 * chan_here].reshape(channels, HW)
    flat_all = pack_all[:, 2 * chan_here :].reshape(devices, small_rows * HW)
    pieces, at = [], 0
    for length in lengths:
        pieces.append(flat_all[:, at : at + length])
        at += length
    full_norm1 = pieces[0].reshape(-1).astype(f32)
    full_norm2 = pieces[1].reshape(-1).astype(f32)
    conv_wf = pieces[2].reshape(devices, taps, chan_here).transpose(1, 0, 2).reshape(taps, channels).astype(f32)
    full_cbias, full_rbias, full_ibias, decay_f = (p.reshape(-1).astype(f32) for p in pieces[3:])
    start_state = start_got.reshape(1, channels)

    in_blocks, gate_blocks = (
        [got[i].reshape(seq_count * wide_here, channels) for i in range(dp_count)]
        for got in (in_got, gate_got)
    )
    out_blocks = [out_got[i].reshape(seq_count * chan_here, width) for i in range(dp_count)]
    w_ffgate, w_ffup, w_ffdown, cotangent, in_blocks[0] = lax.optimization_barrier(
        (w_ffgate, w_ffup, w_ffdown, cotangent, in_blocks[0])
    )
    cotan_rows = cotangent.reshape(rows_here, width)
    cot_flow = Flow(net.seq.gather_steps(net.columns_out(cotan_rows)))
    slab_flows = [Flow(net.gather_dp_steps(w)) for w in (w_ffgate, w_ffup, w_ffdown)]

    token_rows = inputs.reshape(rows_here, width).astype(f32)
    normed_f, scale_one, unit_one = rms_parts(token_rows, full_norm1)
    normed = net.columns_out(normed_f.astype(bf16))
    step_cols = width // dp_count
    normed_parts = [normed[:, i * step_cols : (i + 1) * step_cols] for i in range(dp_count)]
    branch = total([dot(n, w) for n, w in zip(normed_parts, in_blocks)]).astype(bf16)
    branch = beside(branch, cot_flow)
    gate_pre = total([dot(n, w) for n, w in zip(normed_parts, gate_blocks)])
    reset_flags = reset.reshape(rows_here).astype(bf16)
    rim_branch, rim_flags = passed_along(
        (branch[len_here - rim_rows :], reset_flags[len_here - rim_rows :]), "seq", 1
    )
    padded = jnp.concatenate([rim_branch, branch], 0).astype(f32)
    open_pad = (1.0 - jnp.concatenate([rim_flags, reset_flags], 0).astype(f32))[:, None]
    open_masks = [None]
    conv_total = full_cbias + conv_wf[0] * rows_of(padded, rim_rows, len_here)
    running = rows_of(open_pad, rim_rows, len_here)
    for offset in range(1, rim_rows + 1):
        if offset > 1:
            running = running * rows_of(open_pad, rim_rows + 1 - offset, len_here)
        open_masks.append(running)
        conv_total = conv_total + running * conv_wf[offset] * rows_of(
            padded, rim_rows - offset, len_here
        )
    conv_low = conv_total.astype(bf16)
    conv_f = conv_low.astype(f32)
    head_view = conv_low.reshape(rows_here, head_count, HW)
    rgate_blocks = full_rgate.reshape(head_count, HW, HW)
    igate_blocks = full_igate.reshape(head_count, HW, HW)
    rate_pre = (
        jnp.einsum("nhi,hij->nhj", head_view, rgate_blocks, preferred_element_type=f32).reshape(
            rows_here, channels
        )
        + full_rbias
    )
    input_pre = (
        jnp.einsum("nhi,hij->nhj", head_view, igate_blocks, preferred_element_type=f32).reshape(
            rows_here, channels
        )
        + full_ibias
    )
    reset_col = reset.astype(f32).reshape(rows_here, 1)
    rate_pre, input_pre, gate_pre = beside((rate_pre, input_pre, gate_pre), cot_flow, *slab_flows)

    def gate_local(rate_in, input_in, conv_in, decay_in):
        return gate_math(rate_in, input_in, conv_in, decay_in, reset_col)

    (decay_rows, drive_rows), gate_grad_fn = jax.vjp(
        gate_local, rate_pre, input_pre, conv_f, decay_f
    )
    row_shape = jax.ShapeDtypeStruct((rows_here, channels), f32)
    states, prev_states, last_state = scan_call(
        scan_kernel,
        0,
        seq_count,
        (decay_rows, drive_rows, start_state),
        [row_shape, row_shape, jax.ShapeDtypeStruct((1, channels), f32)],
    )
    states = beside(states, cot_flow, *slab_flows)
    final_here = initial_state.shape[1]
    final_state = lax.dynamic_slice_in_dim(
        last_state, lax.axis_index("seq") * final_here, final_here, 1
    )
    state_f = states.astype(bf16).astype(f32)
    gate_act, gate_back = jax.vjp(gelu_tanh, gate_pre)
    mixed_rows = net.columns_out((state_f * gate_act).astype(bf16))
    step_chan = channels // dp_count
    mixed_parts = [mixed_rows[:, i * step_chan : (i + 1) * step_chan] for i in range(dp_count)]
    residual = token_rows + total([dot(m, w) for m, w in zip(mixed_parts, out_blocks)])

    slots = pair_slots(seq_count)
    cot_blocks = cot_flow.finish()
    group_cotan = jnp.stack([cot_blocks[k] for k in slots], 0)
    slab_gate, slab_up = (jnp.concatenate(flow.finish(), 0) for flow in slab_flows[:2])
    slab_down = jnp.concatenate(slab_flows[2].finish(), 1)
    normed_two_f, scale_two, unit_two = rms_parts(residual, full_norm2)
    normed_two = net.columns_out(normed_two_f.astype(bf16))
    group_normed, hidden, d_ffgate, d_ffup, out_part, d_normed_part = ff_call(
        net.order, normed_two, group_cotan, slab_gate, slab_up, slab_down
    )
    group_rows = seq_count * rows_here
    group_normed = group_normed.reshape(group_rows, width)
    group_cotan = group_cotan.reshape(group_rows, width)
    hidden, d_ffgate, d_ffup = (v.reshape(group_rows, -1) for v in (hidden, d_ffgate, d_ffup))

    def block_rows(whole):
        whole = whole.reshape(seq_count, rows_here, width)
        return lambda k: whole[slots.index(k)]

    def dp_chunk(whole, axis):
        size = whole.shape[axis] // dp_count
        return lambda c, k: lax.slice_in_dim(
            whole, (c * net.chips + k) * size, (c * net.chips + k + 1) * size, axis=axis
        )

    d_normed_flow = Flow(net.seq.scatter_steps(block_rows(d_normed_part)))
    gate_part = beside(t_dot(group_normed, d_ffgate).astype(bf16), d_normed_flow)
    up_part = beside(t_dot(group_normed, d_ffup).astype(bf16), d_normed_flow)
    down_part = beside(t_dot(hidden, group_cotan).astype(bf16), d_normed_flow)
    d_normed_sum = d_normed_flow.finish()
    d_normed_sum, out_part, gate_part, up_part, down_part = lax.optimization_barrier(
        (d_normed_sum, out_part, gate_part, up_part, down_part)
    )
    d_normed_two = net.columns_back(d_normed_sum)
    out_flow = Flow(net.seq.scatter_steps(block_rows(out_part)))
    ff_flows = [
        Flow(net.scatter_dp_steps(dp_chunk(part, axis)))
        for part, axis in ((gate_part, 0), (up_part, 0), (down_part, 1))
    ]

    grad_norm2, d_resid_norm = norm_back(d_normed_two, full_norm2, scale_two, unit_two)
    d_residual = cotan_rows.astype(f32) + d_resid_norm
    d_residual_low = d_residual.astype(bf16)
    d_mixed = net.columns_back(jnp.concatenate([dot_t(d_residual_low, w) for w in out_blocks], 1))
    d_mixed = beside(d_mixed, out_flow, *ff_flows)
    d_state = (d_mixed * gate_act).astype(bf16)
    d_gate_pre = gate_back(d_mixed * state_f)[0].astype(bf16)
    d_drive, d_decay = scan_call(
        scan_back_kernel,
        1,
        seq_count,
        (decay_rows, d_state.astype(f32), prev_states),
        [row_shape, row_shape],
    )

    def grad_terms(parts, right):
        return [t_dot(part, right).astype(bf16).reshape(seq_count, -1, right.shape[1]) for part in parts]

    out_terms = grad_terms(mixed_parts, d_residual_low)
    gate_terms = grad_terms(normed_parts, d_gate_pre)
    d_rate_pre, d_input_pre, d_conv_direct, grad_decay = gate_grad_fn((d_decay, d_drive))
    d_rate_low, d_input_low = beside(
        (d_rate_pre.astype(bf16), d_input_pre.astype(bf16)), out_flow, *ff_flows
    )
    d_rate_heads = d_rate_low.reshape(rows_here, head_count, HW)
    d_input_heads = d_input_low.reshape(rows_here, head_count, HW)
    grad_rgate = jnp.einsum("nhi,nhj->hij", head_view, d_rate_heads, preferred_element_type=f32)
    grad_igate = jnp.einsum("nhi,nhj->hij", head_view, d_input_heads, preferred_element_type=f32)
    grad_rbias = jnp.sum(d_rate_low.astype(f32), axis=0)
    grad_ibias = jnp.sum(d_input_low.astype(f32), axis=0)
    d_conv = (
        d_conv_direct
        + jnp.einsum("nhj,hij->nhi", d_rate_heads, rgate_blocks, preferred_element_type=f32).reshape(
            rows_here, channels
        )
        + jnp.einsum("nhj,hij->nhi", d_input_heads, igate_blocks, preferred_element_type=f32).reshape(
            rows_here, channels
        )
    )
    d_conv_low = d_conv.astype(bf16)
    rim_grad, rim_next = passed_along((d_conv_low[:rim_rows], reset_flags[:rim_rows]), "seq", -1)
    grad_ext = jnp.concatenate([d_conv_low, rim_grad], 0).astype(f32)
    open_next = (1.0 - jnp.concatenate([reset_flags, rim_next], 0).astype(f32))[:, None]
    d_conv_f = rows_of(grad_ext, 0, len_here)
    d_branch = conv_wf[0] * d_conv_f
    ahead = None
    conv_grads = [jnp.sum(rows_of(padded, rim_rows, len_here) * d_conv_f, axis=0)]
    for offset in range(1, rim_rows + 1):
        step_open = rows_of(open_next, offset, len_here)
        ahead = step_open if offset == 1 else ahead * step_open
        d_branch = d_branch + ahead * conv_wf[offset] * rows_of(grad_ext, offset, len_here)
        conv_grads.append(
            jnp.sum(
                open_masks[offset] * rows_of(padded, rim_rows - offset, len_here) * d_conv_f,
                axis=0,
            )
        )
    grad_conv = jnp.stack(conv_grads, 0)
    grad_cbias = jnp.sum(d_conv_f, axis=0)
    d_branch_low = beside(d_branch.astype(bf16), out_flow)
    in_terms = grad_terms(normed_parts, d_branch_low)
    d_normed_one = net.columns_back(
        jnp.concatenate(
            [
                dot_t(d_branch_low, left) + dot_t(d_gate_pre, right)
                for left, right in zip(in_blocks, gate_blocks)
            ],
            1,
        )
    )
    grad_norm1, d_token_norm = norm_back(d_normed_one, full_norm1, scale_one, unit_one)
    input_grad = (d_residual + d_token_norm).reshape(seqs_here, len_here, width)

    grad_norm1, input_grad = beside((grad_norm1, input_grad), out_flow)
    ff_out = net.columns_back(out_flow.finish())
    output = (residual + ff_out).astype(bf16).reshape(seqs_here, len_here, width)
    grad_ffgate, grad_ffup, grad_ffdown = (flow.finish() for flow in ff_flows)

    conv_flat = grad_conv.reshape(taps, devices, chan_here).transpose(1, 0, 2)
    flat_grads = jnp.concatenate(
        [
            v.reshape(devices, -1)
            for v in (grad_norm1, grad_norm2, conv_flat, grad_cbias, grad_rbias, grad_ibias, grad_decay)
        ],
        1,
    )
    flat_grads = jnp.pad(flat_grads, ((0, 0), (0, small_rows * HW - flat_grads.shape[1])))
    pack_grads = jnp.concatenate(
        [
            grad_rgate.astype(bf16).reshape(devices, chan_here, HW),
            grad_igate.astype(bf16).reshape(devices, chan_here, HW),
            flat_grads.astype(bf16).reshape(devices, small_rows, HW),
        ],
        1,
    ).reshape(dp_count, seq_count, 2 * chan_here + small_rows, HW)
    pack_terms = [
        lax.dynamic_index_in_dim(pack_grads, net.dp_at(c, k), 0, keepdims=False) for c, k in rel
    ]
    out_pieces = [(2, first, rows, RING_FIRST + CHIP_FIRST - way) for _, first, rows, way in out_pieces]
    grad_in, grad_gate, grad_out, pack_mine = reduce_call(
        net,
        [in_terms, gate_terms, out_terms, pack_terms],
        [(1, 0, wide_here, RING_FIRST)]
        + out_pieces
        + [(3, 0, packed.shape[0], CHIP_FIRST), (0, 0, wide_here, CHIP_FIRST)],
    )
    flat_mine = pack_mine[2 * chan_here :].reshape(-1)
    mine, at = [], 0
    for length in lengths:
        mine.append(flat_mine[at : at + length])
        at += length
    return (
        output,
        input_grad,
        final_state,
        mine[0],
        grad_gate,
        grad_in,
        mine[2].reshape(taps, chan_here),
        mine[3],
        pack_mine[:chan_here],
        mine[4],
        pack_mine[chan_here : 2 * chan_here],
        mine[5],
        mine[6],
        grad_out,
        mine[1],
        grad_ffgate,
        grad_ffup,
        grad_ffdown,
    )


def solution(mesh):
    split = ("dp", "seq")
    return jax.shard_map(
        per_device,
        mesh=mesh,
        in_specs=(
            P("dp", "seq", None),
            P("dp", "seq"),
            P("dp", "seq"),
            P("dp", "seq", None),
            P(split),
            P(split, None),
            P(split, None),
            P(None, split),
            P(split),
            P(split, None),
            P(split),
            P(split, None),
            P(split),
            P(split),
            P(split, None),
            P(split),
            P("dp", "seq"),
            P("dp", "seq"),
            P("seq", "dp"),
        ),
        out_specs=(
            P("dp", "seq", None),
            P("dp", "seq", None),
            P("dp", "seq"),
            P(split),
            P(split, None),
            P(split, None),
            P(None, split),
            P(split),
            P(split, None),
            P(split),
            P(split, None),
            P(split),
            P(split),
            P(split, None),
            P(split),
            P("dp", "seq"),
            P("dp", "seq"),
            P("seq", "dp"),
        ),
        check_vma=False,
    )
```

```python
import functools

import jax
import jax.numpy as jnp
from jax import lax
from jax.experimental import pallas as pl
from jax.experimental.pallas import tpu as pltpu
from jax.sharding import PartitionSpec as P

HW = 256
LANES = 8


epsilon = 1e-06
floor_value = 0.0001
f32 = jnp.float32
bf16 = jnp.bfloat16


def seq_order(count):
    if count % 8:
        return list(range(count))
    wide = count // 4
    path = []
    for z in range(4):
        ys = range(1, wide) if z % 2 == 0 else range(wide - 1, 0, -1)
        path += [z * wide + y for y in ys]
    return path + [z * wide for z in (3, 2, 1, 0)]


class Ring:
    def __init__(self, axis, cycles):
        self.axis = axis
        self.cycles = cycles
        self.count = len(cycles[0])

    def shift(self, value, step):
        pairs = [
            (cycle[i], cycle[(i + step) % self.count])
            for cycle in self.cycles
            for i in range(self.count)
        ]
        return lax.ppermute(value, self.axis, pairs)

    def place(self):
        table = [0] * (self.count * len(self.cycles))
        for cycle in self.cycles:
            for i, device in enumerate(cycle):
                table[device] = i
        return jnp.asarray(table, jnp.int32)[lax.axis_index(self.axis)]

    def gather_steps(self, value):
        count, half = self.count, self.count // 2
        blocks = [value] * count
        if count == 1:
            return blocks
        ahead = behind = value
        for step in range(1, half):
            behind, ahead = yield [self.shift(behind, 1), self.shift(ahead, -1)]
            blocks[count - step] = behind
            blocks[step] = ahead
        rows = value.shape[0]
        if half > 1 and rows % 32 == 0:
            top, bottom = yield [
                self.shift(behind[: rows // 2], 1),
                self.shift(ahead[rows // 2 :], -1),
            ]
            blocks[half] = [top, bottom]
        else:
            blocks[half] = yield [self.shift(behind, 1)]
        return blocks

    def scatter_steps(self, part):
        count, half = self.count, self.count // 2
        if count == 1:
            return part(0).astype(f32)
        far = part(half).astype(bf16)
        if half == 1:
            (got,) = yield [self.shift(far, 1)]
            return part(0).astype(f32) + got.astype(f32)
        rows = far.shape[0]
        assert rows % 2 == 0
        cut = rows // 2
        ahead, behind = far[:cut], far[cut:]
        for k in range(half - 1, -1, -1):
            got_ahead, got_behind = yield [self.shift(ahead, 1), self.shift(behind, -1)]
            got_ahead, got_behind = got_ahead.astype(f32), got_behind.astype(f32)
            if k == 0:
                return part(0).astype(f32) + got_ahead + got_behind
            ahead, behind = part(k).astype(f32), part(count - k).astype(f32)
            if k == half - 1:
                ahead = jnp.concatenate([ahead[:cut] + got_ahead, ahead[cut:]], 0)
                behind = jnp.concatenate([behind[:cut], behind[cut:] + got_behind], 0)
            else:
                ahead, behind = ahead + got_ahead, behind + got_behind
            ahead, behind = ahead.astype(bf16), behind.astype(bf16)


class Flow:
    def __init__(self, steps):
        self.steps, self.pending, self.result = steps, [], None
        self.advance(None)

    def advance(self, arrived):
        try:
            self.pending = self.steps.send(arrived)
        except StopIteration as stop:
            self.pending, self.result = [], stop.value

    def finish(self):
        while self.pending:
            self.advance(self.pending)
        return self.result


def beside(values, *flows):
    values, arrived = lax.optimization_barrier((values, [flow.pending for flow in flows]))
    for flow, got in zip(flows, arrived):
        if got:
            flow.advance(got)
    return values


class Net:
    def __init__(self):
        self.seq_count = lax.axis_size("seq")
        self.dp_count = lax.axis_size("dp")
        self.order = seq_order(self.seq_count)
        self.seq = Ring("seq", [self.order])
        self.cores = 2 if self.dp_count % 2 == 0 else 1
        self.chips = self.dp_count // self.cores


def lookup(table, index):
    value = jnp.int32(table[0])
    for i, entry in enumerate(table):
        value = jnp.where(index == i, jnp.int32(entry), value)
    return value


class Links:
    def __init__(self, order, chips, cores):
        self.count, self.chips, self.cores = len(order), chips, cores
        me, dp = lax.axis_index("seq"), lax.axis_index("dp")
        count = self.count
        place = [0] * count
        for i, device in enumerate(order):
            place[device] = i
        self.seq_at = [
            lookup([order[(place[d] + k) % count] for d in range(count)], me) for k in range(count)
        ]
        self.ring = ({"seq": self.seq_at[1]}, {"seq": self.seq_at[count - 1]})
        chip, core = dp // cores, dp % cores
        self.chip = [
            {"dp": lax.rem(chip + step, chips) * cores + core} for step in range(1, chips)
        ]
        self.core = {"dp": chip * cores + (1 - core)} if cores == 2 else None
        self.dp_at = [
            lax.rem(chip + k, chips) * cores + lax.rem(core + c, cores)
            for c in range(cores)
            for k in range(chips)
        ]

    def greet(self):
        barrier = pltpu.get_barrier_semaphore()
        peers = list(self.ring) + self.chip + ([self.core] if self.cores == 2 else [])
        for peer in peers:
            pl.semaphore_signal(
                barrier, inc=1, device_id=peer, device_id_type=pl.DeviceIdType.MESH
            )
        pl.semaphore_wait(barrier, len(peers))


def remote(source, target, send_sem, recv_sem, peer):
    return pltpu.make_async_remote_copy(
        src_ref=source,
        dst_ref=target,
        send_sem=send_sem,
        recv_sem=recv_sem,
        device_id=peer,
        device_id_type=pl.DeviceIdType.MESH,
    )


RING_FIRST, CHIP_FIRST, RING_ONLY = 0, 1, 2


def gather_kernel(order, chips, cores, pieces, arrays, *refs):
    ins, outs = refs[:arrays], refs[arrays : 2 * arrays]
    own_sem, recv_sem, ring_sem, chip_sem, core_sem = refs[2 * arrays :]
    links = Links(order, chips, cores)
    count, half = links.count, links.count // 2
    links.greet()
    method = [piece[3] for piece in pieces]
    only_ring = {piece[0] for piece in pieces if piece[3] == RING_ONLY}

    base = [sum(chips if way == CHIP_FIRST else 1 for way in method[:p]) for p in range(len(pieces) + 1)]

    def slot(i, r, k):
        return outs[i].at[0 if i in only_ring else links.dp_at[r], links.seq_at[k]]

    owns = [
        pltpu.make_async_copy(ins[i], slot(i, 0, 0), own_sem.at[i])
        for i in range(arrays)
    ]
    for copy in owns:
        copy.start()
    sent = []

    def whole(p, r, k):
        array, first, rows, _ = pieces[p]
        place = slot(array, r, k)
        return place if rows == ins[array].shape[0] else place.at[pl.ds(first, rows)]

    def rows_in(p, r, k, first, rows):
        return slot(pieces[p][0], r, k).at[pl.ds(pieces[p][1] + first, rows)]

    def held(p, r, k):
        array, first, rows, _ = pieces[p]
        if r == 0 and k == 0:
            return ins[array] if rows == ins[array].shape[0] else ins[array].at[pl.ds(first, rows)]
        return whole(p, r, k)

    def cut_of(p):
        return pieces[p][2] // 32 * 16

    def start(copy):
        copy.start()
        sent.append(copy)

    def ring_copies(p, r, s):
        cut, rows = cut_of(p), pieces[p][2]
        if s < half - 1:
            return [
                remote(
                    held(p, r, (count - s) % count), whole(p, r, (count - s) % count),
                    ring_sem.at[base[p] + r, 0, s], recv_sem.at[p, r, count - s - 1], links.ring[0],
                ),
                remote(
                    held(p, r, s), whole(p, r, s),
                    ring_sem.at[base[p] + r, 1, s], recv_sem.at[p, r, s + 1], links.ring[1],
                ),
            ]
        back = count - s
        if not cut:
            return [
                remote(
                    whole(p, r, back), whole(p, r, back),
                    ring_sem.at[base[p] + r, 0, s], recv_sem.at[p, r, half], links.ring[0],
                )
            ]
        top, bottom = rows_in(p, r, back, 0, cut), rows_in(p, r, s, cut, rows - cut)
        return [
            remote(top, top, ring_sem.at[base[p] + r, 0, s], recv_sem.at[p, r, half], links.ring[0]),
            remote(
                bottom, bottom, ring_sem.at[base[p] + r, 1, s], recv_sem.at[p, r, count], links.ring[1]
            ),
        ]

    def arrived(p, r, k):
        cut, rows = cut_of(p), pieces[p][2]
        if k == half and cut:
            for part, sem in (((0, cut), half), ((cut, rows - cut), count)):
                ref = rows_in(p, r, k, *part)
                remote(ref, ref, ring_sem.at[base[p], 0, 0], recv_sem.at[p, r, sem], links.ring[0]).wait_recv()
        else:
            ref = whole(p, r, k)
            remote(ref, ref, ring_sem.at[base[p], 0, 0], recv_sem.at[p, r, k], links.ring[0]).wait_recv()

    def to_chips(p, k):
        for step in range(1, chips):
            start(
                remote(
                    held(p, 0, k), whole(p, 0, k),
                    chip_sem.at[p, step - 1, k], recv_sem.at[p, chips - step, k], links.chip[step - 1],
                )
            )

    def to_core(p, r, k):
        if cores == 2:
            start(
                remote(
                    held(p, r, k), whole(p, r, k),
                    core_sem.at[p, r, k], recv_sem.at[p, chips + r, k], links.core,
                )
            )

    everyone = range(len(pieces))

    def planes(p):
        return range(chips) if method[p] == CHIP_FIRST else range(1)

    for p in everyone:
        if method[p] != RING_ONLY:
            to_chips(p, 0)
        for copy in ring_copies(p, 0, 0):
            start(copy)
    for p in everyone:
        if method[p] != RING_ONLY:
            to_core(p, 0, 0)
    for s in range(1, half + 1):
        steps = sorted({count - s, s})
        before = sorted({(count - s + 1) % count, s - 1})
        for p in everyone:
            for r in planes(p):
                if r == 0 or s > 1:
                    for k in steps:
                        arrived(p, r, k)
                    if s < half:
                        for copy in ring_copies(p, r, s):
                            start(copy)
                    if method[p] == RING_FIRST:
                        for k in steps:
                            to_chips(p, k)
                    if method[p] != RING_ONLY:
                        for k in steps:
                            to_core(p, r, k)
        for p in everyone:
            if method[p] == RING_FIRST:
                for r in range(1, chips):
                    for k in before:
                        arrived_from_chip(links, whole(p, r, k), chip_sem.at[p, 0, 0], recv_sem.at[p, r, k])
                        to_core(p, r, k)
            if method[p] == CHIP_FIRST and s == 1:
                for r in range(1, chips):
                    arrived_from_chip(links, whole(p, r, 0), chip_sem.at[p, 0, 0], recv_sem.at[p, r, 0])
                    for copy in ring_copies(p, r, 0):
                        start(copy)
                    to_core(p, r, 0)
                for r in range(1, chips):
                    for k in steps:
                        arrived(p, r, k)
                    if s < half:
                        for copy in ring_copies(p, r, s):
                            start(copy)
                    for k in steps:
                        to_core(p, r, k)
    for p in everyone:
        if method[p] == RING_FIRST:
            for r in range(1, chips):
                arrived_from_chip(links, whole(p, r, half), chip_sem.at[p, 0, 0], recv_sem.at[p, r, half])
                to_core(p, r, half)
    for p in everyone:
        if method[p] != RING_ONLY and cores == 2:
            for r in range(chips):
                for k in range(count):
                    arrived_from_chip(
                        links, whole(p, chips + r, k), core_sem.at[p, r, k], recv_sem.at[p, chips + r, k]
                    )
    for copy in sent:
        copy.wait_send()
    for copy in owns:
        copy.wait()


def arrived_from_chip(links, ref, send_sem, recv_sem):
    remote(ref, ref, send_sem, recv_sem, links.ring[0]).wait_recv()


def gather_call(net, arrays, pieces):
    chips, cores, count = net.chips, net.cores, net.seq_count
    slots = chips * cores
    only_ring = {piece[0] for piece in pieces if piece[3] == RING_ONLY}
    anywhere = pl.BlockSpec(memory_space=pl.ANY)
    return pl.pallas_call(
        functools.partial(gather_kernel, net.order, chips, cores, pieces, len(arrays)),
        out_shape=[
            jax.ShapeDtypeStruct((1 if i in only_ring else slots, count) + v.shape, v.dtype)
            for i, v in enumerate(arrays)
        ],
        in_specs=[anywhere] * len(arrays),
        out_specs=[anywhere] * len(arrays),
        scratch_shapes=[
            pltpu.SemaphoreType.DMA((len(arrays),)),
            pltpu.SemaphoreType.DMA((len(pieces), slots, count + 1)),
            pltpu.SemaphoreType.DMA(
                (sum(chips if piece[3] == CHIP_FIRST else 1 for piece in pieces), 2, count // 2)
            ),
            pltpu.SemaphoreType.DMA((len(pieces), max(chips - 1, 1), count)),
            pltpu.SemaphoreType.DMA((len(pieces), chips, count)),
        ],
        compiler_params=pltpu.CompilerParams(
            collective_id=3, has_side_effects=True, vmem_limit_bytes=32 * 2**20
        ),
        cost_estimate=pl.CostEstimate(
            flops=0, bytes_accessed=slots * count * sum(v.size for v in arrays) * 4, transcendentals=0
        ),
    )(*arrays)


def add_rows(target, terms, rows):
    if rows % 16:
        target[...] = total([term[...].astype(f32) for term in terms]).astype(target.dtype)
        return

    def body(t, carry):
        at = pl.ds(pl.multiple_of(t * 16, 16), 16)
        target[at] = total([term[at].astype(f32) for term in terms]).astype(target.dtype)
        return carry

    lax.fori_loop(0, rows // 16, body, 0)


def total(terms):
    result = terms[0]
    for term in terms[1:]:
        result = result + term
    return result


def reduce_kernel(order, chips, cores, pieces, arrays, *refs):
    count, half = len(order), len(order) // 2
    parts, refs = refs[:arrays], refs[arrays:]
    outs, refs = refs[:arrays], refs[arrays:]
    mine, refs = refs[:arrays], refs[arrays:]
    other, refs = refs[:arrays], refs[arrays:]
    chip_in, refs = refs[: len(pieces)], refs[len(pieces) :]
    ring_in, refs = refs[: len(pieces)], refs[len(pieces) :]
    load_sem, core_send, core_recv, chip_send, chip_recv, ring_send, ring_recv = refs
    links = Links(order, chips, cores)
    everyone = range(len(pieces))
    method = [piece[3] for piece in pieces]

    loads = [
        [
            pltpu.make_async_copy(parts[i].at[links.dp_at[k]], mine[i].at[k], load_sem.at[i, k])
            for k in range(chips)
        ]
        for i in range(arrays)
    ]
    for copies in loads:
        for copy in copies:
            copy.start()
    links.greet()
    sent = []

    def start(copy):
        copy.start()
        sent.append(copy)

    def rows_of_piece(ref, p, first=0, rows=None):
        array, start_row, piece_rows, _ = pieces[p]
        rows = piece_rows if rows is None else rows
        if rows == ref.shape[0]:
            return ref
        return ref.at[pl.ds(start_row + first, rows)]

    def held(p, k, q):
        return rows_of_piece(mine[pieces[p][0]].at[k, links.seq_at[q]], p)

    def core_copy(p, k, q):
        array = pieces[p][0]
        return remote(
            rows_of_piece(parts[array].at[links.dp_at[chips + k], links.seq_at[q]], p),
            rows_of_piece(other[array].at[k, links.seq_at[q]], p),
            core_send.at[p, k, q], core_recv.at[p, k, q], links.core,
        )

    def steps(d):
        return sorted({d % count, (count - d) % count})

    def planes(p):
        return range(chips) if method[p] == RING_FIRST else range(1)

    if cores == 2:
        for d in range(half, -1, -1):
            for p in everyone:
                for k in reversed(range(chips)):
                    for q in steps(d):
                        start(core_copy(p, k, q))

    loaded = set()

    def core_sum(p, k, q):
        array = pieces[p][0]
        if (array, k) not in loaded:
            loaded.add((array, k))
            loads[array][k].wait()
        if cores == 2:
            core_copy(p, k, q).wait_recv()
            theirs = rows_of_piece(other[array].at[k, links.seq_at[q]], p)
            add_rows(held(p, k, q), [held(p, k, q), theirs], pieces[p][2])

    def chip_copy(p, k, q):
        if method[p] == CHIP_FIRST:
            target = chip_in[p].at[k - 1, links.seq_at[q]]
        else:
            target = chip_in[p].at[k - 1]
        return remote(
            held(p, k, q), target, chip_send.at[p, k - 1, q], chip_recv.at[p, k - 1, q], links.chip[k - 1]
        )

    def chip_sum(p, q):
        for k in range(1, chips):
            chip_copy(p, k, q).wait_recv()
            if method[p] == CHIP_FIRST:
                add_rows(held(p, 0, q), [held(p, 0, q), chip_in[p].at[k - 1, links.seq_at[q]]], pieces[p][2])
            else:
                out = rows_of_piece(outs[pieces[p][0]], p)
                add_rows(out, [out, chip_in[p].at[k - 1]], pieces[p][2])

    def span(p, side, d):
        rows = pieces[p][2]
        cut = rows // 32 * 16
        if d < half:
            return (0, rows)
        if not cut:
            return (0, rows) if side == 0 else None
        return (0, cut) if side == 0 else (cut, rows - cut)

    def ring_copy(p, k, side, d):
        first, rows = span(p, side, d)
        q = d if side == 0 else (count - d) % count
        source = held(p, k, q)
        target = ring_in[p].at[k, side, d - 1]
        if rows != pieces[p][2]:
            source, target = source.at[pl.ds(first, rows)], target.at[pl.ds(first, rows)]
        return remote(
            source, target, ring_send.at[p, k, side, d - 1], ring_recv.at[p, k, side, d - 1], links.ring[side]
        )

    def ring_step(p, k, d):
        if d == 0:
            got = []
            for side in range(2):
                if half > 1 or span(p, side, 1):
                    ring_copy(p, k, side, 1).wait_recv()
                    got.append(ring_in[p].at[k, side, 0])
            target = rows_of_piece(outs[pieces[p][0]], p) if k == 0 else held(p, k, 0)
            add_rows(target, [held(p, k, 0)] + got, pieces[p][2])
            return
        for side in range(2):
            if span(p, side, d) is None:
                continue
            if d < half and span(p, side, d + 1) is not None:
                ring_copy(p, k, side, d + 1).wait_recv()
                first, rows = span(p, side, d + 1)
                target = held(p, k, d if side == 0 else count - d)
                term = ring_in[p].at[k, side, d]
                if rows != pieces[p][2]:
                    target, term = target.at[pl.ds(first, rows)], term.at[pl.ds(first, rows)]
                add_rows(target, [target, term], rows)
            start(ring_copy(p, k, side, d))

    for d in range(half, -1, -1):
        for p in everyone:
            if method[p] == RING_FIRST:
                for k in reversed(planes(p)):
                    for q in steps(d):
                        core_sum(p, k, q)
                    ring_step(p, k, d)
                    if d == 0 and k > 0:
                        start(chip_copy(p, k, 0))
        for p in everyone:
            if method[p] == CHIP_FIRST:
                for q in steps(d):
                    for k in reversed(range(chips)):
                        core_sum(p, k, q)
                        if k > 0:
                            start(chip_copy(p, k, q))
        for p in everyone:
            if method[p] == CHIP_FIRST and d < half:
                for q in steps(d + 1):
                    chip_sum(p, q)
                ring_step(p, 0, d + 1)
    for p in everyone:
        if method[p] == CHIP_FIRST:
            chip_sum(p, 0)
            ring_step(p, 0, 0)
    for p in everyone:
        if method[p] == RING_FIRST:
            chip_sum(p, 0)
    for copy in sent:
        copy.wait_send()


def reduce_call(net, arrays, pieces):
    chips, cores, count = net.chips, net.cores, net.seq_count
    half = count // 2
    anywhere = pl.BlockSpec(memory_space=pl.ANY)
    shapes = [terms.shape[2:] for terms in arrays]
    ahead = max(chips - 1, 1)
    blocks = [(piece[2], shapes[piece[0]][1]) for piece in pieces]
    chip_shapes = [
        (ahead, count) + block if piece[3] == CHIP_FIRST else (ahead,) + block
        for piece, block in zip(pieces, blocks)
    ]
    ring_shapes = [
        (chips if piece[3] == RING_FIRST else 1, 2, half) + block
        for piece, block in zip(pieces, blocks)
    ]
    n = len(pieces)
    return pl.pallas_call(
        functools.partial(reduce_kernel, net.order, chips, cores, pieces, len(arrays)),
        out_shape=[jax.ShapeDtypeStruct(shape, f32) for shape in shapes],
        in_specs=[anywhere] * len(arrays),
        out_specs=[pl.BlockSpec(memory_space=pltpu.VMEM)] * len(arrays),
        scratch_shapes=[pltpu.VMEM((chips, count) + shape, bf16) for shape in shapes]
        + [pltpu.VMEM((chips, count) + shape, bf16) for shape in shapes]
        + [pltpu.VMEM(shape, bf16) for shape in chip_shapes]
        + [pltpu.VMEM(shape, bf16) for shape in ring_shapes]
        + [
            pltpu.SemaphoreType.DMA((len(arrays), chips)),
            pltpu.SemaphoreType.DMA((n, chips, count)),
            pltpu.SemaphoreType.DMA((n, chips, count)),
            pltpu.SemaphoreType.DMA((n, ahead, count)),
            pltpu.SemaphoreType.DMA((n, ahead, count)),
            pltpu.SemaphoreType.DMA((n, chips, 2, half)),
            pltpu.SemaphoreType.DMA((n, chips, 2, half)),
        ],
        compiler_params=pltpu.CompilerParams(
            collective_id=4, has_side_effects=True, vmem_limit_bytes=62 * 2**20
        ),
        cost_estimate=pl.CostEstimate(
            flops=0, bytes_accessed=sum(terms.size for terms in arrays) * 4, transcendentals=0
        ),
    )(*arrays)


def exchange(totals, everyone, send_sem, recv_sem, count):
    me = lax.axis_index("seq")
    everyone[me] = totals[...]
    copies = []
    for step in range(1, count):
        peer = lax.rem(me + step, count)
        copy = pltpu.make_async_remote_copy(
            src_ref=totals,
            dst_ref=everyone.at[me],
            send_sem=send_sem.at[step],
            recv_sem=recv_sem.at[step],
            device_id={"seq": peer},
            device_id_type=pl.DeviceIdType.MESH,
        )
        copy.start()
    for step in range(1, count):
        source = lax.rem(me + count - step, count)
        copy = pltpu.make_async_remote_copy(
            src_ref=totals,
            dst_ref=everyone.at[source],
            send_sem=send_sem.at[step],
            recv_sem=recv_sem.at[step],
            device_id={"seq": source},
            device_id_type=pl.DeviceIdType.MESH,
        )
        copy.wait()


def greet(count):
    me = lax.axis_index("seq")
    barrier = pltpu.get_barrier_semaphore()
    for step in range(1, count):
        pl.semaphore_signal(
            barrier,
            inc=1,
            device_id={"seq": lax.rem(me + step, count)},
            device_id_type=pl.DeviceIdType.MESH,
        )
    pl.semaphore_wait(barrier, count - 1)


def tiles(channels):
    wide = 512 if channels % 512 == 0 else 128
    return [pl.ds(at, wide) for at in range(0, channels, wide)]


def tile_prefix(product, total, step):
    row = lax.broadcasted_iota(jnp.int32, product.shape, 0)
    reach = 1
    while reach < LANES:
        turn = reach if step > 0 else LANES - reach
        inside = row >= reach if step > 0 else row < LANES - reach
        total = total + product * jnp.where(inside, pltpu.roll(total, turn, 0), 0.0)
        product = product * jnp.where(inside, pltpu.roll(product, turn, 0), 1.0)
        reach *= 2
    return (product, total)


def scan_kernel(
    count, decay_ref, drive_ref, start_ref, state_ref, prev_ref, last_ref,
    totals, everyone, send_sem, recv_sem,
):
    greet(count)
    rows, channels = decay_ref.shape
    end = LANES - 1
    for cols in tiles(channels):

        def first_pass(t, carry):
            run_product, run_sum = carry
            at = pl.ds(pl.multiple_of(t * LANES, LANES), LANES)
            product, total = tile_prefix(decay_ref[at, cols], drive_ref[at, cols], 1)
            prev_ref[at, cols] = product
            state_ref[at, cols] = total
            last = product[end:]
            return (last * run_product, last * run_sum + total[end:])

        zero = jnp.zeros((1, cols.size), f32)
        run_product, run_sum = lax.fori_loop(
            0, rows // LANES, first_pass, (zero + 1.0, zero), unroll=4
        )
        totals[0:1, cols] = run_product
        totals[1:2, cols] = run_sum
    exchange(totals, everyone, send_sem, recv_sem, count)
    me = lax.axis_index("seq")
    for cols in tiles(channels):
        state = start_ref[0:1, cols]
        entering = state
        for device in range(count):
            entering = jnp.where(me == device, state, entering)
            state = everyone[device, 0:1, cols] * state + everyone[device, 1:2, cols]
        last_ref[0:1, cols] = state

        def second_pass(t, entry):
            at = pl.ds(pl.multiple_of(t * LANES, LANES), LANES)
            state = prev_ref[at, cols] * entry + state_ref[at, cols]
            row = lax.broadcasted_iota(jnp.int32, state.shape, 0)
            state_ref[at, cols] = state
            prev_ref[at, cols] = jnp.where(row == 0, entry, pltpu.roll(state, 1, 0))
            return state[end:]

        lax.fori_loop(0, rows // LANES, second_pass, entering, unroll=4)


def scan_back_kernel(
    count, decay_ref, d_state_ref, prev_ref, d_drive_ref, d_decay_ref,
    totals, everyone, send_sem, recv_sem,
):
    greet(count)
    rows, channels = decay_ref.shape
    last_tile = rows // LANES - 1
    end = LANES - 1
    for cols in tiles(channels):

        def first_pass(i, carry):
            run_product, run_sum = carry
            at = pl.ds(pl.multiple_of((last_tile - i) * LANES, LANES), LANES)
            decay = decay_ref[at, cols]
            product, total = tile_prefix(decay, decay * d_state_ref[at, cols], -1)
            d_decay_ref[at, cols] = product
            d_drive_ref[at, cols] = total
            first = product[:1]
            return (first * run_product, first * run_sum + total[:1])

        zero = jnp.zeros((1, cols.size), f32)
        run_product, run_sum = lax.fori_loop(
            0, rows // LANES, first_pass, (zero + 1.0, zero), unroll=4
        )
        totals[0:1, cols] = run_product
        totals[1:2, cols] = run_sum
    exchange(totals, everyone, send_sem, recv_sem, count)
    me = lax.axis_index("seq")
    for cols in tiles(channels):
        state = jnp.zeros((1, cols.size), f32)
        entering = state
        for device in reversed(range(count)):
            entering = jnp.where(me == device, state, entering)
            state = everyone[device, 0:1, cols] * state + everyone[device, 1:2, cols]

        def second_pass(i, entry):
            at = pl.ds(pl.multiple_of((last_tile - i) * LANES, LANES), LANES)
            outgoing = d_decay_ref[at, cols] * entry + d_drive_ref[at, cols]
            row = lax.broadcasted_iota(jnp.int32, outgoing.shape, 0)
            incoming = jnp.where(row == end, entry, pltpu.roll(outgoing, end, 0))
            carry = d_state_ref[at, cols] + incoming
            d_drive_ref[at, cols] = carry
            d_decay_ref[at, cols] = carry * prev_ref[at, cols]
            return outgoing[:1]

        lax.fori_loop(0, rows // LANES, second_pass, entering, unroll=4)


def scan_call(kernel, collective_id, count, operands, out_shapes):
    channels = operands[0].shape[1]
    vmem = pl.BlockSpec(memory_space=pltpu.VMEM)
    return pl.pallas_call(
        functools.partial(kernel, count),
        out_shape=out_shapes,
        in_specs=[vmem] * len(operands),
        out_specs=[vmem] * len(out_shapes),
        scratch_shapes=[
            pltpu.VMEM((2, channels), f32),
            pltpu.VMEM((count, 2, channels), f32),
            pltpu.SemaphoreType.DMA((count,)),
            pltpu.SemaphoreType.DMA((count,)),
        ],
        compiler_params=pltpu.CompilerParams(
            collective_id=collective_id, has_side_effects=True, vmem_limit_bytes=40 * 2**20
        ),
        cost_estimate=pl.CostEstimate(
            flops=8 * operands[0].size, bytes_accessed=20 * operands[0].size, transcendentals=0
        ),
    )(*operands)


def gate_parts(conv_ref, both_ref, vectors_ref, reset_ref):
    conv = conv_ref[...].astype(f32)
    pre = contract(conv_ref[...], both_ref[...], 1, 0)
    rate = jax.nn.sigmoid(pre[:, :HW] + vectors_ref[0:1])
    in_gate = jax.nn.sigmoid(pre[:, HW:] + vectors_ref[1:2])
    log_decay = vectors_ref[2:3] * rate
    reset = reset_ref[...]
    keep = 1.0 - reset
    decay = jnp.exp(log_decay)
    bend = jnp.tanh(-log_decay)
    power = 2.0 * bend / (1.0 + bend)
    root = jnp.sqrt(jnp.maximum(power, floor_value))
    return conv, rate, in_gate, decay, keep, power, root, reset + keep * root


def gate_kernel(conv_ref, both_ref, vectors_ref, reset_ref, decay_ref, drive_ref):
    conv, _, in_gate, decay, keep, _, _, share = gate_parts(
        conv_ref, both_ref, vectors_ref, reset_ref
    )
    decay_ref[...] = decay * keep
    drive_ref[...] = share * in_gate * conv


def gate_back_kernel(
    conv_ref, both_ref, vectors_ref, reset_ref, d_decay_ref, d_drive_ref,
    d_conv_ref, grad_ref, sums_ref,
):
    conv, rate, in_gate, decay, keep, power, root, share = gate_parts(
        conv_ref, both_ref, vectors_ref, reset_ref
    )
    d_drive = d_drive_ref[...]
    through = jnp.where(
        power > floor_value, d_drive * keep * in_gate * conv * (decay * decay) / root, 0.0
    )
    d_log = d_decay_ref[...] * decay * keep - through
    d_rate = (d_log * vectors_ref[2:3] * rate * (1.0 - rate)).astype(bf16)
    d_input = (d_drive * share * conv * in_gate * (1.0 - in_gate)).astype(bf16)
    d_both = jnp.concatenate([d_rate, d_input], 1)
    d_conv = (d_drive * share * in_gate + contract(d_both, both_ref[...], 1, 1)).astype(bf16)
    d_conv_ref[...] = d_conv
    grad_ref[...] = contract(conv_ref[...], d_both, 0, 0).astype(bf16)
    sums_ref[0:1] = jnp.sum(d_rate.astype(f32), axis=0, keepdims=True)
    sums_ref[1:2] = jnp.sum(d_input.astype(f32), axis=0, keepdims=True)
    sums_ref[2:3] = jnp.sum(d_log * rate, axis=0, keepdims=True)
    sums_ref[3:4] = jnp.sum(d_conv.astype(f32), axis=0, keepdims=True)


def gate_call(kernel, conv, both, vectors, reset, grads, out_kinds):
    rows, channels = conv.shape
    per_row = pl.BlockSpec((rows, HW), lambda h: (0, h))
    kinds = {
        "rows": (per_row, (rows, channels)),
        "weights": (pl.BlockSpec((HW, 2 * HW), lambda h: (h, 0)), (channels, 2 * HW)),
        "sums": (pl.BlockSpec((4, HW), lambda h: (0, h)), (4, channels)),
    }
    return pl.pallas_call(
        kernel,
        grid=(channels // HW,),
        out_shape=[jax.ShapeDtypeStruct(kinds[kind][1], dtype) for kind, dtype in out_kinds],
        in_specs=[
            per_row,
            kinds["weights"][0],
            pl.BlockSpec((vectors.shape[0], HW), lambda h: (0, h)),
            pl.BlockSpec((rows, 1), lambda h: (0, 0)),
        ]
        + [per_row] * len(grads),
        out_specs=[kinds[kind][0] for kind, _ in out_kinds],
        compiler_params=pltpu.CompilerParams(vmem_limit_bytes=32 * 2**20),
        cost_estimate=pl.CostEstimate(
            flops=4 * rows * channels * HW * (1 + 2 * len(grads)),
            bytes_accessed=24 * rows * channels,
            transcendentals=6 * rows * channels,
        ),
    )(conv, both, vectors, reset, *grads)


def pair_slots(count):
    half = count // 2
    return [k for s in range(1, half) for k in (count - s, s)] + [half, 0]


def gelu_parts(v):
    root, cubic = 0.7978845608028654, 0.044715
    curve = jnp.tanh(root * (v + cubic * v * v * v))
    act = 0.5 * v * (1.0 + curve)
    slope = 0.5 * (1.0 + curve) + 0.5 * v * (1.0 - curve * curve) * root * (
        1.0 + 3.0 * cubic * v * v
    )
    return (act, slope)


def contract(left, right, left_dim, right_dim):
    return lax.dot_general(
        left, right, (((left_dim,), (right_dim,)), ((), ())), preferred_element_type=f32
    )


def ff_kernel(
    order, own_ref, gate_hbm, up_hbm, down_hbm, *refs
):
    cot_count = len(refs) - 21
    cot_hbm, refs = refs[:cot_count], refs[cot_count:]
    blocks_ref, cot_ref, hidden_ref, d_gate_ref, d_up_ref, out_ref, d_in_ref, *refs = refs
    gate_ref, up_ref, down_ref, rows_ref, cots_ref, h_ref, g_ref, u_ref, o_ref, d_ref, *refs = refs
    send_sem, recv_sem, load_sem, store_sem = refs
    count = len(order)
    half = count // 2
    rows, width = own_ref.shape
    hidden_here = gate_ref.shape[1]
    cut = rows // 2
    me = lax.axis_index("seq")
    ahead_of, behind_of = [0] * count, [0] * count
    for i, device in enumerate(order):
        ahead_of[device] = order[(i + 1) % count]
        behind_of[device] = order[(i - 1) % count]
    sides = (lookup(ahead_of, me), lookup(behind_of, me))

    barrier = pltpu.get_barrier_semaphore()
    for side in sides:
        pl.semaphore_signal(
            barrier, inc=1, device_id={"seq": side}, device_id_type=pl.DeviceIdType.MESH
        )
    weights = [
        pltpu.make_async_copy(hbm, vmem, load_sem.at[i])
        for i, (hbm, vmem) in enumerate(
            ((gate_hbm, gate_ref), (up_hbm, up_ref), (down_hbm, down_ref))
        )
    ]
    for copy in weights:
        copy.start()
    keep = pltpu.make_async_copy(own_ref, blocks_ref.at[count - 1], load_sem.at[3])
    keep.start()
    pl.semaphore_wait(barrier, 2)

    def full(side, source, slot, s):
        return pltpu.make_async_remote_copy(
            src_ref=source,
            dst_ref=blocks_ref.at[slot],
            send_sem=send_sem.at[side, s],
            recv_sem=recv_sem.at[slot],
            device_id={"seq": sides[side]},
            device_id_type=pl.DeviceIdType.MESH,
        )

    def part(side):
        at = pl.ds(0, cut) if side == 0 else pl.ds(cut, rows - cut)
        return pltpu.make_async_remote_copy(
            src_ref=blocks_ref.at[2 * (half - 2) + side, at],
            dst_ref=blocks_ref.at[count - 2, at],
            send_sem=send_sem.at[side, half - 1],
            recv_sem=recv_sem.at[count - 2 + side],
            device_id={"seq": sides[side]},
            device_id_type=pl.DeviceIdType.MESH,
        )

    for side in range(2):
        full(side, own_ref, side, 0).start()
    keep.wait()
    for copy in weights:
        copy.wait()

    rows_load = lambda s: pltpu.make_async_copy(
        blocks_ref.at[pl.ds(2 * (s - 1), 2)], rows_ref, load_sem.at[4]
    )

    def cot_loads(s):
        if s < half:
            return [
                pltpu.make_async_copy(cot_hbm[2 * s - 1 + i], cots_ref.at[i], load_sem.at[5 + i])
                for i in range(2)
            ]
        copies = [pltpu.make_async_copy(cot_hbm[0], cots_ref.at[1], load_sem.at[5])]
        first = 0
        for i, part_hbm in enumerate(cot_hbm[2 * half - 1 :]):
            part_rows = part_hbm.shape[0]
            copies.append(
                pltpu.make_async_copy(
                    part_hbm, cots_ref.at[0, pl.ds(first, part_rows)], load_sem.at[6 + i]
                )
            )
            first += part_rows
        return copies

    def stores(s):
        return [
            pltpu.make_async_copy(vmem, hbm.at[s - 1], store_sem.at[i])
            for i, (vmem, hbm) in enumerate(
                (
                    (cots_ref, cot_ref),
                    (h_ref, hidden_ref),
                    (g_ref, d_gate_ref),
                    (u_ref, d_up_ref),
                    (o_ref, out_ref),
                    (d_ref, d_in_ref),
                )
            )
        ]

    def step(s, carry):
        @pl.when(s < half)
        def _():
            for side in range(2):
                full(side, own_ref, 2 * (s - 1) + side, s).wait_recv()

            @pl.when(s < half - 1)
            def _():
                for side in range(2):
                    slot = 2 * (s - 1) + side
                    full(side, blocks_ref.at[slot], slot + 2, s).start()

            @pl.when(s == half - 1)
            def _():
                for side in range(2):
                    part(side).start()

        @pl.when(s == half)
        def _():
            for side in range(2):
                part(side).wait_recv()

        rows_load(s).start()

        @pl.when(s > 1)
        def _():
            for copy in stores(s - 1):
                copy.wait()

        for at_step in range(1, half + 1):

            @pl.when(s == at_step)
            def _():
                copies = cot_loads(at_step)
                for copy in copies:
                    copy.start()
                for copy in copies:
                    copy.wait()

        rows_load(s).wait()
        wide = 256 if hidden_here % 256 == 0 else 128

        def inner(j, carry):
            at = pl.ds(pl.multiple_of(j * wide, wide), wide)
            x = rows_ref[...].reshape(2 * rows, width)
            c = cots_ref[...].reshape(2 * rows, width)
            ff_gate = contract(x, gate_ref[:, at], 1, 0)
            ff_up = contract(x, up_ref[:, at], 1, 0)
            d_hidden = contract(c, down_ref[at, :], 1, 1)
            act, slope = gelu_parts(ff_gate)
            h_ref[:, at] = (act * ff_up).astype(bf16)
            g_ref[:, at] = (d_hidden * ff_up * slope).astype(bf16)
            u_ref[:, at] = (d_hidden * act).astype(bf16)
            return carry

        lax.fori_loop(0, hidden_here // wide, inner, 0)
        out_wide = 512

        def outer(j, carry):
            at = pl.ds(pl.multiple_of(j * out_wide, out_wide), out_wide)
            o_ref[:, at] = contract(h_ref[...], down_ref[:, at], 1, 0).astype(bf16)
            d_ref[:, at] = (
                contract(g_ref[...], gate_ref[at, :], 1, 1)
                + contract(u_ref[...], up_ref[at, :], 1, 1)
            ).astype(bf16)
            return carry

        lax.fori_loop(0, width // out_wide, outer, 0)
        for copy in stores(s):
            copy.start()
        return carry

    lax.fori_loop(1, half + 1, step, 0)
    for copy in stores(half):
        copy.wait()
    for side in range(2):
        for s in range(half - 1):
            full(side, own_ref, side, s).wait_send()
        part(side).wait_send()


def ff_call(order, own, cots, slab_gate, slab_up, slab_down):
    rows, width = own.shape
    count, half = len(order), len(order) // 2
    hidden_here = slab_gate.shape[1]
    anywhere = pl.BlockSpec(memory_space=pl.ANY)
    pair = 2 * rows
    shape = jax.ShapeDtypeStruct
    flops = 12 * count * rows * width * hidden_here
    return pl.pallas_call(
        functools.partial(ff_kernel, order),
        out_shape=[shape((count, rows, width), bf16), shape((half, 2, rows, width), bf16)]
        + [shape((half, pair, hidden_here), bf16)] * 3
        + [shape((half, pair, width), bf16)] * 2,
        in_specs=[anywhere] * (4 + len(cots)),
        out_specs=[anywhere] * 7,
        scratch_shapes=[
            pltpu.VMEM((width, hidden_here), bf16),
            pltpu.VMEM((width, hidden_here), bf16),
            pltpu.VMEM((hidden_here, width), bf16),
            pltpu.VMEM((2, rows, width), bf16),
            pltpu.VMEM((2, rows, width), bf16),
            pltpu.VMEM((pair, hidden_here), bf16),
            pltpu.VMEM((pair, hidden_here), bf16),
            pltpu.VMEM((pair, hidden_here), bf16),
            pltpu.VMEM((pair, width), bf16),
            pltpu.VMEM((pair, width), bf16),
            pltpu.SemaphoreType.DMA((2, half)),
            pltpu.SemaphoreType.DMA((count,)),
            pltpu.SemaphoreType.DMA((8,)),
            pltpu.SemaphoreType.DMA((6,)),
        ],
        compiler_params=pltpu.CompilerParams(
            collective_id=2, has_side_effects=True, vmem_limit_bytes=48 * 2**20
        ),
        cost_estimate=pl.CostEstimate(
            flops=flops, bytes_accessed=60 * 2**20, transcendentals=count * rows * hidden_here
        ),
    )(own, slab_gate, slab_up, slab_down, *cots)


def passed_along(value, axis, steps):
    count = lax.axis_size(axis)
    first, last = (max(0, -steps), min(count, count - steps))
    return lax.ppermute(value, axis, [(source, source + steps) for source in range(first, last)])


def gelu_tanh(values):
    return jax.nn.gelu(values, approximate=True)


def rms_parts(values, norm_gain):
    root_scale = lax.rsqrt(jnp.mean(values * values, axis=-1, keepdims=True) + epsilon)
    unit_rows = values * root_scale
    return (unit_rows * norm_gain, root_scale, unit_rows)


def norm_back(d_normed, norm_gain, root_scale, unit_rows):
    weighted = d_normed * norm_gain
    grad_gain = jnp.sum(d_normed * unit_rows, axis=0)
    d_values = root_scale * (
        weighted - unit_rows * jnp.mean(weighted * unit_rows, axis=-1, keepdims=True)
    )
    return (grad_gain, d_values)


def rows_of(values, first_row, row_count):
    return lax.slice_in_dim(values, first_row, first_row + row_count, axis=values.ndim - 2)


def dot(left, right):
    return jnp.dot(left, right, preferred_element_type=f32)


def dot_t(left, right):
    return lax.dot_general(left, right, (((1,), (1,)), ((), ())), preferred_element_type=f32)


def t_dot(left, right):
    return lax.dot_general(left, right, (((0,), (0,)), ((), ())), preferred_element_type=f32)


def per_device(
    inputs,
    reset,
    initial_state,
    cotangent,
    norm1_gain,
    w_gate,
    w_in,
    conv_w,
    conv_bias,
    w_rgate,
    rgate_bias,
    w_igate,
    igate_bias,
    decay_param,
    w_out,
    norm2_gain,
    w_ffgate,
    w_ffup,
    w_ffdown,
):
    net = Net()
    seqs_here, len_here, width = inputs.shape
    assert seqs_here == 1
    rows_here = len_here
    dp_count, seq_count = net.dp_count, net.seq_count
    devices = dp_count * seq_count
    chan_here, channels = w_rgate.shape[0], w_rgate.shape[0] * devices
    wide_here = norm1_gain.shape[0]
    taps = conv_w.shape[0]
    rim_rows = taps - 1

    vectors = [norm1_gain, norm2_gain, conv_w.reshape(-1), conv_bias, rgate_bias, igate_bias, decay_param]
    lengths = [v.shape[0] for v in vectors]
    flat = jnp.concatenate(vectors)
    small_rows = -(-flat.shape[0] // HW)
    flat = jnp.pad(flat, (0, small_rows * HW - flat.shape[0]))
    half_rows = chan_here * 3 // 5 // 16 * 16
    out_pieces = [(2, 0, half_rows, RING_FIRST), (2, half_rows, chan_here - half_rows, CHIP_FIRST)]
    if half_rows == 0 or chan_here % 16:
        out_pieces = [(2, 0, chan_here, RING_FIRST)]
    small_pieces = [(3, 0, small_rows, RING_FIRST), (4, 0, chan_here, RING_FIRST)]
    full_in, full_gate, full_out, flat_all, full_both, start_state = gather_call(
        net,
        (
            w_in,
            w_gate,
            w_out,
            flat.reshape(small_rows, HW),
            jnp.concatenate([w_rgate, w_igate], 1),
            initial_state,
        ),
        small_pieces
        + [(0, 0, wide_here, RING_FIRST), (1, 0, wide_here, CHIP_FIRST)]
        + out_pieces
        + [(5, 0, 1, RING_ONLY)],
    )
    full_in, full_gate = (v.reshape(width, channels) for v in (full_in, full_gate))
    full_out = full_out.reshape(channels, width)
    full_both = full_both.reshape(channels, 2 * HW)
    start_state = start_state.reshape(1, channels)
    flat_all = flat_all.reshape(devices, small_rows * HW)
    pieces, at = [], 0
    for length in lengths:
        pieces.append(flat_all[:, at : at + length])
        at += length
    full_norm1 = pieces[0].reshape(-1).astype(f32)
    full_norm2 = pieces[1].reshape(-1).astype(f32)
    conv_wf = pieces[2].reshape(devices, taps, chan_here).transpose(1, 0, 2).reshape(taps, channels).astype(f32)
    full_cbias, full_rbias, full_ibias, decay_f = (p.reshape(-1).astype(f32) for p in pieces[3:])
    gate_vectors = jnp.stack([full_rbias, full_ibias, -8.0 * jax.nn.softplus(-decay_f)], 0)
    w_ffgate, w_ffup, w_ffdown, cotangent, full_in = lax.optimization_barrier(
        (w_ffgate, w_ffup, w_ffdown, cotangent, full_in)
    )
    slab_gate, slab_up, slab_down = (
        lax.all_gather(w_ffgate, "dp", axis=0, tiled=True),
        lax.all_gather(w_ffup, "dp", axis=0, tiled=True),
        lax.all_gather(w_ffdown, "dp", axis=1, tiled=True),
    )
    cotan_rows = cotangent.reshape(rows_here, width)
    cot_flow = Flow(net.seq.gather_steps(cotan_rows))

    token_rows = inputs.reshape(rows_here, width).astype(f32)
    normed_f, scale_one, unit_one = rms_parts(token_rows, full_norm1)
    normed = normed_f.astype(bf16)
    branch = dot(normed, full_in).astype(bf16)
    branch = beside(branch, cot_flow)
    gate_pre = dot(normed, full_gate)
    reset_flags = reset.reshape(rows_here).astype(bf16)
    rim_branch, rim_flags = passed_along(
        (branch[len_here - rim_rows :], reset_flags[len_here - rim_rows :]), "seq", 1
    )
    padded = jnp.concatenate([rim_branch, branch], 0).astype(f32)
    open_pad = (1.0 - jnp.concatenate([rim_flags, reset_flags], 0).astype(f32))[:, None]
    open_masks = [None]
    conv_total = full_cbias + conv_wf[0] * rows_of(padded, rim_rows, len_here)
    running = rows_of(open_pad, rim_rows, len_here)
    for offset in range(1, rim_rows + 1):
        if offset > 1:
            running = running * rows_of(open_pad, rim_rows + 1 - offset, len_here)
        open_masks.append(running)
        conv_total = conv_total + running * conv_wf[offset] * rows_of(
            padded, rim_rows - offset, len_here
        )
    conv_low = conv_total.astype(bf16)
    reset_col = reset.astype(f32).reshape(rows_here, 1)
    conv_low, gate_pre = beside((conv_low, gate_pre), cot_flow)
    decay_rows, drive_rows = gate_call(
        gate_kernel, conv_low, full_both, gate_vectors, reset_col, (), [("rows", f32)] * 2
    )
    row_shape = jax.ShapeDtypeStruct((rows_here, channels), f32)
    states, prev_states, last_state = scan_call(
        scan_kernel,
        0,
        seq_count,
        (decay_rows, drive_rows, start_state),
        [row_shape, row_shape, jax.ShapeDtypeStruct((1, channels), f32)],
    )
    states = beside(states, cot_flow)
    final_here = initial_state.shape[1]
    final_state = lax.dynamic_slice_in_dim(
        last_state, lax.axis_index("seq") * final_here, final_here, 1
    )
    state_f = states.astype(bf16).astype(f32)
    gate_act, gate_back = jax.vjp(gelu_tanh, gate_pre)
    mixed_rows = (state_f * gate_act).astype(bf16)
    residual = token_rows + dot(mixed_rows, full_out)

    slots = pair_slots(seq_count)
    cot_blocks = cot_flow.finish()
    cots = [cotan_rows] + [cot_blocks[k] for k in slots[:-2]] + cot_blocks[seq_count // 2]
    normed_two_f, scale_two, unit_two = rms_parts(residual, full_norm2)
    normed_two = normed_two_f.astype(bf16)
    group_normed, group_cotan, hidden, d_ffgate, d_ffup, out_part, d_normed_part = ff_call(
        net.order, normed_two, cots, slab_gate, slab_up, slab_down
    )
    group_rows = seq_count * rows_here
    group_normed = group_normed.reshape(group_rows, width)
    group_cotan = group_cotan.reshape(group_rows, width)
    hidden, d_ffgate, d_ffup = (v.reshape(group_rows, -1) for v in (hidden, d_ffgate, d_ffup))

    def block_rows(whole):
        whole = whole.reshape(seq_count, rows_here, width)
        return lambda k: whole[slots.index(k)]

    d_normed_flow = Flow(net.seq.scatter_steps(block_rows(d_normed_part)))
    gate_part = beside(t_dot(group_normed, d_ffgate).astype(bf16), d_normed_flow)
    up_part = beside(t_dot(group_normed, d_ffup).astype(bf16), d_normed_flow)
    down_part = beside(t_dot(hidden, group_cotan).astype(bf16), d_normed_flow)
    d_normed_sum = d_normed_flow.finish()
    d_normed_sum, out_part, gate_part, up_part, down_part = lax.optimization_barrier(
        (d_normed_sum, out_part, gate_part, up_part, down_part)
    )
    d_normed_two = d_normed_sum
    out_flow = Flow(net.seq.scatter_steps(block_rows(out_part)))
    grad_ffgate, grad_ffup, grad_ffdown = (
        lax.psum_scatter(part, "dp", scatter_dimension=axis, tiled=True).astype(f32)
        for part, axis in ((gate_part, 0), (up_part, 0), (down_part, 1))
    )

    grad_norm2, d_resid_norm = norm_back(d_normed_two, full_norm2, scale_two, unit_two)
    d_residual = cotan_rows.astype(f32) + d_resid_norm
    d_residual_low = d_residual.astype(bf16)
    d_mixed = dot_t(d_residual_low, full_out)
    d_state = (d_mixed * gate_act).astype(bf16)
    d_gate_pre = gate_back(d_mixed * state_f)[0].astype(bf16)
    d_state, d_gate_pre = beside((d_state, d_gate_pre), out_flow)

    def grad_terms(left, right):
        return t_dot(left, right).astype(bf16).reshape(dp_count, seq_count, -1, right.shape[1])

    gate_terms = grad_terms(normed, d_gate_pre)
    d_drive, d_decay = scan_call(
        scan_back_kernel,
        1,
        seq_count,
        (decay_rows, d_state.astype(f32), prev_states),
        [row_shape, row_shape],
    )
    d_drive, d_decay, gate_terms = beside((d_drive, d_decay, gate_terms), out_flow)
    out_terms = grad_terms(mixed_rows, d_residual_low)
    d_conv_low, both_terms, gate_sums = gate_call(
        gate_back_kernel,
        conv_low,
        full_both,
        gate_vectors,
        reset_col,
        (d_decay, d_drive),
        [("rows", bf16), ("weights", bf16), ("sums", f32)],
    )
    d_conv_low, out_terms = beside((d_conv_low, out_terms), out_flow)
    grad_rbias, grad_ibias, rate_sum, grad_cbias = gate_sums
    grad_decay = 8.0 * jax.nn.sigmoid(-decay_f) * rate_sum
    rim_grad, rim_next = passed_along((d_conv_low[:rim_rows], reset_flags[:rim_rows]), "seq", -1)
    grad_ext = jnp.concatenate([d_conv_low, rim_grad], 0).astype(f32)
    open_next = (1.0 - jnp.concatenate([reset_flags, rim_next], 0).astype(f32))[:, None]
    d_conv_f = rows_of(grad_ext, 0, len_here)
    d_branch = conv_wf[0] * d_conv_f
    ahead = None
    conv_grads = [jnp.sum(rows_of(padded, rim_rows, len_here) * d_conv_f, axis=0)]
    for offset in range(1, rim_rows + 1):
        step_open = rows_of(open_next, offset, len_here)
        ahead = step_open if offset == 1 else ahead * step_open
        d_branch = d_branch + ahead * conv_wf[offset] * rows_of(grad_ext, offset, len_here)
        conv_grads.append(
            jnp.sum(
                open_masks[offset] * rows_of(padded, rim_rows - offset, len_here) * d_conv_f,
                axis=0,
            )
        )
    grad_conv = jnp.stack(conv_grads, 0)
    d_branch_low = d_branch.astype(bf16)
    in_terms = grad_terms(normed, d_branch_low)
    d_normed_one = dot_t(d_branch_low, full_in) + dot_t(d_gate_pre, full_gate)
    grad_norm1, d_token_norm = norm_back(d_normed_one, full_norm1, scale_one, unit_one)
    input_grad = (d_residual + d_token_norm).reshape(seqs_here, len_here, width)

    grad_norm1, input_grad = beside((grad_norm1, input_grad), out_flow)
    ff_out = out_flow.finish()
    output = (residual + ff_out).astype(bf16).reshape(seqs_here, len_here, width)

    conv_flat = grad_conv.reshape(taps, devices, chan_here).transpose(1, 0, 2)
    flat_grads = jnp.concatenate(
        [
            v.reshape(devices, -1)
            for v in (grad_norm1, grad_norm2, conv_flat, grad_cbias, grad_rbias, grad_ibias, grad_decay)
        ],
        1,
    )
    flat_grads = jnp.pad(flat_grads, ((0, 0), (0, small_rows * HW - flat_grads.shape[1])))
    flat_terms = flat_grads.astype(bf16).reshape(dp_count, seq_count, small_rows, HW)
    turned = [(i, first, rows, RING_FIRST + CHIP_FIRST - way) for i, first, rows, way in out_pieces]
    grad_in, grad_gate, grad_out, flat_mine, both_mine = reduce_call(
        net,
        [
            in_terms,
            gate_terms,
            out_terms,
            flat_terms,
            both_terms.reshape(dp_count, seq_count, chan_here, 2 * HW),
        ],
        [(1, 0, wide_here, RING_FIRST)]
        + turned
        + [(3, 0, small_rows, CHIP_FIRST), (4, 0, chan_here, CHIP_FIRST), (0, 0, wide_here, CHIP_FIRST)],
    )
    flat_mine = flat_mine.reshape(-1)
    mine, at = [], 0
    for length in lengths:
        mine.append(flat_mine[at : at + length])
        at += length
    return (
        output,
        input_grad,
        final_state,
        mine[0],
        grad_gate,
        grad_in,
        mine[2].reshape(taps, chan_here),
        mine[3],
        both_mine[:, :HW],
        mine[4],
        both_mine[:, HW:],
        mine[5],
        mine[6],
        grad_out,
        mine[1],
        grad_ffgate,
        grad_ffup,
        grad_ffdown,
    )


def solution(mesh):
    split = ("dp", "seq")
    return jax.shard_map(
        per_device,
        mesh=mesh,
        in_specs=(
            P("dp", "seq", None),
            P("dp", "seq"),
            P("dp", "seq"),
            P("dp", "seq", None),
            P(split),
            P(split, None),
            P(split, None),
            P(None, split),
            P(split),
            P(split, None),
            P(split),
            P(split, None),
            P(split),
            P(split),
            P(split, None),
            P(split),
            P("dp", "seq"),
            P("dp", "seq"),
            P("seq", "dp"),
        ),
        out_specs=(
            P("dp", "seq", None),
            P("dp", "seq", None),
            P("dp", "seq"),
            P(split),
            P(split, None),
            P(split, None),
            P(None, split),
            P(split),
            P(split, None),
            P(split),
            P(split, None),
            P(split),
            P(split),
            P(split, None),
            P(split),
            P("dp", "seq"),
            P("dp", "seq"),
            P("seq", "dp"),
        ),
        check_vma=False,
    )
```

```python
import functools

import jax
import jax.numpy as jnp
from jax import lax
from jax.experimental import pallas as pl
from jax.experimental.pallas import tpu as pltpu
from jax.sharding import PartitionSpec as P

HW = 256
LANES = 8
LINE = 128


epsilon = 1e-06
floor_value = 0.0001
f32 = jnp.float32
bf16 = jnp.bfloat16


def seq_order(count):
    if count % 8:
        return list(range(count))
    wide = count // 4
    path = []
    for z in range(4):
        ys = range(1, wide) if z % 2 == 0 else range(wide - 1, 0, -1)
        path += [z * wide + y for y in ys]
    return path + [z * wide for z in (3, 2, 1, 0)]


class Ring:
    def __init__(self, axis, cycles):
        self.axis = axis
        self.cycles = cycles
        self.count = len(cycles[0])

    def shift(self, value, step):
        pairs = [
            (cycle[i], cycle[(i + step) % self.count])
            for cycle in self.cycles
            for i in range(self.count)
        ]
        return lax.ppermute(value, self.axis, pairs)

    def place(self):
        table = [0] * (self.count * len(self.cycles))
        for cycle in self.cycles:
            for i, device in enumerate(cycle):
                table[device] = i
        return jnp.asarray(table, jnp.int32)[lax.axis_index(self.axis)]

    def gather_steps(self, value):
        count, half = self.count, self.count // 2
        blocks = [value] * count
        if count == 1:
            return blocks
        ahead = behind = value
        for step in range(1, half):
            behind, ahead = yield [self.shift(behind, 1), self.shift(ahead, -1)]
            blocks[count - step] = behind
            blocks[step] = ahead
        rows = value.shape[0]
        if half > 1 and rows % 32 == 0:
            top, bottom = yield [
                self.shift(behind[: rows // 2], 1),
                self.shift(ahead[rows // 2 :], -1),
            ]
            blocks[half] = [top, bottom]
        else:
            blocks[half] = yield [self.shift(behind, 1)]
        return blocks

    def scatter_steps(self, part):
        count, half = self.count, self.count // 2
        if count == 1:
            return part(0).astype(f32)
        far = part(half).astype(bf16)
        if half == 1:
            (got,) = yield [self.shift(far, 1)]
            return part(0).astype(f32) + got.astype(f32)
        rows = far.shape[0]
        assert rows % 2 == 0
        cut = rows // 2
        ahead, behind = far[:cut], far[cut:]
        for k in range(half - 1, -1, -1):
            got_ahead, got_behind = yield [self.shift(ahead, 1), self.shift(behind, -1)]
            got_ahead, got_behind = got_ahead.astype(f32), got_behind.astype(f32)
            if k == 0:
                return part(0).astype(f32) + got_ahead + got_behind
            ahead, behind = part(k).astype(f32), part(count - k).astype(f32)
            if k == half - 1:
                ahead = jnp.concatenate([ahead[:cut] + got_ahead, ahead[cut:]], 0)
                behind = jnp.concatenate([behind[:cut], behind[cut:] + got_behind], 0)
            else:
                ahead, behind = ahead + got_ahead, behind + got_behind
            ahead, behind = ahead.astype(bf16), behind.astype(bf16)


class Flow:
    def __init__(self, steps):
        self.steps, self.pending, self.result = steps, [], None
        self.advance(None)

    def advance(self, arrived):
        try:
            self.pending = self.steps.send(arrived)
        except StopIteration as stop:
            self.pending, self.result = [], stop.value

    def finish(self):
        while self.pending:
            self.advance(self.pending)
        return self.result


def beside(values, *flows):
    values, arrived = lax.optimization_barrier((values, [flow.pending for flow in flows]))
    for flow, got in zip(flows, arrived):
        if got:
            flow.advance(got)
    return values


class Net:
    def __init__(self):
        self.seq_count = lax.axis_size("seq")
        self.dp_count = lax.axis_size("dp")
        self.order = seq_order(self.seq_count)
        self.seq = Ring("seq", [self.order])
        self.cores = 2 if self.dp_count % 2 == 0 else 1
        self.chips = self.dp_count // self.cores


def lookup(table, index):
    value = jnp.int32(table[0])
    for i, entry in enumerate(table):
        value = jnp.where(index == i, jnp.int32(entry), value)
    return value


class Links:
    def __init__(self, order, chips, cores):
        self.count, self.chips, self.cores = len(order), chips, cores
        me, dp = lax.axis_index("seq"), lax.axis_index("dp")
        count = self.count
        place = [0] * count
        for i, device in enumerate(order):
            place[device] = i
        self.seq_at = [
            lookup([order[(place[d] + k) % count] for d in range(count)], me) for k in range(count)
        ]
        self.ring = ({"seq": self.seq_at[1]}, {"seq": self.seq_at[count - 1]})
        chip, core = dp // cores, dp % cores
        self.chip = [
            {"dp": lax.rem(chip + step, chips) * cores + core} for step in range(1, chips)
        ]
        self.core = {"dp": chip * cores + (1 - core)} if cores == 2 else None
        self.dp_at = [
            lax.rem(chip + k, chips) * cores + lax.rem(core + c, cores)
            for c in range(cores)
            for k in range(chips)
        ]

    def greet(self):
        barrier = pltpu.get_barrier_semaphore()
        peers = list(self.ring) + self.chip + ([self.core] if self.cores == 2 else [])
        for peer in peers:
            pl.semaphore_signal(
                barrier, inc=1, device_id=peer, device_id_type=pl.DeviceIdType.MESH
            )
        pl.semaphore_wait(barrier, len(peers))


def remote(source, target, send_sem, recv_sem, peer):
    return pltpu.make_async_remote_copy(
        src_ref=source,
        dst_ref=target,
        send_sem=send_sem,
        recv_sem=recv_sem,
        device_id=peer,
        device_id_type=pl.DeviceIdType.MESH,
    )


RING_FIRST, CHIP_FIRST, RING_ONLY = 0, 1, 2


def ring_sends(way, chips, half):
    return {RING_FIRST: half + chips - 1, CHIP_FIRST: chips * half, RING_ONLY: half}[way]


def gather_kernel(order, chips, cores, pieces, arrays, *refs):
    ins, outs = refs[:arrays], refs[arrays : 2 * arrays]
    own_sem, recv_sem, ring_sem, chip_sem, core_sem = refs[2 * arrays :]
    links = Links(order, chips, cores)
    count, half = links.count, links.count // 2
    links.greet()
    method = [piece[3] for piece in pieces]
    only_ring = {piece[0] for piece in pieces if piece[3] == RING_ONLY}

    spans = [1 if way == RING_ONLY else chips * cores for way in method]
    sharing = [p for p in range(len(pieces)) if method[p] != RING_ONLY]

    def landed(p, r, k):
        return recv_sem.at[sum(spans[:p]) + r, k]

    def ring_slot(p, r, side, s):
        at = sum(ring_sends(way, chips, half) for way in method[:p])
        if method[p] == CHIP_FIRST or r == 0:
            at += r * half + s
        else:
            at += half + r - 1
        return ring_sem.at[at, side]

    def slot(i, r, k):
        return outs[i].at[0 if i in only_ring else links.dp_at[r], links.seq_at[k]]

    owns = [
        pltpu.make_async_copy(ins[i], slot(i, 0, 0), own_sem.at[i])
        for i in range(arrays)
    ]
    for copy in owns:
        copy.start()
    sent = []

    def whole(p, r, k):
        array, first, rows, _ = pieces[p]
        place = slot(array, r, k)
        return place if rows == ins[array].shape[0] else place.at[pl.ds(first, rows)]

    def rows_in(p, r, k, first, rows):
        return slot(pieces[p][0], r, k).at[pl.ds(pieces[p][1] + first, rows)]

    def held(p, r, k):
        array, first, rows, _ = pieces[p]
        if r == 0 and k == 0:
            return ins[array] if rows == ins[array].shape[0] else ins[array].at[pl.ds(first, rows)]
        return whole(p, r, k)

    def cut_of(p):
        return pieces[p][2] // 32 * 16

    def start(copy):
        copy.start()
        sent.append(copy)

    def ring_copies(p, r, s):
        cut, rows = cut_of(p), pieces[p][2]
        if s < half - 1:
            return [
                remote(
                    held(p, r, (count - s) % count), whole(p, r, (count - s) % count),
                    ring_slot(p, r, 0, s), landed(p, r, count - s - 1), links.ring[0],
                ),
                remote(
                    held(p, r, s), whole(p, r, s),
                    ring_slot(p, r, 1, s), landed(p, r, s + 1), links.ring[1],
                ),
            ]
        back = count - s
        if not cut:
            return [
                remote(
                    whole(p, r, back), whole(p, r, back),
                    ring_slot(p, r, 0, s), landed(p, r, half), links.ring[0],
                )
            ]
        top, bottom = rows_in(p, r, back, 0, cut), rows_in(p, r, s, cut, rows - cut)
        return [
            remote(top, top, ring_slot(p, r, 0, s), landed(p, r, half), links.ring[0]),
            remote(
                bottom, bottom, ring_slot(p, r, 1, s), landed(p, r, count), links.ring[1]
            ),
        ]

    def arrived(p, r, k):
        cut, rows = cut_of(p), pieces[p][2]
        if k == half and cut:
            for part, sem in (((0, cut), half), ((cut, rows - cut), count)):
                ref = rows_in(p, r, k, *part)
                remote(ref, ref, ring_slot(p, 0, 0, 0), landed(p, r, sem), links.ring[0]).wait_recv()
        else:
            ref = whole(p, r, k)
            remote(ref, ref, ring_slot(p, 0, 0, 0), landed(p, r, k), links.ring[0]).wait_recv()

    def to_chips(p, k):
        for step in range(1, chips):
            start(
                remote(
                    held(p, 0, k), whole(p, 0, k),
                    chip_sem.at[sharing.index(p), step - 1, k], landed(p, chips - step, k), links.chip[step - 1],
                )
            )

    def to_core(p, r, k):
        if cores == 2:
            start(
                remote(
                    held(p, r, k), whole(p, r, k),
                    core_sem.at[sharing.index(p), r, k], landed(p, chips + r, k), links.core,
                )
            )

    everyone = range(len(pieces))

    def planes(p):
        return range(chips) if method[p] == CHIP_FIRST else range(1)

    for p in everyone:
        if method[p] != RING_ONLY:
            to_chips(p, 0)
        for copy in ring_copies(p, 0, 0):
            start(copy)
    for p in everyone:
        if method[p] != RING_ONLY:
            to_core(p, 0, 0)
    for s in range(1, half + 1):
        steps = sorted({count - s, s})
        before = sorted({(count - s + 1) % count, s - 1})
        for p in everyone:
            for r in planes(p):
                if r == 0 or s > 1:
                    for k in steps:
                        arrived(p, r, k)
                    if s < half:
                        for copy in ring_copies(p, r, s):
                            start(copy)
                    if method[p] == RING_FIRST and s < half:
                        for k in steps:
                            to_chips(p, k)
                    if method[p] != RING_ONLY:
                        for k in steps:
                            to_core(p, r, k)
        for p in everyone:
            if method[p] == RING_FIRST:
                for r in range(1, chips):
                    for k in before:
                        arrived_from_chip(links, whole(p, r, k), chip_sem.at[sharing.index(p), 0, 0], landed(p, r, k))
                        to_core(p, r, k)
                    if s == half:
                        for copy in ring_copies(p, r, half - 1):
                            start(copy)
            if method[p] == CHIP_FIRST and s == 1:
                for r in range(1, chips):
                    arrived_from_chip(links, whole(p, r, 0), chip_sem.at[sharing.index(p), 0, 0], landed(p, r, 0))
                    for copy in ring_copies(p, r, 0):
                        start(copy)
                    to_core(p, r, 0)
                for r in range(1, chips):
                    for k in steps:
                        arrived(p, r, k)
                    if s < half:
                        for copy in ring_copies(p, r, s):
                            start(copy)
                    for k in steps:
                        to_core(p, r, k)
    for p in everyone:
        if method[p] == RING_FIRST:
            for r in range(1, chips):
                arrived(p, r, half)
                to_core(p, r, half)
    for p in everyone:
        if method[p] != RING_ONLY and cores == 2:
            for r in range(chips):
                for k in range(count):
                    arrived_from_chip(
                        links, whole(p, chips + r, k), core_sem.at[sharing.index(p), r, k], landed(p, chips + r, k)
                    )
    for copy in sent:
        copy.wait_send()
    for copy in owns:
        copy.wait()


def arrived_from_chip(links, ref, send_sem, recv_sem):
    remote(ref, ref, send_sem, recv_sem, links.ring[0]).wait_recv()


def gather_call(net, arrays, pieces):
    chips, cores, count = net.chips, net.cores, net.seq_count
    slots = chips * cores
    only_ring = {piece[0] for piece in pieces if piece[3] == RING_ONLY}
    shared = sum(piece[3] != RING_ONLY for piece in pieces)
    anywhere = pl.BlockSpec(memory_space=pl.ANY)
    return pl.pallas_call(
        functools.partial(gather_kernel, net.order, chips, cores, pieces, len(arrays)),
        out_shape=[
            jax.ShapeDtypeStruct((1 if i in only_ring else slots, count) + v.shape, v.dtype)
            for i, v in enumerate(arrays)
        ],
        in_specs=[anywhere] * len(arrays),
        out_specs=[anywhere] * len(arrays),
        scratch_shapes=[
            pltpu.SemaphoreType.DMA((len(arrays),)),
            pltpu.SemaphoreType.DMA(
                (sum(1 if piece[3] == RING_ONLY else slots for piece in pieces), count + 1)
            ),
            pltpu.SemaphoreType.DMA(
                (sum(ring_sends(piece[3], chips, count // 2) for piece in pieces), 2)
            ),
            pltpu.SemaphoreType.DMA((shared, max(chips - 1, 1), count)),
            pltpu.SemaphoreType.DMA((shared, chips, count)),
        ],
        compiler_params=pltpu.CompilerParams(
            collective_id=3, has_side_effects=True, vmem_limit_bytes=60 * 2**20
        ),
        cost_estimate=pl.CostEstimate(
            flops=0, bytes_accessed=slots * count * sum(v.size for v in arrays) * 4, transcendentals=0
        ),
    )(*arrays)


def add_rows(target, terms, rows):
    if rows % 16:
        target[...] = total([term[...].astype(f32) for term in terms]).astype(target.dtype)
        return

    def body(t, carry):
        at = pl.ds(pl.multiple_of(t * 16, 16), 16)
        target[at] = total([term[at].astype(f32) for term in terms]).astype(target.dtype)
        return carry

    lax.fori_loop(0, rows // 16, body, 0)


def total(terms):
    result = terms[0]
    for term in terms[1:]:
        result = result + term
    return result


def reduce_kernel(order, chips, cores, pieces, arrays, *refs):
    count, half = len(order), len(order) // 2
    parts, refs = refs[:arrays], refs[arrays:]
    outs, refs = refs[:arrays], refs[arrays:]
    mine, refs = refs[:arrays], refs[arrays:]
    other, refs = refs[:arrays], refs[arrays:]
    chip_in, refs = refs[: len(pieces)], refs[len(pieces) :]
    ring_in, refs = refs[: len(pieces)], refs[len(pieces) :]
    load_sem, core_send, core_recv, chip_send, chip_recv, ring_send, ring_recv = refs
    links = Links(order, chips, cores)
    everyone = range(len(pieces))
    method = [piece[3] for piece in pieces]

    loads = [
        [
            pltpu.make_async_copy(parts[i].at[links.dp_at[k]], mine[i].at[k], load_sem.at[i, k])
            for k in range(chips)
        ]
        for i in range(arrays)
    ]
    for copies in loads:
        for copy in copies:
            copy.start()
    links.greet()
    sent = []

    def start(copy):
        copy.start()
        sent.append(copy)

    def rows_of_piece(ref, p, first=0, rows=None):
        array, start_row, piece_rows, _ = pieces[p]
        rows = piece_rows if rows is None else rows
        if rows == ref.shape[0]:
            return ref
        return ref.at[pl.ds(start_row + first, rows)]

    def held(p, k, q):
        return rows_of_piece(mine[pieces[p][0]].at[k, links.seq_at[q]], p)

    def core_copy(p, k, q):
        array = pieces[p][0]
        return remote(
            rows_of_piece(parts[array].at[links.dp_at[chips + k], links.seq_at[q]], p),
            rows_of_piece(other[array].at[k, links.seq_at[q]], p),
            core_send.at[p, k, q], core_recv.at[p, k, q], links.core,
        )

    def steps(d):
        return sorted({d % count, (count - d) % count})

    def planes(p):
        return range(chips) if method[p] == RING_FIRST else range(1)

    if cores == 2:
        for d in range(half, -1, -1):
            for p in everyone:
                for k in reversed(range(chips)):
                    for q in steps(d):
                        start(core_copy(p, k, q))

    loaded = set()

    def core_sum(p, k, q):
        array = pieces[p][0]
        if (array, k) not in loaded:
            loaded.add((array, k))
            loads[array][k].wait()
        if cores == 2:
            core_copy(p, k, q).wait_recv()
            theirs = rows_of_piece(other[array].at[k, links.seq_at[q]], p)
            add_rows(held(p, k, q), [held(p, k, q), theirs], pieces[p][2])

    def chip_copy(p, k, q):
        if method[p] == CHIP_FIRST:
            target = chip_in[p].at[k - 1, links.seq_at[q]]
        else:
            target = chip_in[p].at[k - 1]
        return remote(
            held(p, k, q), target, chip_send.at[p, k - 1, q], chip_recv.at[p, k - 1, q], links.chip[k - 1]
        )

    def chip_sum(p, q):
        for k in range(1, chips):
            chip_copy(p, k, q).wait_recv()
            if method[p] == CHIP_FIRST:
                add_rows(held(p, 0, q), [held(p, 0, q), chip_in[p].at[k - 1, links.seq_at[q]]], pieces[p][2])
            else:
                out = rows_of_piece(outs[pieces[p][0]], p)
                add_rows(out, [out, chip_in[p].at[k - 1]], pieces[p][2])

    def span(p, side, d):
        rows = pieces[p][2]
        cut = rows // 32 * 16
        if d < half:
            return (0, rows)
        if not cut:
            return (0, rows) if side == 0 else None
        return (0, cut) if side == 0 else (cut, rows - cut)

    def ring_copy(p, k, side, d):
        first, rows = span(p, side, d)
        q = d if side == 0 else (count - d) % count
        source = held(p, k, q)
        target = ring_in[p].at[k, side, d - 1]
        if rows != pieces[p][2]:
            source, target = source.at[pl.ds(first, rows)], target.at[pl.ds(first, rows)]
        return remote(
            source, target, ring_send.at[p, k, side, d - 1], ring_recv.at[p, k, side, d - 1], links.ring[side]
        )

    def ring_step(p, k, d):
        if d == 0:
            got = []
            for side in range(2):
                if half > 1 or span(p, side, 1):
                    ring_copy(p, k, side, 1).wait_recv()
                    got.append(ring_in[p].at[k, side, 0])
            target = rows_of_piece(outs[pieces[p][0]], p) if k == 0 else held(p, k, 0)
            add_rows(target, [held(p, k, 0)] + got, pieces[p][2])
            return
        for side in range(2):
            if span(p, side, d) is None:
                continue
            if d < half and span(p, side, d + 1) is not None:
                ring_copy(p, k, side, d + 1).wait_recv()
                first, rows = span(p, side, d + 1)
                target = held(p, k, d if side == 0 else count - d)
                term = ring_in[p].at[k, side, d]
                if rows != pieces[p][2]:
                    target, term = target.at[pl.ds(first, rows)], term.at[pl.ds(first, rows)]
                add_rows(target, [target, term], rows)
            start(ring_copy(p, k, side, d))

    for d in range(half, -1, -1):
        for p in everyone:
            if method[p] == RING_FIRST:
                for k in reversed(planes(p)):
                    for q in steps(d):
                        core_sum(p, k, q)
                    ring_step(p, k, d)
                    if d == 0 and k > 0:
                        start(chip_copy(p, k, 0))
        for p in everyone:
            if method[p] == CHIP_FIRST:
                for q in steps(d):
                    for k in reversed(range(chips)):
                        core_sum(p, k, q)
                        if k > 0:
                            start(chip_copy(p, k, q))
        for p in everyone:
            if method[p] == CHIP_FIRST and d < half:
                for q in steps(d + 1):
                    chip_sum(p, q)
                ring_step(p, 0, d + 1)
    for p in everyone:
        if method[p] == CHIP_FIRST:
            chip_sum(p, 0)
            ring_step(p, 0, 0)
    for p in everyone:
        if method[p] == RING_FIRST:
            chip_sum(p, 0)
    for copy in sent:
        copy.wait_send()


def reduce_call(net, arrays, pieces):
    chips, cores, count = net.chips, net.cores, net.seq_count
    half = count // 2
    anywhere = pl.BlockSpec(memory_space=pl.ANY)
    shapes = [terms.shape[2:] for terms in arrays]
    ahead = max(chips - 1, 1)
    blocks = [(piece[2], shapes[piece[0]][1]) for piece in pieces]
    chip_shapes = [
        (ahead, count) + block if piece[3] == CHIP_FIRST else (ahead,) + block
        for piece, block in zip(pieces, blocks)
    ]
    ring_shapes = [
        (chips if piece[3] == RING_FIRST else 1, 2, half) + block
        for piece, block in zip(pieces, blocks)
    ]
    n = len(pieces)
    return pl.pallas_call(
        functools.partial(reduce_kernel, net.order, chips, cores, pieces, len(arrays)),
        out_shape=[jax.ShapeDtypeStruct(shape, f32) for shape in shapes],
        in_specs=[anywhere] * len(arrays),
        out_specs=[pl.BlockSpec(memory_space=pltpu.VMEM)] * len(arrays),
        scratch_shapes=[pltpu.VMEM((chips, count) + shape, bf16) for shape in shapes]
        + [pltpu.VMEM((chips, count) + shape, bf16) for shape in shapes]
        + [pltpu.VMEM(shape, bf16) for shape in chip_shapes]
        + [pltpu.VMEM(shape, bf16) for shape in ring_shapes]
        + [
            pltpu.SemaphoreType.DMA((len(arrays), chips)),
            pltpu.SemaphoreType.DMA((n, chips, count)),
            pltpu.SemaphoreType.DMA((n, chips, count)),
            pltpu.SemaphoreType.DMA((n, ahead, count)),
            pltpu.SemaphoreType.DMA((n, ahead, count)),
            pltpu.SemaphoreType.DMA((n, chips, 2, half)),
            pltpu.SemaphoreType.DMA((n, chips, 2, half)),
        ],
        compiler_params=pltpu.CompilerParams(
            collective_id=4, has_side_effects=True, vmem_limit_bytes=63 * 2**20
        ),
        cost_estimate=pl.CostEstimate(
            flops=0, bytes_accessed=sum(terms.size for terms in arrays) * 4, transcendentals=0
        ),
    )(*arrays)


def exchange(totals, everyone, send_sem, recv_sem, count):
    me = lax.axis_index("seq")
    everyone[me] = totals[...]
    copies = []
    for step in range(1, count):
        peer = lax.rem(me + step, count)
        copy = pltpu.make_async_remote_copy(
            src_ref=totals,
            dst_ref=everyone.at[me],
            send_sem=send_sem.at[step],
            recv_sem=recv_sem.at[step],
            device_id={"seq": peer},
            device_id_type=pl.DeviceIdType.MESH,
        )
        copy.start()
    for step in range(1, count):
        source = lax.rem(me + count - step, count)
        copy = pltpu.make_async_remote_copy(
            src_ref=totals,
            dst_ref=everyone.at[source],
            send_sem=send_sem.at[step],
            recv_sem=recv_sem.at[step],
            device_id={"seq": source},
            device_id_type=pl.DeviceIdType.MESH,
        )
        copy.wait()


def greet(count):
    me = lax.axis_index("seq")
    barrier = pltpu.get_barrier_semaphore()
    for step in range(1, count):
        pl.semaphore_signal(
            barrier,
            inc=1,
            device_id={"seq": lax.rem(me + step, count)},
            device_id_type=pl.DeviceIdType.MESH,
        )
    pl.semaphore_wait(barrier, count - 1)


def tiles(channels):
    wide = 512 if channels % 512 == 0 else 128
    return [pl.ds(at, wide) for at in range(0, channels, wide)]


def tile_prefix(product, total, step):
    row = lax.broadcasted_iota(jnp.int32, product.shape, 0)
    reach = 1
    while reach < LANES:
        turn = reach if step > 0 else LANES - reach
        inside = row >= reach if step > 0 else row < LANES - reach
        total = total + product * jnp.where(inside, pltpu.roll(total, turn, 0), 0.0)
        product = product * jnp.where(inside, pltpu.roll(product, turn, 0), 1.0)
        reach *= 2
    return (product, total)


def scan_kernel(
    count, decay_ref, drive_ref, start_ref, state_ref, prev_ref, last_ref,
    totals, everyone, send_sem, recv_sem,
):
    greet(count)
    rows, channels = decay_ref.shape
    end = LANES - 1
    for cols in tiles(channels):

        def first_pass(t, carry):
            run_product, run_sum = carry
            at = pl.ds(pl.multiple_of(t * LANES, LANES), LANES)
            product, total = tile_prefix(decay_ref[at, cols], drive_ref[at, cols], 1)
            prev_ref[at, cols] = product
            state_ref[at, cols] = total
            last = product[end:]
            return (last * run_product, last * run_sum + total[end:])

        zero = jnp.zeros((1, cols.size), f32)
        run_product, run_sum = lax.fori_loop(
            0, rows // LANES, first_pass, (zero + 1.0, zero), unroll=4
        )
        totals[0:1, cols] = run_product
        totals[1:2, cols] = run_sum
    exchange(totals, everyone, send_sem, recv_sem, count)
    me = lax.axis_index("seq")
    for cols in tiles(channels):
        state = start_ref[0:1, cols]
        entering = state
        for device in range(count):
            entering = jnp.where(me == device, state, entering)
            state = everyone[device, 0:1, cols] * state + everyone[device, 1:2, cols]
        last_ref[0:1, cols] = state

        def second_pass(t, entry):
            at = pl.ds(pl.multiple_of(t * LANES, LANES), LANES)
            state = prev_ref[at, cols] * entry + state_ref[at, cols]
            row = lax.broadcasted_iota(jnp.int32, state.shape, 0)
            state_ref[at, cols] = state
            prev_ref[at, cols] = jnp.where(row == 0, entry, pltpu.roll(state, 1, 0))
            return state[end:]

        lax.fori_loop(0, rows // LANES, second_pass, entering, unroll=4)


def scan_back_kernel(
    count, decay_ref, d_state_ref, prev_ref, d_drive_ref, d_decay_ref,
    totals, everyone, send_sem, recv_sem,
):
    greet(count)
    rows, channels = decay_ref.shape
    last_tile = rows // LANES - 1
    end = LANES - 1
    for cols in tiles(channels):

        def first_pass(i, carry):
            run_product, run_sum = carry
            at = pl.ds(pl.multiple_of((last_tile - i) * LANES, LANES), LANES)
            decay = decay_ref[at, cols]
            product, total = tile_prefix(decay, decay * d_state_ref[at, cols], -1)
            d_decay_ref[at, cols] = product
            d_drive_ref[at, cols] = total
            first = product[:1]
            return (first * run_product, first * run_sum + total[:1])

        zero = jnp.zeros((1, cols.size), f32)
        run_product, run_sum = lax.fori_loop(
            0, rows // LANES, first_pass, (zero + 1.0, zero), unroll=4
        )
        totals[0:1, cols] = run_product
        totals[1:2, cols] = run_sum
    exchange(totals, everyone, send_sem, recv_sem, count)
    me = lax.axis_index("seq")
    for cols in tiles(channels):
        state = jnp.zeros((1, cols.size), f32)
        entering = state
        for device in reversed(range(count)):
            entering = jnp.where(me == device, state, entering)
            state = everyone[device, 0:1, cols] * state + everyone[device, 1:2, cols]

        def second_pass(i, entry):
            at = pl.ds(pl.multiple_of((last_tile - i) * LANES, LANES), LANES)
            outgoing = d_decay_ref[at, cols] * entry + d_drive_ref[at, cols]
            row = lax.broadcasted_iota(jnp.int32, outgoing.shape, 0)
            incoming = jnp.where(row == end, entry, pltpu.roll(outgoing, end, 0))
            carry = d_state_ref[at, cols] + incoming
            d_drive_ref[at, cols] = carry
            d_decay_ref[at, cols] = carry * prev_ref[at, cols]
            return outgoing[:1]

        lax.fori_loop(0, rows // LANES, second_pass, entering, unroll=4)


def scan_call(kernel, collective_id, count, operands, out_shapes):
    channels = operands[0].shape[1]
    vmem = pl.BlockSpec(memory_space=pltpu.VMEM)
    return pl.pallas_call(
        functools.partial(kernel, count),
        out_shape=out_shapes,
        in_specs=[vmem] * len(operands),
        out_specs=[vmem] * len(out_shapes),
        scratch_shapes=[
            pltpu.VMEM((2, channels), f32),
            pltpu.VMEM((count, 2, channels), f32),
            pltpu.SemaphoreType.DMA((count,)),
            pltpu.SemaphoreType.DMA((count,)),
        ],
        compiler_params=pltpu.CompilerParams(
            collective_id=collective_id, has_side_effects=True, vmem_limit_bytes=40 * 2**20
        ),
        cost_estimate=pl.CostEstimate(
            flops=8 * operands[0].size, bytes_accessed=20 * operands[0].size, transcendentals=0
        ),
    )(*operands)


def gate_parts(conv_ref, both_ref, vectors_ref, reset_ref):
    conv = conv_ref[...].astype(f32)
    pre = contract(conv_ref[...], both_ref[...], 1, 0)
    rate = jax.nn.sigmoid(pre[:, :HW] + vectors_ref[0:1])
    in_gate = jax.nn.sigmoid(pre[:, HW:] + vectors_ref[1:2])
    log_decay = vectors_ref[2:3] * rate
    reset = reset_ref[...]
    keep = 1.0 - reset
    decay = jnp.exp(log_decay)
    bend = jnp.tanh(-log_decay)
    power = 2.0 * bend / (1.0 + bend)
    root = jnp.sqrt(jnp.maximum(power, floor_value))
    return conv, rate, in_gate, decay, keep, power, root, reset + keep * root


def gate_kernel(conv_ref, both_ref, vectors_ref, reset_ref, decay_ref, drive_ref):
    conv, _, in_gate, decay, keep, _, _, share = gate_parts(
        conv_ref, both_ref, vectors_ref, reset_ref
    )
    decay_ref[...] = decay * keep
    drive_ref[...] = share * in_gate * conv


def gate_back_kernel(
    conv_ref, both_ref, vectors_ref, reset_ref, d_decay_ref, d_drive_ref,
    d_conv_ref, grad_ref, sums_ref,
):
    conv, rate, in_gate, decay, keep, power, root, share = gate_parts(
        conv_ref, both_ref, vectors_ref, reset_ref
    )
    d_drive = d_drive_ref[...]
    through = jnp.where(
        power > floor_value, d_drive * keep * in_gate * conv * (decay * decay) / root, 0.0
    )
    d_log = d_decay_ref[...] * decay * keep - through
    d_rate = (d_log * vectors_ref[2:3] * rate * (1.0 - rate)).astype(bf16)
    d_input = (d_drive * share * conv * in_gate * (1.0 - in_gate)).astype(bf16)
    d_both = jnp.concatenate([d_rate, d_input], 1)
    d_conv = (d_drive * share * in_gate + contract(d_both, both_ref[...], 1, 1)).astype(bf16)
    d_conv_ref[...] = d_conv
    grad_ref[...] = contract(conv_ref[...], d_both, 0, 0).astype(bf16)
    sums_ref[0:1] = jnp.sum(d_rate.astype(f32), axis=0, keepdims=True)
    sums_ref[1:2] = jnp.sum(d_input.astype(f32), axis=0, keepdims=True)
    sums_ref[2:3] = jnp.sum(d_log * rate, axis=0, keepdims=True)
    sums_ref[3:4] = jnp.sum(d_conv.astype(f32), axis=0, keepdims=True)


def gate_call(kernel, conv, both, vectors, reset, grads, out_kinds):
    rows, channels = conv.shape
    per_row = pl.BlockSpec((rows, HW), lambda h: (0, h))
    kinds = {
        "rows": (per_row, (rows, channels)),
        "weights": (pl.BlockSpec((HW, 2 * HW), lambda h: (h, 0)), (channels, 2 * HW)),
        "sums": (pl.BlockSpec((4, HW), lambda h: (0, h)), (4, channels)),
    }
    return pl.pallas_call(
        kernel,
        grid=(channels // HW,),
        out_shape=[jax.ShapeDtypeStruct(kinds[kind][1], dtype) for kind, dtype in out_kinds],
        in_specs=[
            per_row,
            kinds["weights"][0],
            pl.BlockSpec((vectors.shape[0], HW), lambda h: (0, h)),
            pl.BlockSpec((rows, 1), lambda h: (0, 0)),
        ]
        + [per_row] * len(grads),
        out_specs=[kinds[kind][0] for kind, _ in out_kinds],
        compiler_params=pltpu.CompilerParams(vmem_limit_bytes=32 * 2**20),
        cost_estimate=pl.CostEstimate(
            flops=4 * rows * channels * HW * (1 + 2 * len(grads)),
            bytes_accessed=24 * rows * channels,
            transcendentals=6 * rows * channels,
        ),
    )(conv, both, vectors, reset, *grads)


def pair_slots(count):
    half = count // 2
    return [k for s in range(1, half) for k in (count - s, s)] + [half, 0]


def gelu_parts(v):
    root, cubic = 0.7978845608028654, 0.044715
    curve = jnp.tanh(root * (v + cubic * v * v * v))
    act = 0.5 * v * (1.0 + curve)
    slope = 0.5 * (1.0 + curve) + 0.5 * v * (1.0 - curve * curve) * root * (
        1.0 + 3.0 * cubic * v * v
    )
    return (act, slope)


def contract(left, right, left_dim, right_dim):
    return lax.dot_general(
        left, right, (((left_dim,), (right_dim,)), ((), ())), preferred_element_type=f32
    )


def ff_kernel(order, cores, own_ref, gate_hbm, up_hbm, down_hbm, *refs):
    cot_count = len(refs) - 37
    cot_hbm, refs = refs[:cot_count], refs[cot_count:]
    blocks_ref, out_ref, d_in_ref, gate_grad, up_grad, down_grad, sum_ref, *refs = refs
    gate_ref, up_ref, down_ref, rows_ref, cots_ref, h_ref, g_ref, u_ref, o_ref, d_ref, *refs = refs
    lone_refs, refs = refs[:7], refs[7:]
    gate_sum, up_sum, down_sum, landing, mine, *refs = refs
    send_sem, recv_sem, load_sem, store_sem, back_send, back_recv, mine_sem, done_sem = refs
    count = len(order)
    half = count // 2
    rows, width = own_ref.shape
    hidden_here = gate_ref.shape[1]
    cut = rows // 2
    me = lax.axis_index("seq")
    ahead_of, behind_of = [0] * count, [0] * count
    for i, device in enumerate(order):
        ahead_of[device] = order[(i + 1) % count]
        behind_of[device] = order[(i - 1) % count]
    sides = ({"seq": lookup(ahead_of, me)}, {"seq": lookup(behind_of, me)})
    dp = lax.axis_index("dp")
    core = {"dp": dp + 1 - 2 * lax.rem(dp, 2)}

    barrier = pltpu.get_barrier_semaphore()
    peers = list(sides) + ([core] if cores == 2 else [])
    for peer in peers:
        pl.semaphore_signal(barrier, inc=1, device_id=peer, device_id_type=pl.DeviceIdType.MESH)
    weights = [
        pltpu.make_async_copy(hbm, vmem, load_sem.at[i])
        for i, (hbm, vmem) in enumerate(
            ((gate_hbm, gate_ref), (up_hbm, up_ref), (down_hbm, down_ref))
        )
    ]
    for copy in weights:
        copy.start()
    pl.semaphore_wait(barrier, len(peers))

    def full(side, source, slot, s):
        return remote(
            source, blocks_ref.at[slot], send_sem.at[side, s], recv_sem.at[slot], sides[side]
        )

    def part(side):
        at = pl.ds(0, cut) if side == 0 else pl.ds(cut, rows - cut)
        return remote(
            blocks_ref.at[2 * (half - 2) + side, at],
            blocks_ref.at[count - 2, at],
            send_sem.at[side, half - 1],
            recv_sem.at[count - 2 + side],
            sides[side],
        )

    for side in range(2):
        full(side, own_ref, side, 0).start()

    def rows_load(s):
        return pltpu.make_async_copy(
            blocks_ref.at[pl.ds(2 * (s - 1), 2)], rows_ref, load_sem.at[3]
        )

    pair_refs = (rows_ref, cots_ref, h_ref, g_ref, u_ref, o_ref, d_ref)

    def stores(s):
        return [
            pltpu.make_async_copy(o_ref, out_ref.at[s - 1], store_sem.at[0]),
            pltpu.make_async_copy(d_ref, d_in_ref.at[s - 1], store_sem.at[1]),
        ]

    def lone_stores(first):
        at = pl.ds(first * rows, rows)
        return [
            pltpu.make_async_copy(lone_refs[5], out_ref.at[half - 1, at], store_sem.at[2]),
            pltpu.make_async_copy(lone_refs[6], d_in_ref.at[half - 1, at], store_sem.at[3]),
        ]

    wide = 256 if hidden_here % 256 == 0 else 128
    out_wide = 512

    def multiply(refs):
        x_ref, c_ref, h_to, g_to, u_to, o_to, d_to = refs
        many = h_to.shape[0]

        def inner(j, carry):
            at = pl.ds(pl.multiple_of(j * wide, wide), wide)
            x = x_ref[...].reshape(many, width)
            c = c_ref[...].reshape(many, width)
            ff_gate = contract(x, gate_ref[:, at], 1, 0)
            ff_up = contract(x, up_ref[:, at], 1, 0)
            d_hidden = contract(c, down_ref[at, :], 1, 1)
            act, slope = gelu_parts(ff_gate)
            h_to[:, at] = (act * ff_up).astype(bf16)
            g_to[:, at] = (d_hidden * ff_up * slope).astype(bf16)
            u_to[:, at] = (d_hidden * act).astype(bf16)
            return carry

        lax.fori_loop(0, hidden_here // wide, inner, 0)

        def outer(j, carry):
            at = pl.ds(pl.multiple_of(j * out_wide, out_wide), out_wide)
            d_to[:, at] = (
                contract(g_to[...], gate_ref[at, :], 1, 1) + contract(u_to[...], up_ref[at, :], 1, 1)
            ).astype(bf16)
            o_to[:, at] = contract(h_to[...], down_ref[:, at], 1, 0).astype(bf16)
            return carry

        lax.fori_loop(0, width // out_wide, outer, 0)

    def gradients(refs, fresh=False):
        x_ref, c_ref, h_to, g_to, u_to = refs[:5]
        many = h_to.shape[0]
        tile = 256

        def body(j, carry):
            at = pl.ds(pl.multiple_of(j * tile, tile), tile)
            x = x_ref[..., at].reshape(many, tile)
            c = c_ref[..., at].reshape(many, tile)
            terms = (
                contract(x, g_to[...], 0, 0),
                contract(x, u_to[...], 0, 0),
                contract(h_to[...], c, 0, 0),
            )
            places = (
                (gate_sum, (at, slice(None))),
                (up_sum, (at, slice(None))),
                (down_sum, (slice(None), at)),
            )
            for term, (ref, place) in zip(terms, places):
                ref[place] = term if fresh else ref[place] + term
            return carry

        lax.fori_loop(0, width // tile, body, 0)

    def run(copies):
        for copy in copies:
            copy.start()
        for copy in copies:
            copy.wait()

    run(
        [
            pltpu.make_async_copy(own_ref, lone_refs[0], load_sem.at[3]),
            pltpu.make_async_copy(cot_hbm[0], lone_refs[1], load_sem.at[4]),
        ]
    )
    for copy in weights:
        copy.wait()
    multiply(lone_refs)
    for copy in lone_stores(1):
        copy.start()
    gradients(lone_refs, True)
    for copy in lone_stores(1):
        copy.wait()

    def step(s, carry):
        for side in range(2):
            full(side, own_ref, 2 * (s - 1) + side, s).wait_recv()

        @pl.when(s < half - 1)
        def _():
            for side in range(2):
                slot = 2 * (s - 1) + side
                full(side, blocks_ref.at[slot], slot + 2, s).start()

        @pl.when(s == half - 1)
        def _():
            for side in range(2):
                part(side).start()

        rows_load(s).start()
        for at_step in range(1, half):

            @pl.when(s == at_step)
            def _():
                run(
                    [
                        pltpu.make_async_copy(
                            cot_hbm[2 * at_step - 1 + i], cots_ref.at[i], load_sem.at[4 + i]
                        )
                        for i in range(2)
                    ]
                )

        rows_load(s).wait()
        multiply(pair_refs)
        for copy in stores(s):
            copy.start()

        @pl.when(s < half - 1)
        def _():
            gradients(pair_refs)

        for copy in stores(s):
            copy.wait()
        return carry

    lax.fori_loop(1, half, step, 0)
    far, first = [], 0
    for i, part_hbm in enumerate(cot_hbm[2 * half - 1 :]):
        part_rows = part_hbm.shape[0]
        far.append(
            pltpu.make_async_copy(
                part_hbm, lone_refs[1].at[pl.ds(first, part_rows)], load_sem.at[5 + i]
            )
        )
        first += part_rows
    run(far)
    for side in range(2):
        part(side).wait_recv()
    run([pltpu.make_async_copy(blocks_ref.at[count - 2], lone_refs[0], load_sem.at[3])])
    multiply(lone_refs)

    chunks = 2
    chunk = width // chunks

    def part_of(d, side):
        if d == 0:
            return half - 1, rows
        return d - 1, (rows if side == 0 else 0)

    def own_load(d, side):
        pair, first = part_of(d, side)
        return pltpu.make_async_copy(
            d_in_ref.at[pair, pl.ds(first, rows)], mine.at[side, d % 2], mine_sem.at[side, d % 2]
        )

    def back(d, side, c):
        cols = pl.ds(c * chunk, chunk)
        at = pl.ds(0, rows)
        if d == half:
            at = pl.ds(0, cut) if side == 0 else pl.ds(cut, rows - cut)
            source = lone_refs[6].at[at, cols]
        else:
            source = mine.at[side, d % 2, at, cols]
        return remote(
            source,
            landing.at[side, d - 1, at, cols],
            back_send.at[side, d - 1, c],
            back_recv.at[side, d - 1, c],
            sides[side],
        )

    def add_landed(target, terms, first, many, cols):
        def body(t, carry):
            at = pl.ds(pl.multiple_of(first + t * 16, 16), 16)
            target[at, cols] = total([term[at, cols].astype(f32) for term in terms]).astype(target.dtype)
            return carry

        lax.fori_loop(0, many // 16, body, 0)

    for c in range(chunks):
        for side in range(2):
            back(half, side, c).start()
    for copy in lone_stores(0):
        copy.start()
    for side in range(2):
        own_load(half - 1, side).start()
    gradients(pair_refs)
    gradients(lone_refs)

    def finish(total_ref, low_ref, out_hbm, sem):
        def body(t, carry):
            at = pl.ds(pl.multiple_of(t * 16, 16), 16)
            low_ref[at, :] = total_ref[at, :].astype(bf16)
            return carry

        lax.fori_loop(0, total_ref.shape[0] // 16, body, 0)
        copy = pltpu.make_async_copy(low_ref, out_hbm, load_sem.at[sem])
        copy.start()
        return copy

    results = ((gate_sum, gate_ref, gate_grad), (up_sum, up_ref, up_grad), (down_sum, down_ref, down_grad))
    finished = []
    for d in range(half - 1, 0, -1):
        for side in range(2):
            own_load(d, side).wait()
        for c in range(chunks):
            cols = pl.ds(c * chunk, chunk)
            for side in range(2):
                back(d + 1, side, c).wait_recv()
                first, many = (0, rows)
                if d == half - 1:
                    first, many = (0, cut) if side == 0 else (cut, rows - cut)
                held = mine.at[side, d % 2]
                add_landed(held, [held, landing.at[side, d]], first, many, cols)
                back(d, side, c).start()
        for side in range(2):
            if d < half - 1:
                for c in range(chunks):
                    back(d + 1, side, c).wait_send()
            if d > 1 or side == 0:
                own_load(d - 1, side).start()
        if len(finished) < len(results):
            finished.append(finish(*results[len(finished)], len(finished)))
    own_load(0, 0).wait()
    for c in range(chunks):
        cols = pl.ds(c * chunk, chunk)
        for side in range(2):
            back(1, side, c).wait_recv()
        add_landed(sum_ref, [mine.at[0, 0], landing.at[0, 0], landing.at[1, 0]], 0, rows, cols)
    if cores == 2:
        pl.semaphore_signal(done_sem, inc=1, device_id=core, device_id_type=pl.DeviceIdType.MESH)
    while len(finished) < len(results):
        finished.append(finish(*results[len(finished)], len(finished)))
    for copy in finished:
        copy.wait()
    for copy in lone_stores(0):
        copy.wait()
    for side in range(2):
        for c in range(chunks):
            back(half, side, c).wait_send()
            back(1, side, c).wait_send()
        for s in range(half - 1):
            full(side, own_ref, side, s).wait_send()
        part(side).wait_send()
    if cores == 2:
        pl.semaphore_wait(done_sem, 1)


def ff_call(net, own, cots, slab_gate, slab_up, slab_down):
    rows, width = own.shape
    count, half = net.seq_count, net.seq_count // 2
    hidden_here = slab_gate.shape[1]
    anywhere = pl.BlockSpec(memory_space=pl.ANY)
    pair = 2 * rows
    shape = jax.ShapeDtypeStruct
    return pl.pallas_call(
        functools.partial(ff_kernel, net.order, net.cores),
        out_shape=[
            shape((count, rows, width), bf16),
            shape((half, pair, width), bf16),
            shape((half, pair, width), bf16),
            shape((width, hidden_here), bf16),
            shape((width, hidden_here), bf16),
            shape((hidden_here, width), bf16),
            shape((rows, width), f32),
        ],
        in_specs=[anywhere] * (4 + len(cots)),
        out_specs=[anywhere] * 6 + [pl.BlockSpec(memory_space=pltpu.VMEM)],
        scratch_shapes=[
            pltpu.VMEM((width, hidden_here), bf16),
            pltpu.VMEM((width, hidden_here), bf16),
            pltpu.VMEM((hidden_here, width), bf16),
            pltpu.VMEM((2, rows, width), bf16),
            pltpu.VMEM((2, rows, width), bf16),
            pltpu.VMEM((pair, hidden_here), bf16),
            pltpu.VMEM((pair, hidden_here), bf16),
            pltpu.VMEM((pair, hidden_here), bf16),
            pltpu.VMEM((pair, width), bf16),
            pltpu.VMEM((pair, width), bf16),
            pltpu.VMEM((rows, width), bf16),
            pltpu.VMEM((rows, width), bf16),
            pltpu.VMEM((rows, hidden_here), bf16),
            pltpu.VMEM((rows, hidden_here), bf16),
            pltpu.VMEM((rows, hidden_here), bf16),
            pltpu.VMEM((rows, width), bf16),
            pltpu.VMEM((rows, width), bf16),
            pltpu.VMEM((width, hidden_here), f32),
            pltpu.VMEM((width, hidden_here), f32),
            pltpu.VMEM((hidden_here, width), f32),
            pltpu.VMEM((2, half, rows, width), bf16),
            pltpu.VMEM((2, 2, rows, width), bf16),
            pltpu.SemaphoreType.DMA((2, half)),
            pltpu.SemaphoreType.DMA((count,)),
            pltpu.SemaphoreType.DMA((8,)),
            pltpu.SemaphoreType.DMA((4,)),
            pltpu.SemaphoreType.DMA((2, half, 2)),
            pltpu.SemaphoreType.DMA((2, half, 2)),
            pltpu.SemaphoreType.DMA((2, 2)),
            pltpu.SemaphoreType.REGULAR,
        ],
        compiler_params=pltpu.CompilerParams(
            collective_id=2, has_side_effects=True, vmem_limit_bytes=62 * 2**20
        ),
        cost_estimate=pl.CostEstimate(
            flops=18 * count * rows * width * hidden_here,
            bytes_accessed=80 * 2**20,
            transcendentals=count * rows * hidden_here,
        ),
    )(own, slab_gate, slab_up, slab_down, *cots)


def passed_along(value, axis, steps):
    count = lax.axis_size(axis)
    first, last = (max(0, -steps), min(count, count - steps))
    return lax.ppermute(value, axis, [(source, source + steps) for source in range(first, last)])


def gelu_tanh(values):
    return jax.nn.gelu(values, approximate=True)


def rms_parts(values, norm_gain):
    root_scale = lax.rsqrt(jnp.mean(values * values, axis=-1, keepdims=True) + epsilon)
    unit_rows = values * root_scale
    return (unit_rows * norm_gain, root_scale, unit_rows)


def norm_back(d_normed, norm_gain, root_scale, unit_rows):
    weighted = d_normed * norm_gain
    grad_gain = jnp.sum(d_normed * unit_rows, axis=0)
    d_values = root_scale * (
        weighted - unit_rows * jnp.mean(weighted * unit_rows, axis=-1, keepdims=True)
    )
    return (grad_gain, d_values)


def rows_of(values, first_row, row_count):
    return lax.slice_in_dim(values, first_row, first_row + row_count, axis=values.ndim - 2)


def dot(left, right):
    return jnp.dot(left, right, preferred_element_type=f32)


def dot_t(left, right):
    return lax.dot_general(left, right, (((1,), (1,)), ((), ())), preferred_element_type=f32)


def t_dot(left, right):
    return lax.dot_general(left, right, (((0,), (0,)), ((), ())), preferred_element_type=f32)


def per_device(
    inputs,
    reset,
    initial_state,
    cotangent,
    norm1_gain,
    w_gate,
    w_in,
    conv_w,
    conv_bias,
    w_rgate,
    rgate_bias,
    w_igate,
    igate_bias,
    decay_param,
    w_out,
    norm2_gain,
    w_ffgate,
    w_ffup,
    w_ffdown,
):
    net = Net()
    seqs_here, len_here, width = inputs.shape
    assert seqs_here == 1
    rows_here = len_here
    dp_count, seq_count = net.dp_count, net.seq_count
    devices = dp_count * seq_count
    chan_here, channels = w_rgate.shape[0], w_rgate.shape[0] * devices
    wide_here = norm1_gain.shape[0]
    taps = conv_w.shape[0]
    rim_rows = taps - 1

    def lanes(rows):
        return jnp.pad(rows, ((0, 0),) * (rows.ndim - 1) + ((0, LINE - rows.shape[-1]),))

    vectors = [norm1_gain, norm2_gain, conv_w, conv_bias, rgate_bias, igate_bias, decay_param]
    small = jnp.concatenate([lanes(v.reshape(-1, v.shape[-1])) for v in vectors], 0)
    rim_inputs = inputs.reshape(rows_here, width)[rows_here - rim_rows :]
    full_in, full_gate, full_out, small_all, full_both, start_state, rims, flags = gather_call(
        net,
        (
            w_in,
            w_gate,
            w_out,
            small,
            jnp.concatenate([w_rgate, w_igate], 1),
            initial_state,
            rim_inputs,
            reset.astype(f32),
        ),
        [
            (6, 0, rim_rows, RING_ONLY),
            (7, 0, 1, RING_ONLY),
            (3, 0, small.shape[0], RING_FIRST),
            (4, 0, chan_here, RING_FIRST),
            (0, 0, wide_here, RING_FIRST),
            (1, 0, wide_here, CHIP_FIRST),
            (2, 0, chan_here, RING_FIRST),
            (5, 0, 1, RING_ONLY),
        ],
    )
    full_in, full_gate = (v.reshape(width, channels) for v in (full_in, full_gate))
    full_out = full_out.reshape(channels, width)
    full_both = full_both.reshape(channels, 2 * HW)
    start_state = start_state.reshape(1, channels)
    small_all = small_all.reshape(devices, -1, LINE)
    full_norm1 = small_all[:, 0, :wide_here].reshape(-1).astype(f32)
    full_norm2 = small_all[:, 1, :wide_here].reshape(-1).astype(f32)
    conv_wf = small_all[:, 2 : 2 + taps, :chan_here].transpose(1, 0, 2).reshape(taps, channels).astype(f32)
    full_cbias, full_rbias, full_ibias, decay_f = (
        small_all[:, i, :chan_here].reshape(-1).astype(f32) for i in range(2 + taps, 6 + taps)
    )
    gate_vectors = jnp.stack([full_rbias, full_ibias, -8.0 * jax.nn.softplus(-decay_f)], 0)
    at_seq = lax.axis_index("seq")
    last_seq = seq_count - 1

    def neighbour(values, index, there):
        picked = lax.dynamic_index_in_dim(values[0], jnp.clip(index, 0, last_seq), 0, keepdims=False)
        return jnp.where(there, picked, jnp.zeros_like(picked))

    rim_before = neighbour(rims, at_seq - 1, at_seq > 0)
    flags_before = neighbour(flags, at_seq - 1, at_seq > 0)[0, rows_here - rim_rows :]
    flags_after = neighbour(flags, at_seq + 1, at_seq < last_seq)[0, :rim_rows]
    flags_here = reset.reshape(rows_here).astype(f32)
    w_ffgate, w_ffup, w_ffdown, cotangent, full_in = lax.optimization_barrier(
        (w_ffgate, w_ffup, w_ffdown, cotangent, full_in)
    )
    slab_gate, slab_up, slab_down = (
        lax.all_gather(w_ffgate, "dp", axis=0, tiled=True),
        lax.all_gather(w_ffup, "dp", axis=0, tiled=True),
        lax.all_gather(w_ffdown, "dp", axis=1, tiled=True),
    )
    cotan_rows = cotangent.reshape(rows_here, width)
    cot_flow = Flow(net.seq.gather_steps(cotan_rows))

    lead = 8 - rim_rows
    token_rows = inputs.reshape(rows_here, width).astype(f32)
    normed_f, scale_one, unit_one = rms_parts(token_rows, full_norm1)
    normed = normed_f.astype(bf16)
    rim_normed = rms_parts(rim_before.astype(f32), full_norm1)[0].astype(bf16)
    extended = jnp.concatenate([jnp.pad(rim_normed, ((lead, 0), (0, 0))), normed], 0)
    branch = dot(extended, full_in).astype(bf16)
    gate_pre = dot(normed, full_gate)
    branch, gate_pre = beside((branch, gate_pre), cot_flow)
    padded = branch[lead:].astype(f32)
    open_pad = (1.0 - jnp.concatenate([flags_before, flags_here], 0))[:, None]
    open_masks = [None]
    conv_total = full_cbias + conv_wf[0] * rows_of(padded, rim_rows, len_here)
    running = rows_of(open_pad, rim_rows, len_here)
    for offset in range(1, rim_rows + 1):
        if offset > 1:
            running = running * rows_of(open_pad, rim_rows + 1 - offset, len_here)
        open_masks.append(running)
        conv_total = conv_total + running * conv_wf[offset] * rows_of(
            padded, rim_rows - offset, len_here
        )
    conv_low = conv_total.astype(bf16)
    reset_col = reset.astype(f32).reshape(rows_here, 1)
    decay_rows, drive_rows = gate_call(
        gate_kernel, conv_low, full_both, gate_vectors, reset_col, (), [("rows", f32)] * 2
    )
    row_shape = jax.ShapeDtypeStruct((rows_here, channels), f32)
    states, prev_states, last_state = scan_call(
        scan_kernel,
        0,
        seq_count,
        (decay_rows, drive_rows, start_state),
        [row_shape, row_shape, jax.ShapeDtypeStruct((1, channels), f32)],
    )
    states = beside(states, cot_flow)
    final_here = initial_state.shape[1]
    final_state = lax.dynamic_slice_in_dim(
        last_state, lax.axis_index("seq") * final_here, final_here, 1
    )
    state_f = states.astype(bf16).astype(f32)
    gate_act, gate_back = jax.vjp(gelu_tanh, gate_pre)
    mixed_rows = (state_f * gate_act).astype(bf16)
    residual = token_rows + dot(mixed_rows, full_out)

    slots = pair_slots(seq_count)
    cot_blocks = cot_flow.finish()
    cots = [cotan_rows] + [cot_blocks[k] for k in slots[:-2]] + cot_blocks[seq_count // 2]
    normed_two_f, scale_two, unit_two = rms_parts(residual, full_norm2)
    normed_two = normed_two_f.astype(bf16)
    _, out_part, _, gate_part, up_part, down_part, d_normed_two = ff_call(
        net, normed_two, cots, slab_gate, slab_up, slab_down
    )

    def block_rows(whole):
        whole = whole.reshape(seq_count, rows_here, width)
        return lambda k: whole[slots.index(k)]

    d_normed_two, out_part, gate_part, up_part, down_part = lax.optimization_barrier(
        (d_normed_two, out_part, gate_part, up_part, down_part)
    )
    out_flow = Flow(net.seq.scatter_steps(block_rows(out_part)))
    grad_ffgate, grad_ffup, grad_ffdown = (
        lax.psum_scatter(part, "dp", scatter_dimension=axis, tiled=True).astype(f32)
        for part, axis in ((gate_part, 0), (up_part, 0), (down_part, 1))
    )

    grad_norm2, d_resid_norm = norm_back(d_normed_two, full_norm2, scale_two, unit_two)
    d_residual = cotan_rows.astype(f32) + d_resid_norm
    d_residual_low = d_residual.astype(bf16)
    d_mixed = dot_t(d_residual_low, full_out)
    d_state = (d_mixed * gate_act).astype(bf16)
    d_gate_pre = gate_back(d_mixed * state_f)[0].astype(bf16)
    d_state, d_gate_pre = beside((d_state, d_gate_pre), out_flow)

    def grad_terms(left, right):
        return t_dot(left, right).astype(bf16).reshape(dp_count, seq_count, -1, right.shape[1])

    gate_terms = grad_terms(normed, d_gate_pre)
    d_drive, d_decay = scan_call(
        scan_back_kernel,
        1,
        seq_count,
        (decay_rows, d_state.astype(f32), prev_states),
        [row_shape, row_shape],
    )
    d_drive, d_decay, gate_terms = beside((d_drive, d_decay, gate_terms), out_flow)
    out_terms = grad_terms(mixed_rows, d_residual_low)
    d_conv_low, both_terms, gate_sums = gate_call(
        gate_back_kernel,
        conv_low,
        full_both,
        gate_vectors,
        reset_col,
        (d_decay, d_drive),
        [("rows", bf16), ("weights", bf16), ("sums", f32)],
    )
    d_conv_low, out_terms = beside((d_conv_low, out_terms), out_flow)
    grad_rbias, grad_ibias, rate_sum, grad_cbias = gate_sums
    grad_decay = 8.0 * jax.nn.sigmoid(-decay_f) * rate_sum
    rim_grad = passed_along(d_conv_low[:rim_rows], "seq", -1)
    grad_ext = jnp.concatenate([d_conv_low, rim_grad], 0).astype(f32)
    open_next = (1.0 - jnp.concatenate([flags_here, flags_after], 0))[:, None]
    d_conv_f = rows_of(grad_ext, 0, len_here)
    d_branch = conv_wf[0] * d_conv_f
    ahead = None
    conv_grads = [jnp.sum(rows_of(padded, rim_rows, len_here) * d_conv_f, axis=0)]
    for offset in range(1, rim_rows + 1):
        step_open = rows_of(open_next, offset, len_here)
        ahead = step_open if offset == 1 else ahead * step_open
        d_branch = d_branch + ahead * conv_wf[offset] * rows_of(grad_ext, offset, len_here)
        conv_grads.append(
            jnp.sum(
                open_masks[offset] * rows_of(padded, rim_rows - offset, len_here) * d_conv_f,
                axis=0,
            )
        )
    grad_conv = jnp.stack(conv_grads, 0)
    d_branch_low = d_branch.astype(bf16)
    in_terms = grad_terms(normed, d_branch_low)
    d_normed_one = dot_t(d_branch_low, full_in) + dot_t(d_gate_pre, full_gate)
    grad_norm1, d_token_norm = norm_back(d_normed_one, full_norm1, scale_one, unit_one)
    input_grad = (d_residual + d_token_norm).reshape(seqs_here, len_here, width)

    grad_norm1, input_grad = beside((grad_norm1, input_grad), out_flow)
    ff_out = out_flow.finish()
    output = (residual + ff_out).astype(bf16).reshape(seqs_here, len_here, width)

    small_grads = [
        lanes(v.reshape(-1, devices, v.shape[-1] // devices).transpose(1, 0, 2)).astype(bf16)
        for v in (grad_norm1, grad_norm2, grad_conv, grad_cbias, grad_rbias, grad_ibias, grad_decay)
    ]
    small_terms = jnp.concatenate(small_grads, 1).reshape(dp_count, seq_count, -1, LINE)
    half_rows = chan_here * 3 // 5 // 16 * 16
    out_pieces = [(2, 0, half_rows, CHIP_FIRST), (2, half_rows, chan_here - half_rows, RING_FIRST)]
    if half_rows == 0 or chan_here % 16:
        out_pieces = [(2, 0, chan_here, CHIP_FIRST)]
    grad_in, grad_gate, grad_out, small_mine, both_mine = reduce_call(
        net,
        [
            in_terms,
            gate_terms,
            out_terms,
            small_terms,
            both_terms.reshape(dp_count, seq_count, chan_here, 2 * HW),
        ],
        [(1, 0, wide_here, RING_FIRST)]
        + out_pieces
        + [
            (3, 0, small.shape[0], CHIP_FIRST),
            (4, 0, chan_here, CHIP_FIRST),
            (0, 0, wide_here, CHIP_FIRST),
        ],
    )
    mine = [small_mine[i, :wide_here] for i in range(2)]
    mine += [small_mine[2 : 2 + taps, :chan_here]]
    mine += [small_mine[i, :chan_here] for i in range(2 + taps, 6 + taps)]
    return (
        output,
        input_grad,
        final_state,
        mine[0],
        grad_gate,
        grad_in,
        mine[2],
        mine[3],
        both_mine[:, :HW],
        mine[4],
        both_mine[:, HW:],
        mine[5],
        mine[6],
        grad_out,
        mine[1],
        grad_ffgate,
        grad_ffup,
        grad_ffdown,
    )


def solution(mesh):
    split = ("dp", "seq")
    return jax.shard_map(
        per_device,
        mesh=mesh,
        in_specs=(
            P("dp", "seq", None),
            P("dp", "seq"),
            P("dp", "seq"),
            P("dp", "seq", None),
            P(split),
            P(split, None),
            P(split, None),
            P(None, split),
            P(split),
            P(split, None),
            P(split),
            P(split, None),
            P(split),
            P(split),
            P(split, None),
            P(split),
            P("dp", "seq"),
            P("dp", "seq"),
            P("seq", "dp"),
        ),
        out_specs=(
            P("dp", "seq", None),
            P("dp", "seq", None),
            P("dp", "seq"),
            P(split),
            P(split, None),
            P(split, None),
            P(None, split),
            P(split),
            P(split, None),
            P(split),
            P(split, None),
            P(split),
            P(split),
            P(split, None),
            P(split),
            P("dp", "seq"),
            P("dp", "seq"),
            P("seq", "dp"),
        ),
        check_vma=False,
    )
```

```python
import functools

import jax
import jax.numpy as jnp
from jax import lax
from jax.experimental import pallas as pl
from jax.experimental.pallas import tpu as pltpu
from jax.sharding import PartitionSpec as P

HW = 256
LANES = 8
LINE = 128


epsilon = 1e-06
floor_value = 0.0001
f32 = jnp.float32
bf16 = jnp.bfloat16


def seq_order(count):
    if count % 8:
        return list(range(count))
    wide = count // 4
    path = []
    for z in range(4):
        ys = range(1, wide) if z % 2 == 0 else range(wide - 1, 0, -1)
        path += [z * wide + y for y in ys]
    return path + [z * wide for z in (3, 2, 1, 0)]


class Ring:
    def __init__(self, axis, cycles):
        self.axis = axis
        self.cycles = cycles
        self.count = len(cycles[0])

    def shift(self, value, step):
        pairs = [
            (cycle[i], cycle[(i + step) % self.count])
            for cycle in self.cycles
            for i in range(self.count)
        ]
        return lax.ppermute(value, self.axis, pairs)

    def place(self):
        table = [0] * (self.count * len(self.cycles))
        for cycle in self.cycles:
            for i, device in enumerate(cycle):
                table[device] = i
        return jnp.asarray(table, jnp.int32)[lax.axis_index(self.axis)]

    def gather_steps(self, value):
        count, half = self.count, self.count // 2
        blocks = [value] * count
        if count == 1:
            return blocks
        ahead = behind = value
        for step in range(1, half):
            behind, ahead = yield [self.shift(behind, 1), self.shift(ahead, -1)]
            blocks[count - step] = behind
            blocks[step] = ahead
        rows = value.shape[0]
        if half > 1 and rows % 32 == 0:
            top, bottom = yield [
                self.shift(behind[: rows // 2], 1),
                self.shift(ahead[rows // 2 :], -1),
            ]
            blocks[half] = [top, bottom]
        else:
            blocks[half] = yield [self.shift(behind, 1)]
        return blocks

    def scatter_steps(self, part):
        count, half = self.count, self.count // 2
        if count == 1:
            return []
        far = part(half).astype(bf16)
        if half == 1:
            return (yield [self.shift(far, 1)])
        rows = far.shape[0]
        assert rows % 2 == 0
        cut = rows // 2
        ahead, behind = far[:cut], far[cut:]
        for k in range(half - 1, -1, -1):
            got_ahead, got_behind = yield [self.shift(ahead, 1), self.shift(behind, -1)]
            if k == 0:
                return [got_ahead, got_behind]
            got_ahead, got_behind = got_ahead.astype(f32), got_behind.astype(f32)
            ahead, behind = part(k).astype(f32), part(count - k).astype(f32)
            if k == half - 1:
                ahead = jnp.concatenate([ahead[:cut] + got_ahead, ahead[cut:]], 0)
                behind = jnp.concatenate([behind[:cut], behind[cut:] + got_behind], 0)
            else:
                ahead, behind = ahead + got_ahead, behind + got_behind
            ahead, behind = ahead.astype(bf16), behind.astype(bf16)


class Flow:
    def __init__(self, steps):
        self.steps, self.pending, self.result = steps, [], None
        self.advance(None)

    def advance(self, arrived):
        try:
            self.pending = self.steps.send(arrived)
        except StopIteration as stop:
            self.pending, self.result = [], stop.value

    def finish(self):
        while self.pending:
            self.advance(self.pending)
        return self.result


def beside(values, *flows):
    values, arrived = lax.optimization_barrier((values, [flow.pending for flow in flows]))
    for flow, got in zip(flows, arrived):
        if got:
            flow.advance(got)
    return values


class Net:
    def __init__(self):
        self.seq_count = lax.axis_size("seq")
        self.dp_count = lax.axis_size("dp")
        self.order = seq_order(self.seq_count)
        self.seq = Ring("seq", [self.order])
        self.cores = 2 if self.dp_count % 2 == 0 else 1
        self.chips = self.dp_count // self.cores


def lookup(table, index):
    value = jnp.int32(table[0])
    for i, entry in enumerate(table):
        value = jnp.where(index == i, jnp.int32(entry), value)
    return value


class Links:
    def __init__(self, order, chips, cores):
        self.count, self.chips, self.cores = len(order), chips, cores
        me, dp = lax.axis_index("seq"), lax.axis_index("dp")
        count = self.count
        place = [0] * count
        for i, device in enumerate(order):
            place[device] = i
        self.seq_at = [
            lookup([order[(place[d] + k) % count] for d in range(count)], me) for k in range(count)
        ]
        self.ring = ({"seq": self.seq_at[1]}, {"seq": self.seq_at[count - 1]})
        chip, core = dp // cores, dp % cores
        self.chip = [
            {"dp": lax.rem(chip + step, chips) * cores + core} for step in range(1, chips)
        ]
        self.core = {"dp": chip * cores + (1 - core)} if cores == 2 else None
        self.dp_at = [
            lax.rem(chip + k, chips) * cores + lax.rem(core + c, cores)
            for c in range(cores)
            for k in range(chips)
        ]

    def greet(self):
        barrier = pltpu.get_barrier_semaphore()
        peers = list(self.ring) + self.chip + ([self.core] if self.cores == 2 else [])
        for peer in peers:
            pl.semaphore_signal(
                barrier, inc=1, device_id=peer, device_id_type=pl.DeviceIdType.MESH
            )
        pl.semaphore_wait(barrier, len(peers))


def remote(source, target, send_sem, recv_sem, peer):
    return pltpu.make_async_remote_copy(
        src_ref=source,
        dst_ref=target,
        send_sem=send_sem,
        recv_sem=recv_sem,
        device_id=peer,
        device_id_type=pl.DeviceIdType.MESH,
    )


RING_FIRST, CHIP_FIRST, RING_ONLY = 0, 1, 2


def ring_sends(way, chips, half):
    return {RING_FIRST: half + chips - 1, CHIP_FIRST: chips * half, RING_ONLY: half}[way]


def gather_kernel(order, chips, cores, pieces, arrays, *refs):
    ins, outs = refs[:arrays], refs[arrays : 2 * arrays]
    own_sem, recv_sem, ring_sem, chip_sem, core_sem = refs[2 * arrays :]
    links = Links(order, chips, cores)
    count, half = links.count, links.count // 2
    links.greet()
    method = [piece[3] for piece in pieces]
    only_ring = {piece[0] for piece in pieces if piece[3] == RING_ONLY}

    spans = [1 if way == RING_ONLY else chips * cores for way in method]
    sharing = [p for p in range(len(pieces)) if method[p] != RING_ONLY]

    def landed(p, r, k):
        return recv_sem.at[sum(spans[:p]) + r, k]

    def ring_slot(p, r, side, s):
        at = sum(ring_sends(way, chips, half) for way in method[:p])
        if method[p] == CHIP_FIRST or r == 0:
            at += r * half + s
        else:
            at += half + r - 1
        return ring_sem.at[at, side]

    def slot(i, r, k):
        return outs[i].at[0 if i in only_ring else links.dp_at[r], links.seq_at[k]]

    owns = [
        pltpu.make_async_copy(ins[i], slot(i, 0, 0), own_sem.at[i])
        for i in range(arrays)
    ]
    for copy in owns:
        copy.start()
    sent = []

    def whole(p, r, k):
        array, first, rows, _ = pieces[p]
        place = slot(array, r, k)
        return place if rows == ins[array].shape[0] else place.at[pl.ds(first, rows)]

    def rows_in(p, r, k, first, rows):
        return slot(pieces[p][0], r, k).at[pl.ds(pieces[p][1] + first, rows)]

    def held(p, r, k):
        array, first, rows, _ = pieces[p]
        if r == 0 and k == 0:
            return ins[array] if rows == ins[array].shape[0] else ins[array].at[pl.ds(first, rows)]
        return whole(p, r, k)

    def cut_of(p):
        return pieces[p][2] // 32 * 16

    def start(copy):
        copy.start()
        sent.append(copy)

    def ring_copies(p, r, s):
        cut, rows = cut_of(p), pieces[p][2]
        if s < half - 1:
            return [
                remote(
                    held(p, r, (count - s) % count), whole(p, r, (count - s) % count),
                    ring_slot(p, r, 0, s), landed(p, r, count - s - 1), links.ring[0],
                ),
                remote(
                    held(p, r, s), whole(p, r, s),
                    ring_slot(p, r, 1, s), landed(p, r, s + 1), links.ring[1],
                ),
            ]
        back = count - s
        if not cut:
            return [
                remote(
                    whole(p, r, back), whole(p, r, back),
                    ring_slot(p, r, 0, s), landed(p, r, half), links.ring[0],
                )
            ]
        top, bottom = rows_in(p, r, back, 0, cut), rows_in(p, r, s, cut, rows - cut)
        return [
            remote(top, top, ring_slot(p, r, 0, s), landed(p, r, half), links.ring[0]),
            remote(
                bottom, bottom, ring_slot(p, r, 1, s), landed(p, r, count), links.ring[1]
            ),
        ]

    def arrived(p, r, k):
        cut, rows = cut_of(p), pieces[p][2]
        if k == half and cut:
            for part, sem in (((0, cut), half), ((cut, rows - cut), count)):
                ref = rows_in(p, r, k, *part)
                remote(ref, ref, ring_slot(p, 0, 0, 0), landed(p, r, sem), links.ring[0]).wait_recv()
        else:
            ref = whole(p, r, k)
            remote(ref, ref, ring_slot(p, 0, 0, 0), landed(p, r, k), links.ring[0]).wait_recv()

    def to_chips(p, k):
        for step in range(1, chips):
            start(
                remote(
                    held(p, 0, k), whole(p, 0, k),
                    chip_sem.at[sharing.index(p), step - 1, k], landed(p, chips - step, k), links.chip[step - 1],
                )
            )

    def to_core(p, r, k):
        if cores == 2:
            start(
                remote(
                    held(p, r, k), whole(p, r, k),
                    core_sem.at[sharing.index(p), r, k], landed(p, chips + r, k), links.core,
                )
            )

    everyone = range(len(pieces))

    def planes(p):
        return range(chips) if method[p] == CHIP_FIRST else range(1)

    for p in everyone:
        if method[p] != RING_ONLY:
            to_chips(p, 0)
        for copy in ring_copies(p, 0, 0):
            start(copy)
    for p in everyone:
        if method[p] != RING_ONLY:
            to_core(p, 0, 0)
    for s in range(1, half + 1):
        steps = sorted({count - s, s})
        before = sorted({(count - s + 1) % count, s - 1})
        for p in everyone:
            for r in planes(p):
                if r == 0 or s > 1:
                    for k in steps:
                        arrived(p, r, k)
                    if s < half:
                        for copy in ring_copies(p, r, s):
                            start(copy)
                    if method[p] == RING_FIRST and s < half:
                        for k in steps:
                            to_chips(p, k)
                    if method[p] != RING_ONLY:
                        for k in steps:
                            to_core(p, r, k)
        for p in everyone:
            if method[p] == RING_FIRST:
                for r in range(1, chips):
                    for k in before:
                        arrived_from_chip(links, whole(p, r, k), chip_sem.at[sharing.index(p), 0, 0], landed(p, r, k))
                        to_core(p, r, k)
                    if s == half:
                        for copy in ring_copies(p, r, half - 1):
                            start(copy)
            if method[p] == CHIP_FIRST and s == 1:
                for r in range(1, chips):
                    arrived_from_chip(links, whole(p, r, 0), chip_sem.at[sharing.index(p), 0, 0], landed(p, r, 0))
                    for copy in ring_copies(p, r, 0):
                        start(copy)
                    to_core(p, r, 0)
                for r in range(1, chips):
                    for k in steps:
                        arrived(p, r, k)
                    if s < half:
                        for copy in ring_copies(p, r, s):
                            start(copy)
                    for k in steps:
                        to_core(p, r, k)
    for p in everyone:
        if method[p] == RING_FIRST:
            for r in range(1, chips):
                arrived(p, r, half)
                to_core(p, r, half)
    for p in everyone:
        if method[p] != RING_ONLY and cores == 2:
            for r in range(chips):
                for k in range(count):
                    arrived_from_chip(
                        links, whole(p, chips + r, k), core_sem.at[sharing.index(p), r, k], landed(p, chips + r, k)
                    )
    for copy in sent:
        copy.wait_send()
    for copy in owns:
        copy.wait()


def arrived_from_chip(links, ref, send_sem, recv_sem):
    remote(ref, ref, send_sem, recv_sem, links.ring[0]).wait_recv()


def gather_call(net, arrays, pieces):
    chips, cores, count = net.chips, net.cores, net.seq_count
    slots = chips * cores
    only_ring = {piece[0] for piece in pieces if piece[3] == RING_ONLY}
    shared = sum(piece[3] != RING_ONLY for piece in pieces)
    anywhere = pl.BlockSpec(memory_space=pl.ANY)
    return pl.pallas_call(
        functools.partial(gather_kernel, net.order, chips, cores, pieces, len(arrays)),
        out_shape=[
            jax.ShapeDtypeStruct((1 if i in only_ring else slots, count) + v.shape, v.dtype)
            for i, v in enumerate(arrays)
        ],
        in_specs=[anywhere] * len(arrays),
        out_specs=[anywhere] * len(arrays),
        scratch_shapes=[
            pltpu.SemaphoreType.DMA((len(arrays),)),
            pltpu.SemaphoreType.DMA(
                (sum(1 if piece[3] == RING_ONLY else slots for piece in pieces), count + 1)
            ),
            pltpu.SemaphoreType.DMA(
                (sum(ring_sends(piece[3], chips, count // 2) for piece in pieces), 2)
            ),
            pltpu.SemaphoreType.DMA((shared, max(chips - 1, 1), count)),
            pltpu.SemaphoreType.DMA((shared, chips, count)),
        ],
        compiler_params=pltpu.CompilerParams(
            collective_id=3, has_side_effects=True, vmem_limit_bytes=60 * 2**20
        ),
        cost_estimate=pl.CostEstimate(
            flops=0, bytes_accessed=slots * count * sum(v.size for v in arrays) * 4, transcendentals=0
        ),
    )(*arrays)


def add_rows(target, terms, rows):
    if rows % 16:
        target[...] = total([term[...].astype(f32) for term in terms]).astype(target.dtype)
        return

    def body(t, carry):
        at = pl.ds(pl.multiple_of(t * 16, 16), 16)
        target[at] = total([term[at].astype(f32) for term in terms]).astype(target.dtype)
        return carry

    lax.fori_loop(0, rows // 16, body, 0)


def total(terms):
    result = terms[0]
    for term in terms[1:]:
        result = result + term
    return result


def reduce_kernel(order, chips, cores, pieces, arrays, *refs):
    count, half = len(order), len(order) // 2
    parts, refs = refs[:arrays], refs[arrays:]
    outs, refs = refs[:arrays], refs[arrays:]
    mine, refs = refs[:arrays], refs[arrays:]
    other, refs = refs[:arrays], refs[arrays:]
    chip_in, refs = refs[: len(pieces)], refs[len(pieces) :]
    ring_in, refs = refs[: len(pieces)], refs[len(pieces) :]
    load_sem, core_send, core_recv, chip_send, chip_recv, ring_send, ring_recv = refs
    links = Links(order, chips, cores)
    everyone = range(len(pieces))
    method = [piece[3] for piece in pieces]

    loads = [
        [
            pltpu.make_async_copy(parts[i].at[links.dp_at[k]], mine[i].at[k], load_sem.at[i, k])
            for k in range(chips)
        ]
        for i in range(arrays)
    ]
    for copies in loads:
        for copy in copies:
            copy.start()
    links.greet()
    sent = []

    def start(copy):
        copy.start()
        sent.append(copy)

    def rows_of_piece(ref, p, first=0, rows=None):
        array, start_row, piece_rows, _ = pieces[p]
        rows = piece_rows if rows is None else rows
        if rows == ref.shape[0]:
            return ref
        return ref.at[pl.ds(start_row + first, rows)]

    def held(p, k, q):
        return rows_of_piece(mine[pieces[p][0]].at[k, links.seq_at[q]], p)

    def core_copy(p, k, q):
        array = pieces[p][0]
        return remote(
            rows_of_piece(parts[array].at[links.dp_at[chips + k], links.seq_at[q]], p),
            rows_of_piece(other[array].at[k, links.seq_at[q]], p),
            core_send.at[p, k, q], core_recv.at[p, k, q], links.core,
        )

    def steps(d):
        return sorted({d % count, (count - d) % count})

    def planes(p):
        return range(chips) if method[p] == RING_FIRST else range(1)

    if cores == 2:
        for d in range(half, -1, -1):
            for p in everyone:
                for k in reversed(range(chips)):
                    for q in steps(d):
                        start(core_copy(p, k, q))

    loaded = set()

    def core_sum(p, k, q):
        array = pieces[p][0]
        if (array, k) not in loaded:
            loaded.add((array, k))
            loads[array][k].wait()
        if cores == 2:
            core_copy(p, k, q).wait_recv()
            theirs = rows_of_piece(other[array].at[k, links.seq_at[q]], p)
            add_rows(held(p, k, q), [held(p, k, q), theirs], pieces[p][2])

    def chip_copy(p, k, q):
        if method[p] == CHIP_FIRST:
            target = chip_in[p].at[k - 1, links.seq_at[q]]
        else:
            target = chip_in[p].at[k - 1]
        return remote(
            held(p, k, q), target, chip_send.at[p, k - 1, q], chip_recv.at[p, k - 1, q], links.chip[k - 1]
        )

    def chip_sum(p, q):
        for k in range(1, chips):
            chip_copy(p, k, q).wait_recv()
            if method[p] == CHIP_FIRST:
                add_rows(held(p, 0, q), [held(p, 0, q), chip_in[p].at[k - 1, links.seq_at[q]]], pieces[p][2])
            else:
                out = rows_of_piece(outs[pieces[p][0]], p)
                add_rows(out, [out, chip_in[p].at[k - 1]], pieces[p][2])

    def span(p, side, d):
        rows = pieces[p][2]
        cut = rows // 32 * 16
        if d < half:
            return (0, rows)
        if not cut:
            return (0, rows) if side == 0 else None
        return (0, cut) if side == 0 else (cut, rows - cut)

    def ring_copy(p, k, side, d):
        first, rows = span(p, side, d)
        q = d if side == 0 else (count - d) % count
        source = held(p, k, q)
        target = ring_in[p].at[k, side, d - 1]
        if rows != pieces[p][2]:
            source, target = source.at[pl.ds(first, rows)], target.at[pl.ds(first, rows)]
        return remote(
            source, target, ring_send.at[p, k, side, d - 1], ring_recv.at[p, k, side, d - 1], links.ring[side]
        )

    def ring_step(p, k, d):
        if d == 0:
            got = []
            for side in range(2):
                if half > 1 or span(p, side, 1):
                    ring_copy(p, k, side, 1).wait_recv()
                    got.append(ring_in[p].at[k, side, 0])
            target = rows_of_piece(outs[pieces[p][0]], p) if k == 0 else held(p, k, 0)
            add_rows(target, [held(p, k, 0)] + got, pieces[p][2])
            return
        for side in range(2):
            if span(p, side, d) is None:
                continue
            if d < half and span(p, side, d + 1) is not None:
                ring_copy(p, k, side, d + 1).wait_recv()
                first, rows = span(p, side, d + 1)
                target = held(p, k, d if side == 0 else count - d)
                term = ring_in[p].at[k, side, d]
                if rows != pieces[p][2]:
                    target, term = target.at[pl.ds(first, rows)], term.at[pl.ds(first, rows)]
                add_rows(target, [target, term], rows)
            start(ring_copy(p, k, side, d))

    for d in range(half, -1, -1):
        for p in everyone:
            if method[p] == RING_FIRST:
                for k in reversed(planes(p)):
                    for q in steps(d):
                        core_sum(p, k, q)
                    ring_step(p, k, d)
                    if d == 0 and k > 0:
                        start(chip_copy(p, k, 0))
        for p in everyone:
            if method[p] == CHIP_FIRST:
                for q in steps(d):
                    for k in reversed(range(chips)):
                        core_sum(p, k, q)
                        if k > 0:
                            start(chip_copy(p, k, q))
        for p in everyone:
            if method[p] == CHIP_FIRST and d < half:
                for q in steps(d + 1):
                    chip_sum(p, q)
                ring_step(p, 0, d + 1)
    for p in everyone:
        if method[p] == CHIP_FIRST:
            chip_sum(p, 0)
            ring_step(p, 0, 0)
    for p in everyone:
        if method[p] == RING_FIRST:
            chip_sum(p, 0)
    for copy in sent:
        copy.wait_send()


def reduce_call(net, arrays, pieces):
    chips, cores, count = net.chips, net.cores, net.seq_count
    half = count // 2
    anywhere = pl.BlockSpec(memory_space=pl.ANY)
    shapes = [terms.shape[2:] for terms in arrays]
    ahead = max(chips - 1, 1)
    blocks = [(piece[2], shapes[piece[0]][1]) for piece in pieces]
    chip_shapes = [
        (ahead, count) + block if piece[3] == CHIP_FIRST else (ahead,) + block
        for piece, block in zip(pieces, blocks)
    ]
    ring_shapes = [
        (chips if piece[3] == RING_FIRST else 1, 2, half) + block
        for piece, block in zip(pieces, blocks)
    ]
    n = len(pieces)
    return pl.pallas_call(
        functools.partial(reduce_kernel, net.order, chips, cores, pieces, len(arrays)),
        out_shape=[jax.ShapeDtypeStruct(shape, f32) for shape in shapes],
        in_specs=[anywhere] * len(arrays),
        out_specs=[pl.BlockSpec(memory_space=pltpu.VMEM)] * len(arrays),
        scratch_shapes=[pltpu.VMEM((chips, count) + shape, bf16) for shape in shapes]
        + [pltpu.VMEM((chips, count) + shape, bf16) for shape in shapes]
        + [pltpu.VMEM(shape, bf16) for shape in chip_shapes]
        + [pltpu.VMEM(shape, bf16) for shape in ring_shapes]
        + [
            pltpu.SemaphoreType.DMA((len(arrays), chips)),
            pltpu.SemaphoreType.DMA((n, chips, count)),
            pltpu.SemaphoreType.DMA((n, chips, count)),
            pltpu.SemaphoreType.DMA((n, ahead, count)),
            pltpu.SemaphoreType.DMA((n, ahead, count)),
            pltpu.SemaphoreType.DMA((n, chips, 2, half)),
            pltpu.SemaphoreType.DMA((n, chips, 2, half)),
        ],
        compiler_params=pltpu.CompilerParams(
            collective_id=4, has_side_effects=True, vmem_limit_bytes=63 * 2**20
        ),
        cost_estimate=pl.CostEstimate(
            flops=0, bytes_accessed=sum(terms.size for terms in arrays) * 4, transcendentals=0
        ),
    )(*arrays)


def exchange(totals, everyone, send_sem, recv_sem, count):
    me = lax.axis_index("seq")
    everyone[me] = totals[...]
    copies = []
    for step in range(1, count):
        peer = lax.rem(me + step, count)
        copy = pltpu.make_async_remote_copy(
            src_ref=totals,
            dst_ref=everyone.at[me],
            send_sem=send_sem.at[step],
            recv_sem=recv_sem.at[step],
            device_id={"seq": peer},
            device_id_type=pl.DeviceIdType.MESH,
        )
        copy.start()
    for step in range(1, count):
        source = lax.rem(me + count - step, count)
        copy = pltpu.make_async_remote_copy(
            src_ref=totals,
            dst_ref=everyone.at[source],
            send_sem=send_sem.at[step],
            recv_sem=recv_sem.at[step],
            device_id={"seq": source},
            device_id_type=pl.DeviceIdType.MESH,
        )
        copy.wait()


def greet(count):
    me = lax.axis_index("seq")
    barrier = pltpu.get_barrier_semaphore()
    for step in range(1, count):
        pl.semaphore_signal(
            barrier,
            inc=1,
            device_id={"seq": lax.rem(me + step, count)},
            device_id_type=pl.DeviceIdType.MESH,
        )
    pl.semaphore_wait(barrier, count - 1)


def tiles(channels):
    wide = 512 if channels % 512 == 0 else 128
    return [pl.ds(at, wide) for at in range(0, channels, wide)]


def tile_prefix(product, total, step):
    row = lax.broadcasted_iota(jnp.int32, product.shape, 0)
    reach = 1
    while reach < LANES:
        turn = reach if step > 0 else LANES - reach
        inside = row >= reach if step > 0 else row < LANES - reach
        total = total + product * jnp.where(inside, pltpu.roll(total, turn, 0), 0.0)
        product = product * jnp.where(inside, pltpu.roll(product, turn, 0), 1.0)
        reach *= 2
    return (product, total)


def scan_kernel(
    count, decay_ref, drive_ref, start_ref, state_ref, prev_ref, last_ref,
    totals, everyone, send_sem, recv_sem,
):
    greet(count)
    rows, channels = decay_ref.shape
    end = LANES - 1
    for cols in tiles(channels):

        def first_pass(t, carry):
            run_product, run_sum = carry
            at = pl.ds(pl.multiple_of(t * LANES, LANES), LANES)
            product, total = tile_prefix(decay_ref[at, cols], drive_ref[at, cols], 1)
            prev_ref[at, cols] = product
            state_ref[at, cols] = total
            last = product[end:]
            return (last * run_product, last * run_sum + total[end:])

        zero = jnp.zeros((1, cols.size), f32)
        run_product, run_sum = lax.fori_loop(
            0, rows // LANES, first_pass, (zero + 1.0, zero), unroll=4
        )
        totals[0:1, cols] = run_product
        totals[1:2, cols] = run_sum
    exchange(totals, everyone, send_sem, recv_sem, count)
    me = lax.axis_index("seq")
    for cols in tiles(channels):
        state = start_ref[0:1, cols]
        entering = state
        for device in range(count):
            entering = jnp.where(me == device, state, entering)
            state = everyone[device, 0:1, cols] * state + everyone[device, 1:2, cols]
        last_ref[0:1, cols] = state

        def second_pass(t, entry):
            at = pl.ds(pl.multiple_of(t * LANES, LANES), LANES)
            state = prev_ref[at, cols] * entry + state_ref[at, cols]
            row = lax.broadcasted_iota(jnp.int32, state.shape, 0)
            state_ref[at, cols] = state
            prev_ref[at, cols] = jnp.where(row == 0, entry, pltpu.roll(state, 1, 0))
            return state[end:]

        lax.fori_loop(0, rows // LANES, second_pass, entering, unroll=4)


def scan_back_kernel(
    count, decay_ref, d_state_ref, prev_ref, d_drive_ref, d_decay_ref,
    totals, everyone, send_sem, recv_sem,
):
    greet(count)
    rows, channels = decay_ref.shape
    last_tile = rows // LANES - 1
    end = LANES - 1
    for cols in tiles(channels):

        def first_pass(i, carry):
            run_product, run_sum = carry
            at = pl.ds(pl.multiple_of((last_tile - i) * LANES, LANES), LANES)
            decay = decay_ref[at, cols]
            product, total = tile_prefix(decay, decay * d_state_ref[at, cols], -1)
            d_decay_ref[at, cols] = product
            d_drive_ref[at, cols] = total
            first = product[:1]
            return (first * run_product, first * run_sum + total[:1])

        zero = jnp.zeros((1, cols.size), f32)
        run_product, run_sum = lax.fori_loop(
            0, rows // LANES, first_pass, (zero + 1.0, zero), unroll=4
        )
        totals[0:1, cols] = run_product
        totals[1:2, cols] = run_sum
    exchange(totals, everyone, send_sem, recv_sem, count)
    me = lax.axis_index("seq")
    for cols in tiles(channels):
        state = jnp.zeros((1, cols.size), f32)
        entering = state
        for device in reversed(range(count)):
            entering = jnp.where(me == device, state, entering)
            state = everyone[device, 0:1, cols] * state + everyone[device, 1:2, cols]

        def second_pass(i, entry):
            at = pl.ds(pl.multiple_of((last_tile - i) * LANES, LANES), LANES)
            outgoing = d_decay_ref[at, cols] * entry + d_drive_ref[at, cols]
            row = lax.broadcasted_iota(jnp.int32, outgoing.shape, 0)
            incoming = jnp.where(row == end, entry, pltpu.roll(outgoing, end, 0))
            carry = d_state_ref[at, cols] + incoming
            d_drive_ref[at, cols] = carry
            d_decay_ref[at, cols] = carry * prev_ref[at, cols]
            return outgoing[:1]

        lax.fori_loop(0, rows // LANES, second_pass, entering, unroll=4)


def scan_call(kernel, collective_id, count, operands, out_shapes):
    channels = operands[0].shape[1]
    vmem = pl.BlockSpec(memory_space=pltpu.VMEM)
    return pl.pallas_call(
        functools.partial(kernel, count),
        out_shape=out_shapes,
        in_specs=[vmem] * len(operands),
        out_specs=[vmem] * len(out_shapes),
        scratch_shapes=[
            pltpu.VMEM((2, channels), f32),
            pltpu.VMEM((count, 2, channels), f32),
            pltpu.SemaphoreType.DMA((count,)),
            pltpu.SemaphoreType.DMA((count,)),
        ],
        compiler_params=pltpu.CompilerParams(
            collective_id=collective_id, has_side_effects=True, vmem_limit_bytes=40 * 2**20
        ),
        cost_estimate=pl.CostEstimate(
            flops=8 * operands[0].size, bytes_accessed=20 * operands[0].size, transcendentals=0
        ),
    )(*operands)


def gate_parts(conv_ref, both_ref, vectors_ref, reset_ref):
    conv = conv_ref[...].astype(f32)
    pre = contract(conv_ref[...], both_ref[...], 1, 0)
    rate = jax.nn.sigmoid(pre[:, :HW] + vectors_ref[0:1])
    in_gate = jax.nn.sigmoid(pre[:, HW:] + vectors_ref[1:2])
    log_decay = vectors_ref[2:3] * rate
    reset = reset_ref[...]
    keep = 1.0 - reset
    decay = jnp.exp(log_decay)
    bend = jnp.tanh(-log_decay)
    power = 2.0 * bend / (1.0 + bend)
    root = jnp.sqrt(jnp.maximum(power, floor_value))
    return conv, rate, in_gate, decay, keep, power, root, reset + keep * root


def gate_kernel(conv_ref, both_ref, vectors_ref, reset_ref, decay_ref, drive_ref):
    conv, _, in_gate, decay, keep, _, _, share = gate_parts(
        conv_ref, both_ref, vectors_ref, reset_ref
    )
    decay_ref[...] = decay * keep
    drive_ref[...] = share * in_gate * conv


def gate_back_kernel(
    conv_ref, both_ref, vectors_ref, reset_ref, d_decay_ref, d_drive_ref,
    d_conv_ref, grad_ref, sums_ref,
):
    conv, rate, in_gate, decay, keep, power, root, share = gate_parts(
        conv_ref, both_ref, vectors_ref, reset_ref
    )
    d_drive = d_drive_ref[...]
    through = jnp.where(
        power > floor_value, d_drive * keep * in_gate * conv * (decay * decay) / root, 0.0
    )
    d_log = d_decay_ref[...] * decay * keep - through
    d_rate = (d_log * vectors_ref[2:3] * rate * (1.0 - rate)).astype(bf16)
    d_input = (d_drive * share * conv * in_gate * (1.0 - in_gate)).astype(bf16)
    d_both = jnp.concatenate([d_rate, d_input], 1)
    d_conv = (d_drive * share * in_gate + contract(d_both, both_ref[...], 1, 1)).astype(bf16)
    d_conv_ref[...] = d_conv
    grad_ref[...] = contract(conv_ref[...], d_both, 0, 0).astype(bf16)
    sums_ref[0:1] = jnp.sum(d_rate.astype(f32), axis=0, keepdims=True)
    sums_ref[1:2] = jnp.sum(d_input.astype(f32), axis=0, keepdims=True)
    sums_ref[2:3] = jnp.sum(d_log * rate, axis=0, keepdims=True)
    sums_ref[3:4] = jnp.sum(d_conv.astype(f32), axis=0, keepdims=True)


def gate_call(kernel, conv, both, vectors, reset, grads, out_kinds):
    rows, channels = conv.shape
    per_row = pl.BlockSpec((rows, HW), lambda h: (0, h))
    kinds = {
        "rows": (per_row, (rows, channels)),
        "weights": (pl.BlockSpec((HW, 2 * HW), lambda h: (h, 0)), (channels, 2 * HW)),
        "sums": (pl.BlockSpec((4, HW), lambda h: (0, h)), (4, channels)),
    }
    return pl.pallas_call(
        kernel,
        grid=(channels // HW,),
        out_shape=[jax.ShapeDtypeStruct(kinds[kind][1], dtype) for kind, dtype in out_kinds],
        in_specs=[
            per_row,
            kinds["weights"][0],
            pl.BlockSpec((vectors.shape[0], HW), lambda h: (0, h)),
            pl.BlockSpec((rows, 1), lambda h: (0, 0)),
        ]
        + [per_row] * len(grads),
        out_specs=[kinds[kind][0] for kind, _ in out_kinds],
        compiler_params=pltpu.CompilerParams(vmem_limit_bytes=32 * 2**20),
        cost_estimate=pl.CostEstimate(
            flops=4 * rows * channels * HW * (1 + 2 * len(grads)),
            bytes_accessed=24 * rows * channels,
            transcendentals=6 * rows * channels,
        ),
    )(conv, both, vectors, reset, *grads)


def pair_slots(count):
    half = count // 2
    return [k for s in range(1, half) for k in (count - s, s)] + [half, 0]


def gelu_parts(v):
    root, cubic = 0.7978845608028654, 0.044715
    curve = jnp.tanh(root * (v + cubic * v * v * v))
    act = 0.5 * v * (1.0 + curve)
    slope = 0.5 * (1.0 + curve) + 0.5 * v * (1.0 - curve * curve) * root * (
        1.0 + 3.0 * cubic * v * v
    )
    return (act, slope)


def contract(left, right, left_dim, right_dim):
    return lax.dot_general(
        left, right, (((left_dim,), (right_dim,)), ((), ())), preferred_element_type=f32
    )


def ff_kernel(order, cores, own_ref, gate_hbm, up_hbm, down_hbm, *refs):
    cot_count = len(refs) - 37
    cot_hbm, refs = refs[:cot_count], refs[cot_count:]
    blocks_ref, out_ref, d_in_ref, gate_grad, up_grad, down_grad, sum_ref, *refs = refs
    gate_ref, up_ref, down_ref, rows_ref, cots_ref, h_ref, g_ref, u_ref, o_ref, d_ref, *refs = refs
    lone_refs, refs = refs[:7], refs[7:]
    gate_sum, up_sum, down_sum, landing, mine, *refs = refs
    send_sem, recv_sem, load_sem, store_sem, back_send, back_recv, mine_sem, done_sem = refs
    count = len(order)
    half = count // 2
    rows, width = own_ref.shape
    hidden_here = gate_ref.shape[1]
    cut = rows // 2
    me = lax.axis_index("seq")
    ahead_of, behind_of = [0] * count, [0] * count
    for i, device in enumerate(order):
        ahead_of[device] = order[(i + 1) % count]
        behind_of[device] = order[(i - 1) % count]
    sides = ({"seq": lookup(ahead_of, me)}, {"seq": lookup(behind_of, me)})
    dp = lax.axis_index("dp")
    core = {"dp": dp + 1 - 2 * lax.rem(dp, 2)}

    barrier = pltpu.get_barrier_semaphore()
    peers = list(sides) + ([core] if cores == 2 else [])
    for peer in peers:
        pl.semaphore_signal(barrier, inc=1, device_id=peer, device_id_type=pl.DeviceIdType.MESH)
    weights = [
        pltpu.make_async_copy(hbm, vmem, load_sem.at[i])
        for i, (hbm, vmem) in enumerate(
            ((gate_hbm, gate_ref), (up_hbm, up_ref), (down_hbm, down_ref))
        )
    ]
    for copy in weights:
        copy.start()
    pl.semaphore_wait(barrier, len(peers))

    def full(side, source, slot, s):
        return remote(
            source, blocks_ref.at[slot], send_sem.at[side, s], recv_sem.at[slot], sides[side]
        )

    def part(side):
        at = pl.ds(0, cut) if side == 0 else pl.ds(cut, rows - cut)
        return remote(
            blocks_ref.at[2 * (half - 2) + side, at],
            blocks_ref.at[count - 2, at],
            send_sem.at[side, half - 1],
            recv_sem.at[count - 2 + side],
            sides[side],
        )

    for side in range(2):
        full(side, own_ref, side, 0).start()

    def rows_load(s):
        return pltpu.make_async_copy(
            blocks_ref.at[pl.ds(2 * (s - 1), 2)], rows_ref, load_sem.at[3]
        )

    pair_refs = (rows_ref, cots_ref, h_ref, g_ref, u_ref, o_ref, d_ref)

    def stores(s):
        return [
            pltpu.make_async_copy(o_ref, out_ref.at[s - 1], store_sem.at[0]),
            pltpu.make_async_copy(d_ref, d_in_ref.at[s - 1], store_sem.at[1]),
        ]

    def lone_stores(first):
        at = pl.ds(first * rows, rows)
        return [
            pltpu.make_async_copy(lone_refs[5], out_ref.at[half - 1, at], store_sem.at[2]),
            pltpu.make_async_copy(lone_refs[6], d_in_ref.at[half - 1, at], store_sem.at[3]),
        ]

    wide = 256 if hidden_here % 256 == 0 else 128
    out_wide = 512

    def multiply(refs):
        x_ref, c_ref, h_to, g_to, u_to, o_to, d_to = refs
        many = h_to.shape[0]

        def inner(j, carry):
            at = pl.ds(pl.multiple_of(j * wide, wide), wide)
            x = x_ref[...].reshape(many, width)
            c = c_ref[...].reshape(many, width)
            ff_gate = contract(x, gate_ref[:, at], 1, 0)
            ff_up = contract(x, up_ref[:, at], 1, 0)
            d_hidden = contract(c, down_ref[at, :], 1, 1)
            act, slope = gelu_parts(ff_gate)
            h_to[:, at] = (act * ff_up).astype(bf16)
            g_to[:, at] = (d_hidden * ff_up * slope).astype(bf16)
            u_to[:, at] = (d_hidden * act).astype(bf16)
            return carry

        lax.fori_loop(0, hidden_here // wide, inner, 0)

        def outer(j, carry):
            at = pl.ds(pl.multiple_of(j * out_wide, out_wide), out_wide)
            d_to[:, at] = (
                contract(g_to[...], gate_ref[at, :], 1, 1) + contract(u_to[...], up_ref[at, :], 1, 1)
            ).astype(bf16)
            o_to[:, at] = contract(h_to[...], down_ref[:, at], 1, 0).astype(bf16)
            return carry

        lax.fori_loop(0, width // out_wide, outer, 0)

    def gradients(refs, fresh=False):
        x_ref, c_ref, h_to, g_to, u_to = refs[:5]
        many = h_to.shape[0]
        tile = 256

        def body(j, carry):
            at = pl.ds(pl.multiple_of(j * tile, tile), tile)
            x = x_ref[..., at].reshape(many, tile)
            c = c_ref[..., at].reshape(many, tile)
            terms = (
                contract(x, g_to[...], 0, 0),
                contract(x, u_to[...], 0, 0),
                contract(h_to[...], c, 0, 0),
            )
            places = (
                (gate_sum, (at, slice(None))),
                (up_sum, (at, slice(None))),
                (down_sum, (slice(None), at)),
            )
            for term, (ref, place) in zip(terms, places):
                ref[place] = term if fresh else ref[place] + term
            return carry

        lax.fori_loop(0, width // tile, body, 0)

    def run(copies):
        for copy in copies:
            copy.start()
        for copy in copies:
            copy.wait()

    run(
        [
            pltpu.make_async_copy(own_ref, lone_refs[0], load_sem.at[3]),
            pltpu.make_async_copy(cot_hbm[0], lone_refs[1], load_sem.at[4]),
        ]
    )
    for copy in weights:
        copy.wait()
    multiply(lone_refs)
    for copy in lone_stores(1):
        copy.start()
    gradients(lone_refs, True)
    for copy in lone_stores(1):
        copy.wait()

    def step(s, carry):
        for side in range(2):
            full(side, own_ref, 2 * (s - 1) + side, s).wait_recv()

        @pl.when(s < half - 1)
        def _():
            for side in range(2):
                slot = 2 * (s - 1) + side
                full(side, blocks_ref.at[slot], slot + 2, s).start()

        @pl.when(s == half - 1)
        def _():
            for side in range(2):
                part(side).start()

        rows_load(s).start()
        for at_step in range(1, half):

            @pl.when(s == at_step)
            def _():
                run(
                    [
                        pltpu.make_async_copy(
                            cot_hbm[2 * at_step - 1 + i], cots_ref.at[i], load_sem.at[4 + i]
                        )
                        for i in range(2)
                    ]
                )

        rows_load(s).wait()
        multiply(pair_refs)
        for copy in stores(s):
            copy.start()

        @pl.when(s < half - 1)
        def _():
            gradients(pair_refs)

        for copy in stores(s):
            copy.wait()
        return carry

    lax.fori_loop(1, half, step, 0)
    far, first = [], 0
    for i, part_hbm in enumerate(cot_hbm[2 * half - 1 :]):
        part_rows = part_hbm.shape[0]
        far.append(
            pltpu.make_async_copy(
                part_hbm, lone_refs[1].at[pl.ds(first, part_rows)], load_sem.at[5 + i]
            )
        )
        first += part_rows
    run(far)
    for side in range(2):
        part(side).wait_recv()
    run([pltpu.make_async_copy(blocks_ref.at[count - 2], lone_refs[0], load_sem.at[3])])
    multiply(lone_refs)

    chunks = 2
    chunk = width // chunks

    def part_of(d, side):
        if d == 0:
            return half - 1, rows
        return d - 1, (rows if side == 0 else 0)

    def own_load(d, side):
        pair, first = part_of(d, side)
        return pltpu.make_async_copy(
            d_in_ref.at[pair, pl.ds(first, rows)], mine.at[side, d % 2], mine_sem.at[side, d % 2]
        )

    def back(d, side, c):
        cols = pl.ds(c * chunk, chunk)
        at = pl.ds(0, rows)
        if d == half:
            at = pl.ds(0, cut) if side == 0 else pl.ds(cut, rows - cut)
            source = lone_refs[6].at[at, cols]
        else:
            source = mine.at[side, d % 2, at, cols]
        return remote(
            source,
            landing.at[side, d - 1, at, cols],
            back_send.at[side, d - 1, c],
            back_recv.at[side, d - 1, c],
            sides[side],
        )

    def add_landed(target, terms, first, many, cols):
        def body(t, carry):
            at = pl.ds(pl.multiple_of(first + t * 16, 16), 16)
            target[at, cols] = total([term[at, cols].astype(f32) for term in terms]).astype(target.dtype)
            return carry

        lax.fori_loop(0, many // 16, body, 0)

    for c in range(chunks):
        for side in range(2):
            back(half, side, c).start()
    for copy in lone_stores(0):
        copy.start()
    for side in range(2):
        own_load(half - 1, side).start()
    gradients(pair_refs)
    gradients(lone_refs)

    def finish(total_ref, low_ref, out_hbm, sem):
        def body(t, carry):
            at = pl.ds(pl.multiple_of(t * 16, 16), 16)
            low_ref[at, :] = total_ref[at, :].astype(bf16)
            return carry

        lax.fori_loop(0, total_ref.shape[0] // 16, body, 0)
        copy = pltpu.make_async_copy(low_ref, out_hbm, load_sem.at[sem])
        copy.start()
        return copy

    results = ((gate_sum, gate_ref, gate_grad), (up_sum, up_ref, up_grad), (down_sum, down_ref, down_grad))
    finished = []
    for d in range(half - 1, 0, -1):
        for side in range(2):
            own_load(d, side).wait()
        for c in range(chunks):
            cols = pl.ds(c * chunk, chunk)
            for side in range(2):
                back(d + 1, side, c).wait_recv()
                first, many = (0, rows)
                if d == half - 1:
                    first, many = (0, cut) if side == 0 else (cut, rows - cut)
                held = mine.at[side, d % 2]
                add_landed(held, [held, landing.at[side, d]], first, many, cols)
                back(d, side, c).start()
        for side in range(2):
            if d < half - 1:
                for c in range(chunks):
                    back(d + 1, side, c).wait_send()
            if d > 1 or side == 0:
                own_load(d - 1, side).start()
        if len(finished) < len(results):
            finished.append(finish(*results[len(finished)], len(finished)))
    own_load(0, 0).wait()
    for c in range(chunks):
        cols = pl.ds(c * chunk, chunk)
        for side in range(2):
            back(1, side, c).wait_recv()
        add_landed(sum_ref, [mine.at[0, 0], landing.at[0, 0], landing.at[1, 0]], 0, rows, cols)
    if cores == 2:
        pl.semaphore_signal(done_sem, inc=1, device_id=core, device_id_type=pl.DeviceIdType.MESH)
    while len(finished) < len(results):
        finished.append(finish(*results[len(finished)], len(finished)))
    for copy in finished:
        copy.wait()
    for copy in lone_stores(0):
        copy.wait()
    for side in range(2):
        for c in range(chunks):
            back(half, side, c).wait_send()
            back(1, side, c).wait_send()
        for s in range(half - 1):
            full(side, own_ref, side, s).wait_send()
        part(side).wait_send()
    if cores == 2:
        pl.semaphore_wait(done_sem, 1)


def ff_call(net, own, cots, slab_gate, slab_up, slab_down):
    rows, width = own.shape
    count, half = net.seq_count, net.seq_count // 2
    hidden_here = slab_gate.shape[1]
    anywhere = pl.BlockSpec(memory_space=pl.ANY)
    pair = 2 * rows
    shape = jax.ShapeDtypeStruct
    return pl.pallas_call(
        functools.partial(ff_kernel, net.order, net.cores),
        out_shape=[
            shape((count, rows, width), bf16),
            shape((half, pair, width), bf16),
            shape((half, pair, width), bf16),
            shape((width, hidden_here), bf16),
            shape((width, hidden_here), bf16),
            shape((hidden_here, width), bf16),
            shape((rows, width), f32),
        ],
        in_specs=[anywhere] * (4 + len(cots)),
        out_specs=[anywhere] * 6 + [pl.BlockSpec(memory_space=pltpu.VMEM)],
        scratch_shapes=[
            pltpu.VMEM((width, hidden_here), bf16),
            pltpu.VMEM((width, hidden_here), bf16),
            pltpu.VMEM((hidden_here, width), bf16),
            pltpu.VMEM((2, rows, width), bf16),
            pltpu.VMEM((2, rows, width), bf16),
            pltpu.VMEM((pair, hidden_here), bf16),
            pltpu.VMEM((pair, hidden_here), bf16),
            pltpu.VMEM((pair, hidden_here), bf16),
            pltpu.VMEM((pair, width), bf16),
            pltpu.VMEM((pair, width), bf16),
            pltpu.VMEM((rows, width), bf16),
            pltpu.VMEM((rows, width), bf16),
            pltpu.VMEM((rows, hidden_here), bf16),
            pltpu.VMEM((rows, hidden_here), bf16),
            pltpu.VMEM((rows, hidden_here), bf16),
            pltpu.VMEM((rows, width), bf16),
            pltpu.VMEM((rows, width), bf16),
            pltpu.VMEM((width, hidden_here), f32),
            pltpu.VMEM((width, hidden_here), f32),
            pltpu.VMEM((hidden_here, width), f32),
            pltpu.VMEM((2, half, rows, width), bf16),
            pltpu.VMEM((2, 2, rows, width), bf16),
            pltpu.SemaphoreType.DMA((2, half)),
            pltpu.SemaphoreType.DMA((count,)),
            pltpu.SemaphoreType.DMA((8,)),
            pltpu.SemaphoreType.DMA((4,)),
            pltpu.SemaphoreType.DMA((2, half, 2)),
            pltpu.SemaphoreType.DMA((2, half, 2)),
            pltpu.SemaphoreType.DMA((2, 2)),
            pltpu.SemaphoreType.REGULAR,
        ],
        compiler_params=pltpu.CompilerParams(
            collective_id=2, has_side_effects=True, vmem_limit_bytes=62 * 2**20
        ),
        cost_estimate=pl.CostEstimate(
            flops=18 * count * rows * width * hidden_here,
            bytes_accessed=80 * 2**20,
            transcendentals=count * rows * hidden_here,
        ),
    )(own, slab_gate, slab_up, slab_down, *cots)


def result_kernel(arrived, *refs):
    ins, outs = refs[: 5 + arrived], refs[5 + arrived :]
    for source, target in zip(ins[:3], outs[:3]):
        target[...] = source[...].astype(f32)
    terms = [ins[3][0]] + [ref[...] for ref in ins[4 : 4 + arrived]]
    outs[3][...] = (ins[4 + arrived][...] + total([term.astype(f32) for term in terms])).astype(bf16)


def result_call(grads, out_part, arrived, residual):
    parts = 4
    rows, width = residual.shape
    pair = out_part.shape[0] - 1

    def cut(v):
        return pl.BlockSpec((v.shape[0] // parts, v.shape[1]), lambda i: (i, 0))

    own = pl.BlockSpec((1, rows // parts, width), lambda i: (pair, parts + i, 0))
    return pl.pallas_call(
        functools.partial(result_kernel, len(arrived)),
        grid=(parts,),
        out_shape=[jax.ShapeDtypeStruct(v.shape, f32) for v in grads]
        + [jax.ShapeDtypeStruct(residual.shape, bf16)],
        in_specs=[cut(v) for v in grads] + [own] + [cut(v) for v in arrived] + [cut(residual)],
        out_specs=[cut(v) for v in grads] + [cut(residual)],
        compiler_params=pltpu.CompilerParams(vmem_limit_bytes=60 * 2**20),
    )(*grads, out_part, *arrived, residual)


def passed_along(value, axis, steps):
    count = lax.axis_size(axis)
    first, last = (max(0, -steps), min(count, count - steps))
    return lax.ppermute(value, axis, [(source, source + steps) for source in range(first, last)])


def gelu_tanh(values):
    return jax.nn.gelu(values, approximate=True)


def rms_parts(values, norm_gain):
    root_scale = lax.rsqrt(jnp.mean(values * values, axis=-1, keepdims=True) + epsilon)
    unit_rows = values * root_scale
    return (unit_rows * norm_gain, root_scale, unit_rows)


def norm_back(d_normed, norm_gain, root_scale, unit_rows):
    weighted = d_normed * norm_gain
    grad_gain = jnp.sum(d_normed * unit_rows, axis=0)
    d_values = root_scale * (
        weighted - unit_rows * jnp.mean(weighted * unit_rows, axis=-1, keepdims=True)
    )
    return (grad_gain, d_values)


def rows_of(values, first_row, row_count):
    return lax.slice_in_dim(values, first_row, first_row + row_count, axis=values.ndim - 2)


def dot(left, right):
    return jnp.dot(left, right, preferred_element_type=f32)


def dot_t(left, right):
    return lax.dot_general(left, right, (((1,), (1,)), ((), ())), preferred_element_type=f32)


def t_dot(left, right):
    return lax.dot_general(left, right, (((0,), (0,)), ((), ())), preferred_element_type=f32)


def per_device(
    inputs,
    reset,
    initial_state,
    cotangent,
    norm1_gain,
    w_gate,
    w_in,
    conv_w,
    conv_bias,
    w_rgate,
    rgate_bias,
    w_igate,
    igate_bias,
    decay_param,
    w_out,
    norm2_gain,
    w_ffgate,
    w_ffup,
    w_ffdown,
):
    net = Net()
    seqs_here, len_here, width = inputs.shape
    assert seqs_here == 1
    rows_here = len_here
    dp_count, seq_count = net.dp_count, net.seq_count
    devices = dp_count * seq_count
    chan_here, channels = w_rgate.shape[0], w_rgate.shape[0] * devices
    wide_here = norm1_gain.shape[0]
    taps = conv_w.shape[0]
    rim_rows = taps - 1

    def lanes(rows):
        return jnp.pad(rows, ((0, 0),) * (rows.ndim - 1) + ((0, LINE - rows.shape[-1]),))

    vectors = [norm1_gain, norm2_gain, conv_w, conv_bias, rgate_bias, igate_bias, decay_param]
    small_rows = 6 + taps
    small, at_row = None, 0
    for v in vectors:
        v = v.reshape(-1, v.shape[-1])
        below = small_rows - at_row - v.shape[0]
        placed = lax.pad(v, jnp.zeros((), bf16), ((at_row, below, 0), (0, LINE - v.shape[1], 0)))
        small = placed if small is None else small + placed
        at_row += v.shape[0]
    rim_inputs = inputs.reshape(rows_here, width)[rows_here - rim_rows :]
    full_in, full_gate, full_out, small_all, full_both, start_state, rims, flags = gather_call(
        net,
        (
            w_in,
            w_gate,
            w_out,
            small,
            jnp.concatenate([w_rgate, w_igate], 1),
            initial_state,
            rim_inputs,
            reset.astype(f32),
        ),
        [
            (6, 0, rim_rows, RING_ONLY),
            (7, 0, 1, RING_ONLY),
            (3, 0, small.shape[0], RING_FIRST),
            (4, 0, chan_here, RING_FIRST),
            (0, 0, wide_here, RING_FIRST),
            (1, 0, wide_here, CHIP_FIRST),
            (2, 0, chan_here, RING_FIRST),
            (5, 0, 1, RING_ONLY),
        ],
    )
    full_in, full_gate = (v.reshape(width, channels) for v in (full_in, full_gate))
    full_out = full_out.reshape(channels, width)
    full_both = full_both.reshape(channels, 2 * HW)
    start_state = start_state.reshape(1, channels)
    small_all = small_all.reshape(devices, -1, LINE)
    full_norm1 = small_all[:, 0, :wide_here].reshape(-1).astype(f32)
    full_norm2 = small_all[:, 1, :wide_here].reshape(-1).astype(f32)
    conv_wf = small_all[:, 2 : 2 + taps, :chan_here].transpose(1, 0, 2).reshape(taps, channels).astype(f32)
    full_cbias, full_rbias, full_ibias, decay_f = (
        small_all[:, i, :chan_here].reshape(-1).astype(f32) for i in range(2 + taps, 6 + taps)
    )
    gate_vectors = jnp.stack([full_rbias, full_ibias, -8.0 * jax.nn.softplus(-decay_f)], 0)
    at_seq = lax.axis_index("seq")
    last_seq = seq_count - 1

    def neighbour(values, index, there):
        picked = lax.dynamic_index_in_dim(values[0], jnp.clip(index, 0, last_seq), 0, keepdims=False)
        return jnp.where(there, picked, jnp.zeros_like(picked))

    rim_before = neighbour(rims, at_seq - 1, at_seq > 0)
    flags_before = neighbour(flags, at_seq - 1, at_seq > 0)[0, rows_here - rim_rows :]
    flags_after = neighbour(flags, at_seq + 1, at_seq < last_seq)[0, :rim_rows]
    flags_here = reset.reshape(rows_here).astype(f32)
    w_ffgate, w_ffup, w_ffdown, cotangent, full_in = lax.optimization_barrier(
        (w_ffgate, w_ffup, w_ffdown, cotangent, full_in)
    )
    slab_gate, slab_up, slab_down = (
        lax.all_gather(w_ffgate, "dp", axis=0, tiled=True),
        lax.all_gather(w_ffup, "dp", axis=0, tiled=True),
        lax.all_gather(w_ffdown, "dp", axis=1, tiled=True),
    )
    cotan_rows = cotangent.reshape(rows_here, width)
    cot_flow = Flow(net.seq.gather_steps(cotan_rows))

    lead = 8 - rim_rows
    token_rows = inputs.reshape(rows_here, width).astype(f32)
    normed_f, scale_one, unit_one = rms_parts(token_rows, full_norm1)
    normed = normed_f.astype(bf16)
    rim_normed = rms_parts(rim_before.astype(f32), full_norm1)[0].astype(bf16)
    extended = jnp.concatenate([jnp.pad(rim_normed, ((lead, 0), (0, 0))), normed], 0)
    branch = dot(extended, full_in).astype(bf16)
    gate_pre = dot(normed, full_gate)
    branch, gate_pre = beside((branch, gate_pre), cot_flow)
    padded = branch[lead:].astype(f32)
    open_pad = (1.0 - jnp.concatenate([flags_before, flags_here], 0))[:, None]
    open_masks = [None]
    conv_total = full_cbias + conv_wf[0] * rows_of(padded, rim_rows, len_here)
    running = rows_of(open_pad, rim_rows, len_here)
    for offset in range(1, rim_rows + 1):
        if offset > 1:
            running = running * rows_of(open_pad, rim_rows + 1 - offset, len_here)
        open_masks.append(running)
        conv_total = conv_total + running * conv_wf[offset] * rows_of(
            padded, rim_rows - offset, len_here
        )
    conv_low = conv_total.astype(bf16)
    reset_col = reset.astype(f32).reshape(rows_here, 1)
    decay_rows, drive_rows = gate_call(
        gate_kernel, conv_low, full_both, gate_vectors, reset_col, (), [("rows", f32)] * 2
    )
    row_shape = jax.ShapeDtypeStruct((rows_here, channels), f32)
    states, prev_states, last_state = scan_call(
        scan_kernel,
        0,
        seq_count,
        (decay_rows, drive_rows, start_state),
        [row_shape, row_shape, jax.ShapeDtypeStruct((1, channels), f32)],
    )
    states = beside(states, cot_flow)
    final_here = initial_state.shape[1]
    final_state = lax.dynamic_slice_in_dim(
        last_state, lax.axis_index("seq") * final_here, final_here, 1
    )
    state_f = states.astype(bf16).astype(f32)
    gate_act, gate_back = jax.vjp(gelu_tanh, gate_pre)
    mixed_rows = (state_f * gate_act).astype(bf16)
    residual = token_rows + dot(mixed_rows, full_out)

    slots = pair_slots(seq_count)
    cot_blocks = cot_flow.finish()
    cots = [cotan_rows] + [cot_blocks[k] for k in slots[:-2]] + cot_blocks[seq_count // 2]
    normed_two_f, scale_two, unit_two = rms_parts(residual, full_norm2)
    normed_two = normed_two_f.astype(bf16)
    _, out_part, _, gate_part, up_part, down_part, d_normed_two = ff_call(
        net, normed_two, cots, slab_gate, slab_up, slab_down
    )

    def block_rows(whole):
        whole = whole.reshape(seq_count, rows_here, width)
        return lambda k: whole[slots.index(k)]

    d_normed_two, out_part, gate_part, up_part, down_part = lax.optimization_barrier(
        (d_normed_two, out_part, gate_part, up_part, down_part)
    )
    out_flow = Flow(net.seq.scatter_steps(block_rows(out_part)))
    grad_ffgate, grad_ffup, grad_ffdown = (
        lax.psum_scatter(part, "dp", scatter_dimension=axis, tiled=True)
        for part, axis in ((gate_part, 0), (up_part, 0), (down_part, 1))
    )

    grad_norm2, d_resid_norm = norm_back(d_normed_two, full_norm2, scale_two, unit_two)
    d_residual = cotan_rows.astype(f32) + d_resid_norm
    d_residual_low = d_residual.astype(bf16)
    d_mixed = dot_t(d_residual_low, full_out)
    d_state = (d_mixed * gate_act).astype(bf16).astype(f32)
    d_gate_pre = gate_back(d_mixed * state_f)[0].astype(bf16)
    d_state, d_gate_pre = beside((d_state, d_gate_pre), out_flow)

    def grad_terms(left, right):
        return t_dot(left, right).astype(bf16).reshape(dp_count, seq_count, -1, right.shape[1])

    gate_terms = grad_terms(normed, d_gate_pre)
    d_drive, d_decay = scan_call(
        scan_back_kernel,
        1,
        seq_count,
        (decay_rows, d_state, prev_states),
        [row_shape, row_shape],
    )
    d_drive, d_decay, gate_terms = beside((d_drive, d_decay, gate_terms), out_flow)
    out_terms = grad_terms(mixed_rows, d_residual_low)
    d_conv_low, both_terms, gate_sums = gate_call(
        gate_back_kernel,
        conv_low,
        full_both,
        gate_vectors,
        reset_col,
        (d_decay, d_drive),
        [("rows", bf16), ("weights", bf16), ("sums", f32)],
    )
    d_conv_low, out_terms = beside((d_conv_low, out_terms), out_flow)
    grad_rbias, grad_ibias, rate_sum, grad_cbias = gate_sums
    grad_decay = 8.0 * jax.nn.sigmoid(-decay_f) * rate_sum
    rim_grad = passed_along(d_conv_low[:rim_rows], "seq", -1)
    grad_ext = jnp.concatenate([d_conv_low, rim_grad], 0).astype(f32)
    open_next = (1.0 - jnp.concatenate([flags_here, flags_after], 0))[:, None]
    d_conv_f = rows_of(grad_ext, 0, len_here)
    d_branch = conv_wf[0] * d_conv_f
    ahead = None
    conv_grads = [jnp.sum(rows_of(padded, rim_rows, len_here) * d_conv_f, axis=0)]
    for offset in range(1, rim_rows + 1):
        step_open = rows_of(open_next, offset, len_here)
        ahead = step_open if offset == 1 else ahead * step_open
        d_branch = d_branch + ahead * conv_wf[offset] * rows_of(grad_ext, offset, len_here)
        conv_grads.append(
            jnp.sum(
                open_masks[offset] * rows_of(padded, rim_rows - offset, len_here) * d_conv_f,
                axis=0,
            )
        )
    grad_conv = jnp.stack(conv_grads, 0)
    d_branch_low = d_branch.astype(bf16)
    in_terms = grad_terms(normed, d_branch_low)
    d_normed_one = dot_t(d_branch_low, full_in) + dot_t(d_gate_pre, full_gate)
    grad_norm1, d_token_norm = norm_back(d_normed_one, full_norm1, scale_one, unit_one)
    input_grad = (d_residual + d_token_norm).reshape(seqs_here, len_here, width)

    grad_norm1, input_grad = beside((grad_norm1, input_grad), out_flow)
    arrived = out_flow.finish()

    small_grads = [
        lanes(v.reshape(-1, devices, v.shape[-1] // devices).transpose(1, 0, 2)).astype(bf16)
        for v in (grad_norm1, grad_norm2, grad_conv, grad_cbias, grad_rbias, grad_ibias, grad_decay)
    ]
    small_terms = jnp.concatenate(small_grads, 1).reshape(dp_count, seq_count, -1, LINE)
    half_rows = chan_here * 3 // 5 // 16 * 16
    out_pieces = [(2, 0, half_rows, CHIP_FIRST), (2, half_rows, chan_here - half_rows, RING_FIRST)]
    if half_rows == 0 or chan_here % 16:
        out_pieces = [(2, 0, chan_here, CHIP_FIRST)]
    grad_in, grad_gate, grad_out, small_mine, both_mine = reduce_call(
        net,
        [
            in_terms,
            gate_terms,
            out_terms,
            small_terms,
            both_terms.reshape(dp_count, seq_count, chan_here, 2 * HW),
        ],
        [(1, 0, wide_here, RING_FIRST)]
        + out_pieces
        + [
            (3, 0, small.shape[0], CHIP_FIRST),
            (4, 0, chan_here, CHIP_FIRST),
            (0, 0, wide_here, CHIP_FIRST),
        ],
    )
    ff_grads, arrived, grad_in = lax.optimization_barrier(
        ((grad_ffgate, grad_ffup, grad_ffdown), arrived, grad_in)
    )
    grad_ffgate, grad_ffup, grad_ffdown, output = result_call(ff_grads, out_part, arrived, residual)
    output = output.reshape(seqs_here, len_here, width)
    mine = [small_mine[i, :wide_here] for i in range(2)]
    mine += [small_mine[2 : 2 + taps, :chan_here]]
    mine += [small_mine[i, :chan_here] for i in range(2 + taps, 6 + taps)]
    return (
        output,
        input_grad,
        final_state,
        mine[0],
        grad_gate,
        grad_in,
        mine[2],
        mine[3],
        both_mine[:, :HW],
        mine[4],
        both_mine[:, HW:],
        mine[5],
        mine[6],
        grad_out,
        mine[1],
        grad_ffgate,
        grad_ffup,
        grad_ffdown,
    )


def solution(mesh):
    split = ("dp", "seq")
    return jax.shard_map(
        per_device,
        mesh=mesh,
        in_specs=(
            P("dp", "seq", None),
            P("dp", "seq"),
            P("dp", "seq"),
            P("dp", "seq", None),
            P(split),
            P(split, None),
            P(split, None),
            P(None, split),
            P(split),
            P(split, None),
            P(split),
            P(split, None),
            P(split),
            P(split),
            P(split, None),
            P(split),
            P("dp", "seq"),
            P("dp", "seq"),
            P("seq", "dp"),
        ),
        out_specs=(
            P("dp", "seq", None),
            P("dp", "seq", None),
            P("dp", "seq"),
            P(split),
            P(split, None),
            P(split, None),
            P(None, split),
            P(split),
            P(split, None),
            P(split),
            P(split, None),
            P(split),
            P(split),
            P(split, None),
            P(split),
            P("dp", "seq"),
            P("dp", "seq"),
            P("seq", "dp"),
        ),
        check_vma=False,
    )
```
